32 devices in a mesh: gx: 8 (over y, x, core), yz: 4 (over z).
Axes of the slice: x: 2, y: 2, z: 4, core: 2. Of those that a mesh axis runs over, the one named last changes fastest.
Arguments:
- positions: float32 [3, 1536], P(None, ('gx', 'yz')), may hold values from -6 to 6
- velocities: float32 [3, 1536], P(None, ('gx', 'yz')), may hold values from -6 to 6
- forces_start: float32 [3, 1536], P(None, ('gx', 'yz')), may hold values from -6 to 6
- species: int32 [1536], P(('gx', 'yz')), may hold values from 0 to 7
- live_atoms: int32 [32], P(('gx', 'yz')), may hold values from 12 to 48, as said below
- send_list: int32 [8, 384], P(None, ('gx', 'yz')), may hold values from 0 to 47, as said below
- neighbours: int32 [1536, 128], P(('gx', 'yz')), may hold values from 0 to 143, as said below
- neighbour_count: int32 [1536], P(('gx', 'yz')), may hold values from 64 to 128
- radial_weight: bfloat16 [8, 512], replicated, may hold values from -4 to 4
- species_embed: bfloat16 [2, 8, 512], replicated, may hold values from -2 to 2
- env_weight: bfloat16 [1, 512, 64], replicated, may hold values from -0.25 to 0.25
- latent_weight: bfloat16 [1, 576, 512], replicated, may hold values from -0.25 to 0.25
- readout: bfloat16 [512], replicated, may hold values from -0.0625 to 0.0625
Outputs:
- positions_end: float32 [3, 1536], P(None, ('gx', 'yz'))
- velocities_end: float32 [3, 1536], P(None, ('gx', 'yz'))
- forces_end: float32 [3, 1536], P(None, ('gx', 'yz'))
The draws below stay inside these ranges and needn't reach their ends.
Inputs may be any that keep to these rules, and one draw needn't show every extreme that they name: `live_atoms`: atoms in use are the first ones of a domain's slots; some domain uses all 48 in every draw. `send_list`: each row names distinct atoms in use of the sending domain. `neighbours`: each entry names an own atom in use or a ghost slot.
All inputs are finite; a program needn't handle non-finite values.
Results may differ from the reference program's by a relative error of at most 0.038.
Values sent between devices are 32-bit elements; how exact they have to be, the bound alone decides.
No kernel may reach another device: no remote copies, remote signals or barrier semaphores. Data moves between devices by JAX's collectives and lax.ppermute only.
A program may use at most 64 MiB of HBM per device.

```python
import math
import jax
import jax.numpy as jnp
import numpy as np
from jax import lax

ATOM_DEV = 48
SLOTS = 128
LATENT = 512
FEATURES = 64
BASIS = 8
SPECIES = 8
LAYERS = 1
CENTRES = 4
GHOSTS = 12
ATOMS = 1536
N_GX = 8
N_YZ = 4


def live_counts(key):
    first_key, second_key, third_key = jax.random.split(key, 3)
    devices = N_GX * N_YZ
    first_draw = jax.random.randint(first_key, (devices,), 0, 9)
    second_draw = jax.random.randint(second_key, (devices,), 0, 9)
    factor = 2 + jnp.minimum(6, first_draw * second_draw // 10)
    counts = factor * ATOM_DEV // 8
    chosen = jax.random.randint(third_key, (), 0, devices)
    return jnp.where(jnp.arange(devices) == chosen, ATOM_DEV, counts).astype(jnp.int32)


def draw_live_atoms(key, part):
    return live_counts(key)


def draw_send_list(key, part):
    live_count = live_counts(key)
    key = jax.random.fold_in(key, 11)
    devices = N_GX * N_YZ
    noise_bits = jax.random.randint(key, (devices, 8, ATOM_DEV), 0, 65536)
    slot_ids = jnp.arange(ATOM_DEV, dtype=jnp.int32)
    scores = noise_bits * ATOM_DEV + slot_ids[None, None, :]
    scores = jnp.where(slot_ids[None, None, :] < live_count[:, None, None], scores, -1 - slot_ids[None, None, :])
    chosen = lax.top_k(scores, GHOSTS)[1]
    return chosen.transpose(1, 0, 2).reshape(8, devices * GHOSTS).astype(jnp.int32)


def draw_neighbours(key, part):
    live_count = live_counts(key)
    key = jax.random.fold_in(key, 12)
    devices = N_GX * N_YZ
    span_top = live_count[:, None, None] + 8 * GHOSTS
    raw_draw = jax.random.randint(key, (devices, ATOM_DEV, SLOTS), 0, span_top)
    picked = jnp.where(raw_draw < live_count[:, None, None], raw_draw, ATOM_DEV + raw_draw - live_count[:, None, None])
    return picked.reshape(devices * ATOM_DEV, SLOTS).astype(jnp.int32)


def draw_neighbour_count(key, part):
    key = jax.random.fold_in(key, 13)
    first_key, second_key = jax.random.split(key)
    devices = N_GX * N_YZ
    counts = SLOTS // 2 + jax.random.randint(first_key, (devices, ATOM_DEV), 0, SLOTS // 2 + 1)
    chosen = jax.random.randint(second_key, (devices, 1), 0, ATOM_DEV)
    counts = jnp.where(jnp.arange(ATOM_DEV)[None, :] == chosen, SLOTS, counts)
    return counts.reshape(devices * ATOM_DEV).astype(jnp.int32)


def draw_radial_weight(key, part):
    key = jax.random.fold_in(key, 14)
    sign_key, size_key = jax.random.split(key)
    sign_part = (2 * jax.random.randint(sign_key, (BASIS, LATENT), 0, 2) - 1).astype(jnp.float32)
    magnitude = jax.random.uniform(size_key, (BASIS, LATENT), jnp.float32, 2.5, 4.0)
    return (sign_part * magnitude).astype(jnp.bfloat16)


def plant(entries, key, least, top_value):
    place = [jax.random.randint(jax.random.fold_in(key, axis), (), 0, length) for axis, length in enumerate(entries.shape)]
    longest = entries.shape.index(max(entries.shape))
    neighbour = place[:longest] + [(place[longest] + 1) % entries.shape[longest]] + place[longest + 1:]
    return entries.at[tuple(place)].set(least).at[tuple(neighbour)].set(top_value)


def shard_levels(stream_key, extent, shards, smallest, top_value):
    level = 1.0
    for axis_at, blocks in shards:
        steps = jax.random.uniform(jax.random.fold_in(jax.random.fold_in(stream_key, 6), axis_at), (blocks,), jnp.float32, smallest / len(shards), top_value / len(shards))
        level = level * jnp.repeat(jnp.exp(steps), extent[axis_at] // blocks).reshape((-1,) + (1,) * (len(extent) - 1 - axis_at))
    return level


def rank_table(count, lean):
    loads = [(1 << 20) // math.isqrt(rank ** lean) + 1 for rank in range(1, count + 1)]
    spread = 1 + sum(loads) // (1 << 30)
    return np.cumsum(np.array([max(1, weight // spread) for weight in loads]))


def ranked(own_key, extent, number_of, skew):
    table = rank_table(number_of, skew)
    lot = jax.random.randint(jax.random.fold_in(own_key, 1), extent, 0, int(table[number_of - 1]))
    rank = jnp.searchsorted(jnp.asarray(table, jnp.int32), lot, side="right")
    return jax.random.permutation(jax.random.fold_in(own_key, 2), number_of)[rank].astype(jnp.int32)


def scatter_about(stream_key, shape, width, bound, shards=(), kind=jnp.bfloat16):
    level = shard_levels(stream_key, shape, shards, -0.22, 0.18) if shards else 1.0
    entries = jax.random.normal(stream_key, shape, jnp.float32) * width * level
    return jnp.minimum(jnp.maximum(entries, -bound), bound).astype(kind)


def setup_inputs(seed: int = 0) -> dict:
    keys = jax.random.split(jax.random.key(seed), 14)
    return {
        "positions": scatter_about(keys[0], (3, ATOMS), 1.5, 6.0, ((1, 32),), jnp.float32),
        "velocities": scatter_about(keys[1], (3, ATOMS), 1.0, 6.0, ((1, 32),), jnp.float32),
        "forces_start": scatter_about(keys[2], (3, ATOMS), 1.0, 6.0, ((1, 32),), jnp.float32),
        "species": plant(ranked(keys[3], (ATOMS,), SPECIES, 2), jax.random.fold_in(keys[3], 3), 0, SPECIES - 1).astype(jnp.int32),
        "live_atoms": draw_live_atoms(jax.random.fold_in(keys[13], 71), 0),
        "send_list": draw_send_list(jax.random.fold_in(keys[13], 71), 0),
        "neighbours": draw_neighbours(jax.random.fold_in(keys[13], 71), 0),
        "neighbour_count": draw_neighbour_count(jax.random.fold_in(keys[13], 71), 0),
        "radial_weight": draw_radial_weight(jax.random.fold_in(keys[13], 71), 0),
        "species_embed": scatter_about(keys[9], (2, SPECIES, LATENT), 0.5, 2.0),
        "env_weight": scatter_about(keys[10], (LAYERS, LATENT, FEATURES), LATENT ** -0.5, 0.25),
        "latent_weight": scatter_about(keys[11], (LAYERS, LATENT + FEATURES, LATENT), (LATENT + FEATURES) ** -0.5, 0.25),
        "readout": scatter_about(keys[12], (LATENT,), (16 * LATENT) ** -0.5, 0.0625),
    }


RADIUS = 6.0
STEP = 0.25
COUPLING = 4.0
MASSES = (1.008, 12.011, 14.007, 15.999, 32.06, 22.99, 35.45, 30.97)
OFFSETS = ((-1, -1), (-1, 0), (-1, 1), (0, -1), (0, 1), (1, -1), (1, 0), (1, 1))

def inverse_mass(species):
    inv_total = jnp.zeros(species.shape, jnp.float32)
    for spec_id in range(len(MASSES)):
        inv_total = inv_total + jnp.where(species == spec_id, jnp.float32(1.0 / MASSES[spec_id]), jnp.float32(0.0))
    return inv_total

def block_energy(centre_pos, neigh_pos, centre_kind, neigh_kind, pair_mask, radial_weight, species_embed, env_weight, latent_weight, readout):
    count_c = centre_pos.shape[1]
    slot_n = neigh_pos.shape[2]
    row_count = count_c * slot_n
    scaled = (neigh_pos - centre_pos[:, :, None]) * (1.0 / RADIUS)
    vectors = scaled.reshape(3, row_count)
    square = lax.optimization_barrier(jnp.sum(vectors * vectors, axis=0))
    envelope = jnp.square(jnp.maximum(1.0 - square, 0.0)) * pair_mask.reshape(row_count)
    basis_n = radial_weight.shape[0]
    basis_mid = (jnp.arange(basis_n, dtype=jnp.float32) + 0.5) / basis_n
    basis_vals = jnp.exp(-2.0 * basis_n * basis_n * jnp.square(square[:, None] - basis_mid[None, :]))
    centre_embed = jnp.dot(centre_kind, species_embed[0], preferred_element_type=jnp.float32)
    feat_width = centre_embed.shape[1]
    preact = jnp.dot(basis_vals.astype(jnp.bfloat16), radial_weight, preferred_element_type=jnp.float32)
    preact = preact + jnp.dot(neigh_kind, species_embed[1], preferred_element_type=jnp.float32)
    preact = (preact.reshape(count_c, slot_n, feat_width) + centre_embed[:, None, :]).reshape(row_count, feat_width)
    hidden = jax.nn.silu(preact)
    norm_scale = slot_n ** (-0.5)
    for layer_id in range(env_weight.shape[0]):
        weights = jnp.dot(hidden.astype(jnp.bfloat16), env_weight[layer_id], preferred_element_type=jnp.float32) * envelope[:, None]
        tensor = vectors[:, :, None] * weights[None, :, :]
        grouped = tensor.reshape(3, count_c, slot_n, weights.shape[1])
        centre_tensor = lax.optimization_barrier(jnp.sum(grouped, axis=2)) * norm_scale
        inner_prod = COUPLING * lax.optimization_barrier(jnp.sum(grouped * centre_tensor[:, :, None, :], axis=0)).reshape(row_count, weights.shape[1])
        joined = jnp.concatenate([hidden, inner_prod], axis=1).astype(jnp.bfloat16)
        hidden = hidden + jax.nn.silu(jnp.dot(joined, latent_weight[layer_id], preferred_element_type=jnp.float32))
    pair_energy = jnp.dot(hidden.astype(jnp.bfloat16), readout, preferred_element_type=jnp.float32)
    return jnp.sum(pair_energy * envelope)

def block_update(forces, block_id, ext_pos, ext_kinds, neighbours, counts, live_count, params):
    first = (block_id * CENTRES).astype(jnp.int32)
    centre_pos = lax.dynamic_slice_in_dim(ext_pos, first, CENTRES, 1)
    neigh_idx = lax.dynamic_slice_in_dim(neighbours, first, CENTRES, 0)
    neigh_pos = ext_pos[:, neigh_idx]
    centre_kind = lax.dynamic_slice_in_dim(ext_kinds, first, CENTRES, 0)
    neigh_kind = ext_kinds[neigh_idx.reshape(-1)]
    block_counts = lax.dynamic_slice_in_dim(counts, first, CENTRES, 0)
    slot_n = neighbours.shape[1]
    alive_rows = first + jnp.arange(CENTRES, dtype=jnp.int32) < live_count
    in_use = (jnp.arange(slot_n, dtype=jnp.int32)[None, :] < block_counts[:, None]) & alive_rows[:, None]
    pair_mask = jnp.where(in_use, jnp.float32(1.0), jnp.float32(0.0))

    def energy_of(centre_arg, neigh_arg):
        return block_energy(centre_arg, neigh_arg, centre_kind, neigh_kind, pair_mask, *params)
    energy, pullback = jax.vjp(energy_of, centre_pos, neigh_pos)
    grad_c, grad_n = pullback(jnp.ones_like(energy))
    current = lax.dynamic_slice_in_dim(forces, first, CENTRES, 1)
    forces = lax.dynamic_update_slice_in_dim(forces, current - grad_c, first, 1)
    return forces.at[:, neigh_idx.reshape(-1)].add(-grad_n.reshape(3, -1))

def domain_forces(ext_pos, ext_kinds, neighbours, counts, live_count, params):

    def one_block(forces, block_id):
        return (block_update(forces, block_id, ext_pos, ext_kinds, neighbours, counts, live_count, params), None)
    blocks = jnp.arange(neighbours.shape[0] // CENTRES, dtype=jnp.int32)
    return lax.scan(one_block, jnp.zeros((3, ext_pos.shape[1]), jnp.float32), blocks)[0]

def evaluate(coords, species, send_list, neighbours, neighbour_count, live_atoms, params):
    dev_n = N_GX * N_YZ
    pos_dev = coords.reshape(3, dev_n, ATOM_DEV).transpose(1, 0, 2)
    spec_dev = species.reshape(dev_n, ATOM_DEV)
    sends = send_list.reshape(8, dev_n, GHOSTS).transpose(1, 0, 2)
    sent_pos = jax.vmap(lambda pos_one, send_one: pos_one[:, send_one])(pos_dev, sends)
    sent_spec = jax.vmap(lambda spec_one, send_one: spec_one[send_one])(spec_dev, sends)
    ghost_pos = []
    ghost_spec = []
    for direction, (step_a, step_b) in enumerate(OFFSETS):
        grid_pos = sent_pos[:, :, direction].reshape(N_GX, N_YZ, 3, GHOSTS)
        ghost_pos.append(jnp.roll(grid_pos, (step_a, step_b), axis=(0, 1)).reshape(dev_n, 3, GHOSTS))
        grid_spec = sent_spec[:, direction].reshape(N_GX, N_YZ, GHOSTS)
        ghost_spec.append(jnp.roll(grid_spec, (step_a, step_b), axis=(0, 1)).reshape(dev_n, GHOSTS))
    ext_pos = jnp.concatenate([pos_dev] + ghost_pos, axis=2)
    ext_spec = jnp.concatenate([spec_dev] + ghost_spec, axis=1)
    ext_kinds = (ext_spec[:, :, None] == jnp.arange(SPECIES, dtype=jnp.int32)[None, None, :]).astype(jnp.bfloat16)
    nb_dev = neighbours.reshape(dev_n, ATOM_DEV, SLOTS)
    cnt_dev = neighbour_count.reshape(dev_n, ATOM_DEV)
    ext_forces = lax.map(lambda items: domain_forces(items[0], items[1], items[2], items[3], items[4], params), (ext_pos, ext_kinds, nb_dev, cnt_dev, live_atoms))
    local = ext_forces[:, :, :ATOM_DEV]
    returned = []
    for direction, (step_a, step_b) in enumerate(OFFSETS):
        start_col = ATOM_DEV + direction * GHOSTS
        grid_force = ext_forces[:, :, start_col:start_col + GHOSTS].reshape(N_GX, N_YZ, 3, GHOSTS)
        returned.append(jnp.roll(grid_force, (-step_a, -step_b), axis=(0, 1)).reshape(dev_n, 3, GHOSTS))
    returned = jnp.stack(returned, axis=2)
    local = jax.vmap(lambda force_one, send_one, back_one: force_one.at[:, send_one.reshape(-1)].add(back_one.reshape(3, -1)))(local, sends, returned)
    return local.transpose(1, 0, 2).reshape(3, dev_n * ATOM_DEV)

def reference(positions, velocities, forces_start, species, live_atoms, send_list, neighbours, neighbour_count, radial_weight, species_embed, env_weight, latent_weight, readout):
    params = (radial_weight, species_embed, env_weight, latent_weight, readout)
    inverse = inverse_mass(species)
    half = velocities + 0.5 * STEP * inverse * forces_start
    moved = positions + STEP * half
    forces_mid = evaluate(moved, species, send_list, neighbours, neighbour_count, live_atoms, params)
    velocities_mid = half + 0.5 * STEP * inverse * forces_mid
    half_two = velocities_mid + 0.5 * STEP * inverse * forces_mid
    positions_end = moved + STEP * half_two
    forces_end = evaluate(positions_end, species, send_list, neighbours, neighbour_count, live_atoms, params)
    velocities_end = half_two + 0.5 * STEP * inverse * forces_end
    return (positions_end, velocities_end, forces_end)
```

```python
import jax
import jax.numpy as jnp
from jax import lax
from jax.experimental import pallas as pl
from jax.experimental.pallas import tpu as pltpu
from jax.sharding import PartitionSpec as P

SPECIES = 8
RADIUS = 6.0
STEP = 0.25
COUPLING = 4.0
MASSES = (1.008, 12.011, 14.007, 15.999, 32.06, 22.99, 35.45, 30.97)

LANES = 256
BASIS_PAD = 16

F32 = jnp.float32
BF16 = jnp.bfloat16


def mm(left, right):
    return jnp.dot(left, right, preferred_element_type=F32)


def mm_nt(left, right):
    return lax.dot_general(left, right, (((1,), (1,)), ((), ())), preferred_element_type=F32)


def split3(values):
    high = values.astype(BF16)
    rest = values - high.astype(F32)
    mid = rest.astype(BF16)
    low = (rest - mid.astype(F32)).astype(BF16)
    return jnp.concatenate([high.astype(F32), mid.astype(F32), low.astype(F32)], axis=0).astype(BF16)


def one_hot(ids, rows):
    row_ids = lax.broadcasted_iota(jnp.int32, (rows, ids.shape[1]), 0)
    return jnp.where(row_ids == ids, 1.0, 0.0).astype(BF16)


def compact_kernel(live_ref, count_ref, slots_ref, neigh_ref, centre_ref, total_ref):
    atom_n = count_ref.shape[1]
    slot_n = slots_ref.shape[0]
    blocks, lanes = neigh_ref.shape
    atom_row = lax.broadcasted_iota(jnp.int32, (1, atom_n), 1)
    used = jnp.where(atom_row < live_ref[0], count_ref[...], 0).astype(F32)
    row_i = lax.broadcasted_iota(jnp.int32, (atom_n, atom_n), 0)
    col_i = lax.broadcasted_iota(jnp.int32, (atom_n, atom_n), 1)
    end = jnp.sum(jnp.where(col_i <= row_i, used, 0.0), axis=1, keepdims=True)
    own = jnp.sum(jnp.where(col_i == row_i, used, 0.0), axis=1, keepdims=True)
    total = jnp.sum(used)
    total_ref[0] = total.astype(jnp.int32)
    lane = lax.broadcasted_iota(jnp.int32, (1, lanes), 1)

    def one_block(block, carry):
        place = (lane + block * lanes).astype(F32)
        past = end <= place
        centre = jnp.sum(jnp.where(past, 1.0, 0.0), axis=0, keepdims=True)
        start = jnp.sum(jnp.where(past, own, 0.0), axis=0, keepdims=True)
        slot = (place - start).astype(jnp.int32)
        centre_id = centre.astype(jnp.int32)
        rows = mm(slots_ref[...], one_hot(centre_id, atom_n))
        slot_ids = lax.broadcasted_iota(jnp.int32, (slot_n, lanes), 0)
        neigh = jnp.sum(jnp.where(slot_ids == slot, rows, 0.0), axis=0, keepdims=True)
        valid = place < total
        neigh_ref[pl.ds(block, 1), :] = jnp.where(valid, neigh.astype(jnp.int32), -1)
        centre_ref[pl.ds(block, 1), :] = jnp.where(valid, centre_id, -1)
        return carry

    lax.fori_loop(0, blocks, one_block, 0)


def compact_pairs(live_atoms, neighbour_count, neighbours):
    atom_n, slot_n = neighbours.shape
    blocks = atom_n * slot_n // LANES
    smem = pl.BlockSpec(memory_space=pltpu.SMEM)
    vmem = pl.BlockSpec(memory_space=pltpu.VMEM)
    return pl.pallas_call(
        compact_kernel,
        out_shape=(
            jax.ShapeDtypeStruct((blocks, LANES), jnp.int32),
            jax.ShapeDtypeStruct((blocks, LANES), jnp.int32),
            jax.ShapeDtypeStruct((1,), jnp.int32),
        ),
        in_specs=[smem, vmem, vmem],
        out_specs=(vmem, vmem, smem),
        compiler_params=pltpu.CompilerParams(vmem_limit_bytes=16 * 2**20),
        name="compact_pairs",
    )(live_atoms, neighbour_count.reshape(1, atom_n), neighbours.T.astype(BF16))


def silu_pair(half_in):
    bent = jnp.tanh(half_in)
    part = half_in * bent
    return half_in + part, (1.0 + bent) * (1.0 + (half_in - part))


def force_kernel(
    total_ref,
    neigh_ref,
    centre_ref,
    pos_ref,
    kind_ref,
    embed_ref,
    radial_ref,
    env_t_ref,
    latent_t_ref,
    back_ref,
    back_inner_ref,
    readout_ref,
    radial_back_ref,
    out_ref,
    hot_s,
    use_s,
    u_s,
    hidden_s,
    slope_s,
    raw_s,
    bent_s,
    ain_s,
    energy_s,
    c_s,
    dc_s,
    f_s,
):
    blocks, lanes = neigh_ref.shape
    ext_n = pos_ref.shape[1]
    atom_n = hot_s.shape[1] - ext_n
    basis_n = SPECIES
    features = env_t_ref.shape[0]
    count = (total_ref[0] + lanes - 1) // lanes
    scale = COUPLING * (blocks * lanes // atom_n) ** (-0.5)

    pos8 = jnp.concatenate([pos_ref[...], jnp.zeros((5, ext_n), F32)], axis=0) * (1.0 / RADIUS)
    pos_parts = split3(jnp.concatenate([pos8, -pos8[:, :atom_n]], axis=1))
    row8 = lax.broadcasted_iota(jnp.int32, (SPECIES, ext_n), 0)
    kinds = jnp.where(row8 == kind_ref[...], 1.0, 0.0)
    none = jnp.zeros((SPECIES, ext_n), F32)
    neigh_embed = mm(embed_ref[...], jnp.concatenate([kinds, none], axis=0).astype(BF16))
    own_embed = mm(
        embed_ref[...],
        jnp.concatenate([none, kinds], axis=0)[:, :atom_n].astype(BF16),
    )
    weight_in = jnp.concatenate(
        [neigh_embed, own_embed, radial_ref[...].astype(F32)], axis=1
    ).astype(BF16)

    mid_row = lax.broadcasted_iota(jnp.int32, (BASIS_PAD, lanes), 0).astype(F32)
    mids = (mid_row + 0.5) / basis_n
    sharp = 2.0 * basis_n * basis_n

    def geometry(block):
        vec = u_s[block]
        square = jnp.sum(vec * vec, axis=0, keepdims=True)
        inside = jnp.maximum(1.0 - square, 0.0)
        inside = jnp.where(centre_ref[pl.ds(block, 1), :] >= 0, inside, 0.0)
        apart = square - mids
        return vec, inside, apart, jnp.exp(-sharp * apart * apart)

    c_s[...] = jnp.zeros_like(c_s)
    dc_s[...] = jnp.zeros_like(dc_s)
    f_s[...] = jnp.zeros_like(f_s)

    def first(block, carry):
        hot_j = one_hot(neigh_ref[pl.ds(block, 1), :], ext_n)
        hot_c = one_hot(centre_ref[pl.ds(block, 1), :], atom_n)
        hot = jnp.concatenate([hot_j, hot_c], axis=0)
        hot_s[block] = hot
        parts = mm(pos_parts, hot)
        u_s[block] = parts[0:8] + parts[8:16] + parts[16:24]
        vec, inside, _, basis = geometry(block)
        use = jnp.concatenate([hot_c * vec[k : k + 1].astype(BF16) for k in range(3)], axis=0)
        use_s[block] = use
        pre = mm(weight_in, jnp.concatenate([hot, basis.astype(BF16)], axis=0))
        hidden, slope = silu_pair(pre)
        hidden = hidden.astype(BF16)
        hidden_s[block] = hidden
        slope_s[block] = slope.astype(BF16)
        raw = mm(env_t_ref[...], hidden)
        raw_s[block] = raw
        c_s[...] += mm_nt((raw * (inside * inside)).astype(BF16), use)
        return carry

    lax.fori_loop(0, count, first, 0)
    c_all = c_s[...] * scale
    c_b = c_all.astype(BF16)

    def second(block, carry):
        vec, inside, _, _ = geometry(block)
        use = use_s[block]
        env = inside * inside
        weight = raw_s[block] * env
        inner = weight * mm(c_b, use)
        hidden = hidden_s[block]
        later = mm(latent_t_ref[...], jnp.concatenate([hidden, inner.astype(BF16)], axis=0))
        gain, bent = silu_pair(later)
        bent = bent.astype(BF16)
        bent_s[block] = bent
        energy = mm(readout_ref[...], (hidden.astype(F32) + gain).astype(BF16))
        energy_s[block] = energy[0:8]
        a_in = mm(back_inner_ref[...], bent) * env
        ain_s[block] = a_in
        dc_s[...] += mm_nt((a_in * weight).astype(BF16), use)
        return carry

    lax.fori_loop(0, count, second, 0)
    dc_b = (dc_s[...] * scale).astype(BF16)
    both = jnp.concatenate([c_all.T, dc_s[...].T * scale], axis=1).astype(BF16)

    def third(block, carry):
        vec, inside, apart, basis = geometry(block)
        use = use_s[block]
        hot = hot_s[block]
        env = inside * inside
        raw = raw_s[block]
        weight = raw * env
        a_in = ain_s[block]
        d_weight = a_in * mm(c_b, use) + mm(dc_b, use)
        d_env = jnp.sum(d_weight * raw, axis=0, keepdims=True) + energy_s[block][0:1]
        ones = jnp.ones((BASIS_PAD, lanes), BF16)
        d_hidden = mm(
            back_ref[...], jnp.concatenate([bent_s[block], d_weight.astype(BF16), ones], axis=0)
        )
        d_pre = (d_hidden * slope_s[block].astype(F32)).astype(BF16)
        d_basis = mm(radial_back_ref[...], d_pre)
        d_square = env * jnp.sum(d_basis * basis * apart, axis=0, keepdims=True) * (-2.0 * sharp)
        d_square = d_square - 2.0 * inside * d_env
        d_all = mm(both, jnp.concatenate([a_in * weight, weight], axis=0).astype(BF16))
        hot_c = hot[ext_n:].astype(F32)
        picked = [
            jnp.sum(d_all[k * atom_n : (k + 1) * atom_n] * hot_c, axis=0, keepdims=True)
            for k in range(3)
        ]
        d_vec = jnp.concatenate(picked + [jnp.zeros((5, lanes), F32)], axis=0)
        d_vec = (d_vec + 2.0 * d_square * vec) * (1.0 / RADIUS)
        f_s[...] += mm_nt(split3(d_vec), hot)
        return carry

    lax.fori_loop(0, count, third, 0)
    summed = f_s[0:8] + f_s[8:16] + f_s[16:24]
    on_centre = summed[0:3, ext_n:]
    on_neigh = summed[0:3, :ext_n]
    out_ref[...] = jnp.concatenate([on_centre - on_neigh[:, :atom_n], -on_neigh[:, atom_n:]], axis=1)


def pair_forces(pairs, ext_pos, ext_kind, weights):
    neigh, centre, total = pairs
    blocks, lanes = neigh.shape
    ext_n = ext_pos.shape[1]
    features, latent = weights[2].shape
    atom_n = weights[-1]
    smem = pl.BlockSpec(memory_space=pltpu.SMEM)
    vmem = pl.BlockSpec(memory_space=pltpu.VMEM)
    operands = (total, neigh, centre, ext_pos, ext_kind) + tuple(weights[:-1])
    pair_rows = blocks * lanes
    return pl.pallas_call(
        force_kernel,
        out_shape=jax.ShapeDtypeStruct((3, ext_n), F32),
        in_specs=[smem] + [vmem] * (len(operands) - 1),
        out_specs=vmem,
        scratch_shapes=[
            pltpu.VMEM((blocks, ext_n + atom_n, lanes), BF16),
            pltpu.VMEM((blocks, 3 * atom_n, lanes), BF16),
            pltpu.VMEM((blocks, 8, lanes), F32),
            pltpu.VMEM((blocks, latent, lanes), BF16),
            pltpu.VMEM((blocks, latent, lanes), BF16),
            pltpu.VMEM((blocks, features, lanes), F32),
            pltpu.VMEM((blocks, latent, lanes), BF16),
            pltpu.VMEM((blocks, features, lanes), F32),
            pltpu.VMEM((blocks, 8, lanes), F32),
            pltpu.VMEM((features, 3 * atom_n), F32),
            pltpu.VMEM((features, 3 * atom_n), F32),
            pltpu.VMEM((24, ext_n + atom_n), F32),
        ],
        compiler_params=pltpu.CompilerParams(vmem_limit_bytes=48 * 2**20),
        cost_estimate=pl.CostEstimate(
            flops=pair_rows * latent * 2700, bytes_accessed=4 * 2**20, transcendentals=0
        ),
        name="pair_forces",
    )(*operands)


def padded(cells, sides, width):
    for axis, dim in sides:
        count = lax.axis_size(axis)
        head = lax.slice_in_dim(cells, 0, width, axis=dim)
        tail = lax.slice_in_dim(cells, cells.shape[dim] - width, cells.shape[dim], axis=dim)
        cells = jnp.concatenate(
            [
                lax.ppermute(tail, axis, [(i, (i + 1) % count) for i in range(count)]),
                cells,
                lax.ppermute(head, axis, [((i + 1) % count, i) for i in range(count)]),
            ],
            axis=dim,
        )
    return cells


def inverse_mass(species):
    inv_total = jnp.zeros(species.shape, jnp.float32)
    for spec_id in range(len(MASSES)):
        inv_total = inv_total + jnp.where(
            species == spec_id, jnp.float32(1.0 / MASSES[spec_id]), jnp.float32(0.0)
        )
    return inv_total


def pick_columns(values, select):
    return lax.dot_general(
        values,
        select,
        (((1,), (1,)), ((), ())),
        precision=lax.Precision.HIGHEST,
        preferred_element_type=jnp.float32,
    )


def forward_gx_first(payload):
    ghost_len = payload.shape[2]
    packed = jnp.stack([payload[0:3], payload[5:8]]).reshape(2, -1)
    spread = padded(packed, (("gx", 0),), 1).reshape(4, 3, 4, ghost_len)
    from_low = spread[0]
    from_high = spread[3]
    packed = jnp.stack(
        [
            jnp.stack([from_high[0], payload[3], from_low[0]]),
            jnp.stack([from_high[2], payload[4], from_low[2]]),
        ]
    ).reshape(2, -1)
    spread = padded(packed, (("yz", 0),), 1).reshape(4, 3, 4, ghost_len)
    from_below = spread[0]
    from_above = spread[3]
    return jnp.stack(
        [
            from_above[0],
            from_high[1],
            from_below[0],
            from_above[1],
            from_below[1],
            from_above[2],
            from_low[1],
            from_below[2],
        ]
    )


def return_gx_first(ghost_force):
    ghost_len = ghost_force.shape[2]
    packed = jnp.stack(
        [
            jnp.stack([ghost_force[2], ghost_force[4], ghost_force[7]]),
            jnp.stack([ghost_force[0], ghost_force[3], ghost_force[5]]),
        ]
    ).reshape(2, -1)
    spread = padded(packed, (("yz", 0),), 1).reshape(4, 3, 3, ghost_len)
    from_below = spread[0]
    from_above = spread[3]
    packed = jnp.stack(
        [
            jnp.stack([from_below[2], ghost_force[6], from_above[2]]),
            jnp.stack([from_below[0], ghost_force[1], from_above[0]]),
        ]
    ).reshape(2, -1)
    spread = padded(packed, (("gx", 0),), 1).reshape(4, 3, 3, ghost_len)
    from_low = spread[0]
    from_high = spread[3]
    return jnp.stack(
        [
            from_low[0],
            from_low[1],
            from_low[2],
            from_below[1],
            from_above[1],
            from_high[0],
            from_high[1],
            from_high[2],
        ]
    )


def prepare_weights(radial_weight, species_embed, env_weight, latent_weight, readout, atom_n):
    latent = readout.shape[0]
    half = BF16(0.5)
    radial_t = radial_weight.T * half
    embed_t = jnp.concatenate([species_embed[1].T, species_embed[0].T], axis=1) * half
    radial_pad = BASIS_PAD - radial_weight.shape[0]
    readout_row = readout[None, :]
    zeros = jnp.zeros((BASIS_PAD - 1, latent), BF16)
    folded = (latent_weight[0].astype(F32) * (0.5 * readout_row.astype(F32))).astype(BF16)
    scale = COUPLING * 128**-0.5
    return (
        embed_t,
        jnp.pad(radial_t, ((0, 0), (0, radial_pad))),
        env_weight[0].T,
        latent_weight[0].T * half,
        jnp.concatenate([folded[:latent], env_weight[0], readout[:, None], zeros.T], axis=1),
        folded[latent:],
        jnp.concatenate([readout_row, zeros], axis=0),
        jnp.pad(radial_weight * half, ((0, radial_pad), (0, 0))),
        atom_n,
    )


def body(
    positions,
    velocities,
    forces_start,
    species,
    live_atoms,
    send_list,
    neighbours,
    neighbour_count,
    radial_weight,
    species_embed,
    env_weight,
    latent_weight,
    readout,
):
    atom_n = positions.shape[1]
    ghost_len = send_list.shape[1]
    species_float = species.astype(jnp.float32)
    inverse = inverse_mass(species)
    weights = prepare_weights(
        radial_weight, species_embed, env_weight, latent_weight, readout, atom_n
    )
    pairs = compact_pairs(live_atoms, neighbour_count, neighbours)
    send_pick = (
        send_list.reshape(-1)[:, None] == jnp.arange(atom_n, dtype=jnp.int32)[None, :]
    ).astype(jnp.float32)

    def evaluate(coords):
        sources = jnp.concatenate([coords, species_float[None]], axis=0)
        payload = pick_columns(sources, send_pick).reshape(4, 8, ghost_len).transpose(1, 0, 2)
        ghosts = forward_gx_first(payload)
        ext_pos = jnp.concatenate(
            [coords, ghosts[:, 0:3].transpose(1, 0, 2).reshape(3, -1)], axis=1
        )
        ext_species = jnp.concatenate([species_float, ghosts[:, 3].reshape(-1)])
        forces = pair_forces(pairs, ext_pos, ext_species.astype(jnp.int32)[None, :], weights)
        ghost_force = forces[:, atom_n:].reshape(3, 8, -1).transpose(1, 0, 2)
        returned = return_gx_first(ghost_force)
        back = jnp.dot(
            returned.transpose(1, 0, 2).reshape(3, -1),
            send_pick,
            precision=lax.Precision.HIGHEST,
            preferred_element_type=jnp.float32,
        )
        return forces[:, :atom_n] + back

    half = velocities + 0.5 * STEP * inverse * forces_start
    moved = positions + STEP * half
    forces_mid = evaluate(moved)
    velocities_mid = half + 0.5 * STEP * inverse * forces_mid
    half_two = velocities_mid + 0.5 * STEP * inverse * forces_mid
    positions_end = moved + STEP * half_two
    forces_end = evaluate(positions_end)
    velocities_end = half_two + 0.5 * STEP * inverse * forces_end
    return (positions_end, velocities_end, forces_end)


def solution(mesh):
    placed = (
        P(None, ("gx", "yz")),
        P(None, ("gx", "yz")),
        P(None, ("gx", "yz")),
        P(("gx", "yz")),
        P(("gx", "yz")),
        P(None, ("gx", "yz")),
        P(("gx", "yz"), None),
        P(("gx", "yz")),
        P(),
        P(),
        P(),
        P(),
        P(),
    )
    return jax.shard_map(
        body,
        mesh=mesh,
        in_specs=placed,
        out_specs=(P(None, ("gx", "yz")), P(None, ("gx", "yz")), P(None, ("gx", "yz"))),
        check_vma=False,
    )
```

```python
import jax
import jax.numpy as jnp
from jax import lax
from jax.experimental import pallas as pl
from jax.experimental.pallas import tpu as pltpu
from jax.sharding import PartitionSpec as P

SPECIES = 8
RADIUS = 6.0
STEP = 0.25
COUPLING = 4.0
MASSES = (1.008, 12.011, 14.007, 15.999, 32.06, 22.99, 35.45, 30.97)

LANES = 512
BASIS_PAD = 16

F32 = jnp.float32
BF16 = jnp.bfloat16


def mm(left, right):
    return jnp.dot(left, right, preferred_element_type=F32)


def mm_nt(left, right):
    return lax.dot_general(left, right, (((1,), (1,)), ((), ())), preferred_element_type=F32)


def split3(values):
    high = values.astype(BF16)
    rest = values - high.astype(F32)
    mid = rest.astype(BF16)
    low = (rest - mid.astype(F32)).astype(BF16)
    return jnp.concatenate([high.astype(F32), mid.astype(F32), low.astype(F32)], axis=0).astype(BF16)


def one_hot(ids, rows):
    row_ids = lax.broadcasted_iota(jnp.int32, (rows, ids.shape[1]), 0)
    return jnp.where(row_ids == ids, 1.0, 0.0).astype(BF16)


def compact_kernel(live_ref, count_ref, slots_ref, neigh_ref, centre_ref, total_ref):
    atom_n = count_ref.shape[1]
    slot_n = slots_ref.shape[0]
    blocks, lanes = neigh_ref.shape
    atom_row = lax.broadcasted_iota(jnp.int32, (1, atom_n), 1)
    used = jnp.where(atom_row < live_ref[0], count_ref[...], 0).astype(F32)
    row_i = lax.broadcasted_iota(jnp.int32, (atom_n, atom_n), 0)
    col_i = lax.broadcasted_iota(jnp.int32, (atom_n, atom_n), 1)
    end = jnp.sum(jnp.where(col_i <= row_i, used, 0.0), axis=1, keepdims=True)
    own = jnp.sum(jnp.where(col_i == row_i, used, 0.0), axis=1, keepdims=True)
    total = jnp.sum(used)
    total_ref[0] = total.astype(jnp.int32)
    lane = lax.broadcasted_iota(jnp.int32, (1, lanes), 1)

    def one_block(block, carry):
        place = (lane + block * lanes).astype(F32)
        past = end <= place
        centre = jnp.sum(jnp.where(past, 1.0, 0.0), axis=0, keepdims=True)
        start = jnp.sum(jnp.where(past, own, 0.0), axis=0, keepdims=True)
        slot = (place - start).astype(jnp.int32)
        centre_id = centre.astype(jnp.int32)
        rows = mm(slots_ref[...], one_hot(centre_id, atom_n))
        slot_ids = lax.broadcasted_iota(jnp.int32, (slot_n, lanes), 0)
        neigh = jnp.sum(jnp.where(slot_ids == slot, rows, 0.0), axis=0, keepdims=True)
        valid = place < total
        neigh_ref[pl.ds(block, 1), :] = jnp.where(valid, neigh.astype(jnp.int32), -1)
        centre_ref[pl.ds(block, 1), :] = jnp.where(valid, centre_id, -1)
        return carry

    lax.fori_loop(0, blocks, one_block, 0)


def compact_pairs(live_atoms, neighbour_count, neighbours):
    atom_n, slot_n = neighbours.shape
    blocks = atom_n * slot_n // LANES
    smem = pl.BlockSpec(memory_space=pltpu.SMEM)
    vmem = pl.BlockSpec(memory_space=pltpu.VMEM)
    return pl.pallas_call(
        compact_kernel,
        out_shape=(
            jax.ShapeDtypeStruct((blocks, LANES), jnp.int32),
            jax.ShapeDtypeStruct((blocks, LANES), jnp.int32),
            jax.ShapeDtypeStruct((1,), jnp.int32),
        ),
        in_specs=[smem, vmem, vmem],
        out_specs=(vmem, vmem, smem),
        compiler_params=pltpu.CompilerParams(vmem_limit_bytes=16 * 2**20),
        name="compact_pairs",
    )(live_atoms, neighbour_count.reshape(1, atom_n), neighbours.T.astype(BF16))


def silu_pair(half_in):
    bent = jnp.tanh(half_in)
    part = half_in * bent
    return half_in + part, (1.0 + bent) * (1.0 + (half_in - part))


def force_kernel(
    total_ref,
    neigh_ref,
    centre_ref,
    pos_ref,
    kind_ref,
    embed_ref,
    radial_ref,
    on_hidden_ref,
    on_inner_ref,
    on_bent_ref,
    on_weight_ref,
    readout_ref,
    radial_back_ref,
    out_ref,
    hot_s,
    use_s,
    u_s,
    slope_s,
    raw_s,
    part_s,
    ain_s,
    energy_s,
    c_s,
    dc_s,
    f_s,
):
    blocks, lanes = neigh_ref.shape
    ext_n = pos_ref.shape[1]
    atom_n = hot_s.shape[1] - ext_n
    basis_n = SPECIES
    latent, features = on_inner_ref.shape
    count = (total_ref[0] + lanes - 1) // lanes
    scale = COUPLING * (blocks * lanes // atom_n) ** (-0.5)

    pos8 = jnp.concatenate([pos_ref[...], jnp.zeros((5, ext_n), F32)], axis=0) * (1.0 / RADIUS)
    pos_parts = split3(jnp.concatenate([pos8, -pos8[:, :atom_n]], axis=1))
    row8 = lax.broadcasted_iota(jnp.int32, (SPECIES, ext_n), 0)
    kinds = jnp.where(row8 == kind_ref[...], 1.0, 0.0)
    none = jnp.zeros((SPECIES, ext_n), F32)
    neigh_embed = mm(embed_ref[...], jnp.concatenate([kinds, none], axis=0).astype(BF16))
    own_embed = mm(
        embed_ref[...],
        jnp.concatenate([none, kinds], axis=0)[:, :atom_n].astype(BF16),
    )
    weight_in = jnp.concatenate(
        [neigh_embed, own_embed, radial_ref[...].astype(F32)], axis=1
    ).astype(BF16)

    mid_row = lax.broadcasted_iota(jnp.int32, (BASIS_PAD, lanes), 0).astype(F32)
    mids = (mid_row + 0.5) / basis_n
    sharp = 2.0 * basis_n * basis_n

    def geometry(block):
        vec = u_s[block]
        square = jnp.sum(vec * vec, axis=0, keepdims=True)
        inside = jnp.maximum(1.0 - square, 0.0)
        inside = jnp.where(centre_ref[pl.ds(block, 1), :] >= 0, inside, 0.0)
        apart = square - mids
        return vec, inside, apart, jnp.exp(-sharp * apart * apart)

    c_s[...] = jnp.zeros_like(c_s)
    dc_s[...] = jnp.zeros_like(dc_s)
    f_s[...] = jnp.zeros_like(f_s)

    def first(block, carry):
        hot_j = one_hot(neigh_ref[pl.ds(block, 1), :], ext_n)
        hot_c = one_hot(centre_ref[pl.ds(block, 1), :], atom_n)
        hot = jnp.concatenate([hot_j, hot_c], axis=0)
        hot_s[block] = hot
        parts = mm(pos_parts, hot)
        u_s[block] = parts[0:8] + parts[8:16] + parts[16:24]
        vec, inside, _, basis = geometry(block)
        use = jnp.concatenate([hot_c * vec[k : k + 1].astype(BF16) for k in range(3)], axis=0)
        use_s[block] = use
        pre = mm(weight_in, jnp.concatenate([hot, basis.astype(BF16)], axis=0))
        hidden, slope = silu_pair(pre)
        slope_s[block] = slope.astype(BF16)
        taken = mm(on_hidden_ref[...], hidden.astype(BF16))
        part_s[block] = taken[:latent]
        raw = taken[latent : latent + features]
        raw_s[block] = raw
        energy_s[block] = taken[latent + features : latent + features + 8]
        c_s[...] += mm_nt((raw * (inside * inside)).astype(BF16), use)
        return carry

    lax.fori_loop(0, count, first, 0)
    c_all = c_s[...] * scale
    c_b = c_all.astype(BF16)

    def second(block, carry):
        vec, inside, _, _ = geometry(block)
        use = use_s[block]
        env = inside * inside
        weight = raw_s[block] * env
        inner = weight * mm(c_b, use)
        later = part_s[block] + mm(on_inner_ref[...], inner.astype(BF16))
        gain, bent = silu_pair(later)
        readout = jnp.concatenate([readout_ref[...]] * (lanes // 128), axis=1)
        energy_s[block] += jnp.sum(gain * readout, axis=0, keepdims=True)
        taken = mm(on_bent_ref[...], bent.astype(BF16))
        part_s[block] = taken[:latent]
        a_in = taken[latent:] * env
        ain_s[block] = a_in
        dc_s[...] += mm_nt((a_in * weight).astype(BF16), use)
        return carry

    lax.fori_loop(0, count, second, 0)
    c_dc = jnp.concatenate([c_all, dc_s[...] * scale], axis=0).astype(BF16)
    both = jnp.concatenate([c_all.T, dc_s[...].T * scale], axis=1).astype(BF16)

    def third(block, carry):
        vec, inside, apart, basis = geometry(block)
        use = use_s[block]
        hot = hot_s[block]
        env = inside * inside
        raw = raw_s[block]
        weight = raw * env
        a_in = ain_s[block]
        along = mm(c_dc, use)
        d_weight = a_in * along[:features] + along[features:]
        d_env = jnp.sum(d_weight * raw, axis=0, keepdims=True) + energy_s[block][0:1]
        ones = jnp.ones((BASIS_PAD, lanes), BF16)
        d_hidden = part_s[block] + mm(
            on_weight_ref[...], jnp.concatenate([d_weight.astype(BF16), ones], axis=0)
        )
        d_pre = (d_hidden * slope_s[block].astype(F32)).astype(BF16)
        d_basis = mm(radial_back_ref[...], d_pre)
        d_square = env * jnp.sum(d_basis * basis * apart, axis=0, keepdims=True) * (-2.0 * sharp)
        d_square = d_square - 2.0 * inside * d_env
        d_all = mm(both, jnp.concatenate([a_in * weight, weight], axis=0).astype(BF16))
        hot_c = hot[ext_n:].astype(F32)
        picked = [
            jnp.sum(d_all[k * atom_n : (k + 1) * atom_n] * hot_c, axis=0, keepdims=True)
            for k in range(3)
        ]
        d_vec = jnp.concatenate(picked + [jnp.zeros((5, lanes), F32)], axis=0)
        d_vec = (d_vec + 2.0 * d_square * vec) * (1.0 / RADIUS)
        f_s[...] += mm_nt(split3(d_vec), hot)
        return carry

    lax.fori_loop(0, count, third, 0)
    summed = f_s[0:8] + f_s[8:16] + f_s[16:24]
    on_centre = summed[0:3, ext_n:]
    on_neigh = summed[0:3, :ext_n]
    out_ref[...] = jnp.concatenate([on_centre - on_neigh[:, :atom_n], -on_neigh[:, atom_n:]], axis=1)


def pair_forces(pairs, ext_pos, ext_kind, weights):
    neigh, centre, total = pairs
    blocks, lanes = neigh.shape
    ext_n = ext_pos.shape[1]
    latent, features = weights[3].shape
    atom_n = weights[-1]
    smem = pl.BlockSpec(memory_space=pltpu.SMEM)
    vmem = pl.BlockSpec(memory_space=pltpu.VMEM)
    operands = (total, neigh, centre, ext_pos, ext_kind) + tuple(weights[:-1])
    pair_rows = blocks * lanes
    return pl.pallas_call(
        force_kernel,
        out_shape=jax.ShapeDtypeStruct((3, ext_n), F32),
        in_specs=[smem] + [vmem] * (len(operands) - 1),
        out_specs=vmem,
        scratch_shapes=[
            pltpu.VMEM((blocks, ext_n + atom_n, lanes), BF16),
            pltpu.VMEM((blocks, 3 * atom_n, lanes), BF16),
            pltpu.VMEM((blocks, 8, lanes), F32),
            pltpu.VMEM((blocks, latent, lanes), BF16),
            pltpu.VMEM((blocks, features, lanes), F32),
            pltpu.VMEM((blocks, latent, lanes), F32),
            pltpu.VMEM((blocks, features, lanes), F32),
            pltpu.VMEM((blocks, 8, lanes), F32),
            pltpu.VMEM((features, 3 * atom_n), F32),
            pltpu.VMEM((features, 3 * atom_n), F32),
            pltpu.VMEM((24, ext_n + atom_n), F32),
        ],
        compiler_params=pltpu.CompilerParams(vmem_limit_bytes=48 * 2**20),
        cost_estimate=pl.CostEstimate(
            flops=pair_rows * latent * 2700, bytes_accessed=4 * 2**20, transcendentals=0
        ),
        name="pair_forces",
    )(*operands)


def padded(cells, sides, width):
    for axis, dim in sides:
        count = lax.axis_size(axis)
        head = lax.slice_in_dim(cells, 0, width, axis=dim)
        tail = lax.slice_in_dim(cells, cells.shape[dim] - width, cells.shape[dim], axis=dim)
        cells = jnp.concatenate(
            [
                lax.ppermute(tail, axis, [(i, (i + 1) % count) for i in range(count)]),
                cells,
                lax.ppermute(head, axis, [((i + 1) % count, i) for i in range(count)]),
            ],
            axis=dim,
        )
    return cells


def inverse_mass(species):
    inv_total = jnp.zeros(species.shape, jnp.float32)
    for spec_id in range(len(MASSES)):
        inv_total = inv_total + jnp.where(
            species == spec_id, jnp.float32(1.0 / MASSES[spec_id]), jnp.float32(0.0)
        )
    return inv_total


def pick_columns(values, select):
    return lax.dot_general(
        values,
        select,
        (((1,), (1,)), ((), ())),
        precision=lax.Precision.HIGHEST,
        preferred_element_type=jnp.float32,
    )


def forward_gx_first(payload):
    ghost_len = payload.shape[2]
    packed = jnp.stack([payload[0:3], payload[5:8]]).reshape(2, -1)
    spread = padded(packed, (("gx", 0),), 1).reshape(4, 3, 4, ghost_len)
    from_low = spread[0]
    from_high = spread[3]
    packed = jnp.stack(
        [
            jnp.stack([from_high[0], payload[3], from_low[0]]),
            jnp.stack([from_high[2], payload[4], from_low[2]]),
        ]
    ).reshape(2, -1)
    spread = padded(packed, (("yz", 0),), 1).reshape(4, 3, 4, ghost_len)
    from_below = spread[0]
    from_above = spread[3]
    return jnp.stack(
        [
            from_above[0],
            from_high[1],
            from_below[0],
            from_above[1],
            from_below[1],
            from_above[2],
            from_low[1],
            from_below[2],
        ]
    )


def return_gx_first(ghost_force):
    ghost_len = ghost_force.shape[2]
    packed = jnp.stack(
        [
            jnp.stack([ghost_force[2], ghost_force[4], ghost_force[7]]),
            jnp.stack([ghost_force[0], ghost_force[3], ghost_force[5]]),
        ]
    ).reshape(2, -1)
    spread = padded(packed, (("yz", 0),), 1).reshape(4, 3, 3, ghost_len)
    from_below = spread[0]
    from_above = spread[3]
    packed = jnp.stack(
        [
            jnp.stack([from_below[2], ghost_force[6], from_above[2]]),
            jnp.stack([from_below[0], ghost_force[1], from_above[0]]),
        ]
    ).reshape(2, -1)
    spread = padded(packed, (("gx", 0),), 1).reshape(4, 3, 3, ghost_len)
    from_low = spread[0]
    from_high = spread[3]
    return jnp.stack(
        [
            from_low[0],
            from_low[1],
            from_low[2],
            from_below[1],
            from_above[1],
            from_high[0],
            from_high[1],
            from_high[2],
        ]
    )


def prepare_weights(radial_weight, species_embed, env_weight, latent_weight, readout, atom_n):
    latent = readout.shape[0]
    half = BF16(0.5)
    radial_t = radial_weight.T * half
    embed_t = jnp.concatenate([species_embed[1].T, species_embed[0].T], axis=1) * half
    radial_pad = BASIS_PAD - radial_weight.shape[0]
    readout_row = readout[None, :]
    zeros = jnp.zeros((BASIS_PAD - 1, latent), BF16)
    folded = (latent_weight[0].astype(F32) * (0.5 * readout_row.astype(F32))).astype(BF16)
    latent_t = latent_weight[0].T * half
    return (
        embed_t,
        jnp.pad(radial_t, ((0, 0), (0, radial_pad))),
        jnp.concatenate([latent_t[:, :latent], env_weight[0].T, readout_row, zeros], axis=0),
        latent_t[:, latent:],
        folded,
        jnp.concatenate([env_weight[0], readout[:, None], zeros.T], axis=1),
        jnp.broadcast_to(readout.astype(F32)[:, None], (latent, 128)),
        jnp.pad(radial_weight * half, ((0, radial_pad), (0, 0))),
        atom_n,
    )


def body(
    positions,
    velocities,
    forces_start,
    species,
    live_atoms,
    send_list,
    neighbours,
    neighbour_count,
    radial_weight,
    species_embed,
    env_weight,
    latent_weight,
    readout,
):
    atom_n = positions.shape[1]
    ghost_len = send_list.shape[1]
    species_float = species.astype(jnp.float32)
    inverse = inverse_mass(species)
    weights = prepare_weights(
        radial_weight, species_embed, env_weight, latent_weight, readout, atom_n
    )
    pairs = compact_pairs(live_atoms, neighbour_count, neighbours)
    send_pick = (
        send_list.reshape(-1)[:, None] == jnp.arange(atom_n, dtype=jnp.int32)[None, :]
    ).astype(jnp.float32)

    def evaluate(coords):
        sources = jnp.concatenate([coords, species_float[None]], axis=0)
        payload = pick_columns(sources, send_pick).reshape(4, 8, ghost_len).transpose(1, 0, 2)
        ghosts = forward_gx_first(payload)
        ext_pos = jnp.concatenate(
            [coords, ghosts[:, 0:3].transpose(1, 0, 2).reshape(3, -1)], axis=1
        )
        ext_species = jnp.concatenate([species_float, ghosts[:, 3].reshape(-1)])
        forces = pair_forces(pairs, ext_pos, ext_species.astype(jnp.int32)[None, :], weights)
        ghost_force = forces[:, atom_n:].reshape(3, 8, -1).transpose(1, 0, 2)
        returned = return_gx_first(ghost_force)
        back = jnp.dot(
            returned.transpose(1, 0, 2).reshape(3, -1),
            send_pick,
            precision=lax.Precision.HIGHEST,
            preferred_element_type=jnp.float32,
        )
        return forces[:, :atom_n] + back

    half = velocities + 0.5 * STEP * inverse * forces_start
    moved = positions + STEP * half
    forces_mid = evaluate(moved)
    velocities_mid = half + 0.5 * STEP * inverse * forces_mid
    half_two = velocities_mid + 0.5 * STEP * inverse * forces_mid
    positions_end = moved + STEP * half_two
    forces_end = evaluate(positions_end)
    velocities_end = half_two + 0.5 * STEP * inverse * forces_end
    return (positions_end, velocities_end, forces_end)


def solution(mesh):
    placed = (
        P(None, ("gx", "yz")),
        P(None, ("gx", "yz")),
        P(None, ("gx", "yz")),
        P(("gx", "yz")),
        P(("gx", "yz")),
        P(None, ("gx", "yz")),
        P(("gx", "yz"), None),
        P(("gx", "yz")),
        P(),
        P(),
        P(),
        P(),
        P(),
    )
    return jax.shard_map(
        body,
        mesh=mesh,
        in_specs=placed,
        out_specs=(P(None, ("gx", "yz")), P(None, ("gx", "yz")), P(None, ("gx", "yz"))),
        check_vma=False,
    )
```

```python
import jax
import jax.numpy as jnp
from jax import lax
from jax.experimental import pallas as pl
from jax.experimental.pallas import tpu as pltpu
from jax.sharding import PartitionSpec as P

SPECIES = 8
RADIUS = 6.0
STEP = 0.25
COUPLING = 4.0
MASSES = (1.008, 12.011, 14.007, 15.999, 32.06, 22.99, 35.45, 30.97)

LANES = 1024
BASIS_PAD = 16

F32 = jnp.float32
BF16 = jnp.bfloat16


def mm(left, right):
    return jnp.dot(left, right, preferred_element_type=F32)


def mm_nt(left, right):
    return lax.dot_general(left, right, (((1,), (1,)), ((), ())), preferred_element_type=F32)


def split3(values):
    high = values.astype(BF16)
    rest = values - high.astype(F32)
    mid = rest.astype(BF16)
    low = (rest - mid.astype(F32)).astype(BF16)
    return jnp.concatenate([high.astype(F32), mid.astype(F32), low.astype(F32)], axis=0).astype(BF16)


def one_hot(ids, rows):
    row_ids = lax.broadcasted_iota(jnp.int32, (rows, ids.shape[1]), 0)
    return jnp.where(row_ids == ids, 1.0, 0.0).astype(BF16)


def compact_kernel(live_ref, count_ref, slots_ref, neigh_ref, centre_ref, total_ref):
    atom_n = count_ref.shape[1]
    slot_n = slots_ref.shape[0]
    blocks, lanes = neigh_ref.shape
    atom_row = lax.broadcasted_iota(jnp.int32, (1, atom_n), 1)
    used = jnp.where(atom_row < live_ref[0], count_ref[...], 0).astype(F32)
    row_i = lax.broadcasted_iota(jnp.int32, (atom_n, atom_n), 0)
    col_i = lax.broadcasted_iota(jnp.int32, (atom_n, atom_n), 1)
    end = jnp.sum(jnp.where(col_i <= row_i, used, 0.0), axis=1, keepdims=True)
    own = jnp.sum(jnp.where(col_i == row_i, used, 0.0), axis=1, keepdims=True)
    total = jnp.sum(used)
    total_ref[0] = total.astype(jnp.int32)
    lane = lax.broadcasted_iota(jnp.int32, (1, lanes), 1)

    def one_block(block, carry):
        place = (lane + block * lanes).astype(F32)
        past = end <= place
        centre = jnp.sum(jnp.where(past, 1.0, 0.0), axis=0, keepdims=True)
        start = jnp.sum(jnp.where(past, own, 0.0), axis=0, keepdims=True)
        slot = (place - start).astype(jnp.int32)
        centre_id = centre.astype(jnp.int32)
        rows = mm(slots_ref[...], one_hot(centre_id, atom_n))
        slot_ids = lax.broadcasted_iota(jnp.int32, (slot_n, lanes), 0)
        neigh = jnp.sum(jnp.where(slot_ids == slot, rows, 0.0), axis=0, keepdims=True)
        valid = place < total
        neigh_ref[pl.ds(block, 1), :] = jnp.where(valid, neigh.astype(jnp.int32), -1)
        centre_ref[pl.ds(block, 1), :] = jnp.where(valid, centre_id, -1)
        return carry

    lax.fori_loop(0, blocks, one_block, 0)


def compact_pairs(live_atoms, neighbour_count, neighbours):
    atom_n, slot_n = neighbours.shape
    blocks = atom_n * slot_n // LANES
    smem = pl.BlockSpec(memory_space=pltpu.SMEM)
    vmem = pl.BlockSpec(memory_space=pltpu.VMEM)
    return pl.pallas_call(
        compact_kernel,
        out_shape=(
            jax.ShapeDtypeStruct((blocks, LANES), jnp.int32),
            jax.ShapeDtypeStruct((blocks, LANES), jnp.int32),
            jax.ShapeDtypeStruct((1,), jnp.int32),
        ),
        in_specs=[smem, vmem, vmem],
        out_specs=(vmem, vmem, smem),
        compiler_params=pltpu.CompilerParams(vmem_limit_bytes=16 * 2**20),
        name="compact_pairs",
    )(live_atoms, neighbour_count.reshape(1, atom_n), neighbours.T.astype(BF16))


def silu_pair(half_in):
    bent = jnp.tanh(half_in)
    part = half_in * bent
    return half_in + part, (1.0 + bent) * (1.0 + (half_in - part))


def force_kernel(
    total_ref,
    neigh_ref,
    centre_ref,
    pos_ref,
    kind_ref,
    embed_ref,
    radial_ref,
    on_hidden_ref,
    on_inner_ref,
    on_bent_ref,
    on_weight_ref,
    readout_ref,
    radial_back_ref,
    out_ref,
    hot_s,
    use_s,
    u_s,
    slope_s,
    raw_s,
    part_s,
    ain_s,
    energy_s,
    c_s,
    dc_s,
    f_s,
):
    blocks, lanes = neigh_ref.shape
    ext_n = pos_ref.shape[1]
    atom_n = hot_s.shape[1] - ext_n
    basis_n = SPECIES
    latent, features = on_inner_ref.shape
    count = (total_ref[0] + lanes - 1) // lanes
    scale = COUPLING * (blocks * lanes // atom_n) ** (-0.5)

    pos8 = jnp.concatenate([pos_ref[...], jnp.zeros((5, ext_n), F32)], axis=0) * (1.0 / RADIUS)
    pos_parts = split3(jnp.concatenate([pos8, -pos8[:, :atom_n]], axis=1))
    row8 = lax.broadcasted_iota(jnp.int32, (SPECIES, ext_n), 0)
    kinds = jnp.where(row8 == kind_ref[...], 1.0, 0.0)
    none = jnp.zeros((SPECIES, ext_n), F32)
    neigh_embed = mm(embed_ref[...], jnp.concatenate([kinds, none], axis=0).astype(BF16))
    own_embed = mm(
        embed_ref[...],
        jnp.concatenate([none, kinds], axis=0)[:, :atom_n].astype(BF16),
    )
    weight_in = jnp.concatenate(
        [neigh_embed, own_embed, radial_ref[...].astype(F32)], axis=1
    ).astype(BF16)

    mid_row = lax.broadcasted_iota(jnp.int32, (BASIS_PAD, lanes), 0).astype(F32)
    mids = (mid_row + 0.5) / basis_n
    sharp = 2.0 * basis_n * basis_n

    def geometry(block):
        vec = u_s[block]
        square = jnp.sum(vec * vec, axis=0, keepdims=True)
        inside = jnp.maximum(1.0 - square, 0.0)
        inside = jnp.where(centre_ref[pl.ds(block, 1), :] >= 0, inside, 0.0)
        apart = square - mids
        return vec, inside, apart, jnp.exp(-sharp * apart * apart)

    c_s[...] = jnp.zeros_like(c_s)
    dc_s[...] = jnp.zeros_like(dc_s)
    f_s[...] = jnp.zeros_like(f_s)

    def first(block, carry):
        hot_j = one_hot(neigh_ref[pl.ds(block, 1), :], ext_n)
        hot_c = one_hot(centre_ref[pl.ds(block, 1), :], atom_n)
        hot = jnp.concatenate([hot_j, hot_c], axis=0)
        hot_s[block] = hot
        parts = mm(pos_parts, hot)
        u_s[block] = parts[0:8] + parts[8:16] + parts[16:24]
        vec, inside, _, basis = geometry(block)
        use = jnp.concatenate([hot_c * vec[k : k + 1].astype(BF16) for k in range(3)], axis=0)
        use_s[block] = use
        pre = mm(weight_in, jnp.concatenate([hot, basis.astype(BF16)], axis=0))
        hidden, slope = silu_pair(pre)
        slope_s[block] = slope.astype(BF16)
        taken = mm(on_hidden_ref[...], hidden.astype(BF16))
        part_s[block] = taken[:latent]
        raw = taken[latent : latent + features]
        raw_s[block] = raw
        energy_s[block] = taken[latent + features : latent + features + 8]
        c_s[...] += mm_nt((raw * (inside * inside)).astype(BF16), use)
        return carry

    lax.fori_loop(0, count, first, 0)
    c_all = c_s[...] * scale
    c_b = c_all.astype(BF16)

    def second(block, carry):
        vec, inside, _, _ = geometry(block)
        use = use_s[block]
        env = inside * inside
        weight = raw_s[block] * env
        inner = weight * mm(c_b, use)
        later = part_s[block] + mm(on_inner_ref[...], inner.astype(BF16))
        gain, bent = silu_pair(later)
        readout = jnp.concatenate([readout_ref[...]] * (lanes // 128), axis=1)
        energy_s[block] += jnp.sum(gain * readout, axis=0, keepdims=True)
        taken = mm(on_bent_ref[...], bent.astype(BF16))
        part_s[block] = taken[:latent]
        a_in = taken[latent:] * env
        ain_s[block] = a_in
        dc_s[...] += mm_nt((a_in * weight).astype(BF16), use)
        return carry

    lax.fori_loop(0, count, second, 0)
    c_dc = jnp.concatenate([c_all, dc_s[...] * scale], axis=0).astype(BF16)
    both = jnp.concatenate([c_all.T, dc_s[...].T * scale], axis=1).astype(BF16)

    def third(block, carry):
        vec, inside, apart, basis = geometry(block)
        use = use_s[block]
        hot = hot_s[block]
        env = inside * inside
        raw = raw_s[block]
        weight = raw * env
        a_in = ain_s[block]
        along = mm(c_dc, use)
        d_weight = a_in * along[:features] + along[features:]
        d_env = jnp.sum(d_weight * raw, axis=0, keepdims=True) + energy_s[block][0:1]
        ones = jnp.ones((BASIS_PAD, lanes), BF16)
        d_hidden = part_s[block] + mm(
            on_weight_ref[...], jnp.concatenate([d_weight.astype(BF16), ones], axis=0)
        )
        d_pre = (d_hidden * slope_s[block].astype(F32)).astype(BF16)
        d_basis = mm(radial_back_ref[...], d_pre)
        d_square = env * jnp.sum(d_basis * basis * apart, axis=0, keepdims=True) * (-2.0 * sharp)
        d_square = d_square - 2.0 * inside * d_env
        d_all = mm(both, jnp.concatenate([a_in * weight, weight], axis=0).astype(BF16))
        hot_c = hot[ext_n:].astype(F32)
        picked = [
            jnp.sum(d_all[k * atom_n : (k + 1) * atom_n] * hot_c, axis=0, keepdims=True)
            for k in range(3)
        ]
        d_vec = jnp.concatenate(picked + [jnp.zeros((5, lanes), F32)], axis=0)
        d_vec = (d_vec + 2.0 * d_square * vec) * (1.0 / RADIUS)
        f_s[...] += mm_nt(split3(d_vec), hot)
        return carry

    lax.fori_loop(0, count, third, 0)
    summed = f_s[0:8] + f_s[8:16] + f_s[16:24]
    on_centre = summed[0:3, ext_n:]
    on_neigh = summed[0:3, :ext_n]
    out_ref[...] = jnp.concatenate([on_centre - on_neigh[:, :atom_n], -on_neigh[:, atom_n:]], axis=1)


def pair_forces(pairs, ext_pos, ext_kind, weights):
    neigh, centre, total = pairs
    blocks, lanes = neigh.shape
    ext_n = ext_pos.shape[1]
    latent, features = weights[3].shape
    atom_n = weights[-1]
    smem = pl.BlockSpec(memory_space=pltpu.SMEM)
    vmem = pl.BlockSpec(memory_space=pltpu.VMEM)
    operands = (total, neigh, centre, ext_pos, ext_kind) + tuple(weights[:-1])
    pair_rows = blocks * lanes
    return pl.pallas_call(
        force_kernel,
        out_shape=jax.ShapeDtypeStruct((3, ext_n), F32),
        in_specs=[smem] + [vmem] * (len(operands) - 1),
        out_specs=vmem,
        scratch_shapes=[
            pltpu.VMEM((blocks, ext_n + atom_n, lanes), BF16),
            pltpu.VMEM((blocks, 3 * atom_n, lanes), BF16),
            pltpu.VMEM((blocks, 8, lanes), F32),
            pltpu.VMEM((blocks, latent, lanes), BF16),
            pltpu.VMEM((blocks, features, lanes), F32),
            pltpu.VMEM((blocks, latent, lanes), F32),
            pltpu.VMEM((blocks, features, lanes), F32),
            pltpu.VMEM((blocks, 8, lanes), F32),
            pltpu.VMEM((features, 3 * atom_n), F32),
            pltpu.VMEM((features, 3 * atom_n), F32),
            pltpu.VMEM((24, ext_n + atom_n), F32),
        ],
        compiler_params=pltpu.CompilerParams(vmem_limit_bytes=48 * 2**20),
        cost_estimate=pl.CostEstimate(
            flops=pair_rows * latent * 2700, bytes_accessed=4 * 2**20, transcendentals=0
        ),
        name="pair_forces",
    )(*operands)


def padded(cells, sides, width):
    for axis, dim in sides:
        count = lax.axis_size(axis)
        head = lax.slice_in_dim(cells, 0, width, axis=dim)
        tail = lax.slice_in_dim(cells, cells.shape[dim] - width, cells.shape[dim], axis=dim)
        cells = jnp.concatenate(
            [
                lax.ppermute(tail, axis, [(i, (i + 1) % count) for i in range(count)]),
                cells,
                lax.ppermute(head, axis, [((i + 1) % count, i) for i in range(count)]),
            ],
            axis=dim,
        )
    return cells


def inverse_mass(species):
    inv_total = jnp.zeros(species.shape, jnp.float32)
    for spec_id in range(len(MASSES)):
        inv_total = inv_total + jnp.where(
            species == spec_id, jnp.float32(1.0 / MASSES[spec_id]), jnp.float32(0.0)
        )
    return inv_total


def pick_columns(values, select):
    return lax.dot_general(
        values,
        select,
        (((1,), (1,)), ((), ())),
        precision=lax.Precision.HIGHEST,
        preferred_element_type=jnp.float32,
    )


def forward_gx_first(payload):
    ghost_len = payload.shape[2]
    packed = jnp.stack([payload[0:3], payload[5:8]]).reshape(2, -1)
    spread = padded(packed, (("gx", 0),), 1).reshape(4, 3, 4, ghost_len)
    from_low = spread[0]
    from_high = spread[3]
    packed = jnp.stack(
        [
            jnp.stack([from_high[0], payload[3], from_low[0]]),
            jnp.stack([from_high[2], payload[4], from_low[2]]),
        ]
    ).reshape(2, -1)
    spread = padded(packed, (("yz", 0),), 1).reshape(4, 3, 4, ghost_len)
    from_below = spread[0]
    from_above = spread[3]
    return jnp.stack(
        [
            from_above[0],
            from_high[1],
            from_below[0],
            from_above[1],
            from_below[1],
            from_above[2],
            from_low[1],
            from_below[2],
        ]
    )


def return_gx_first(ghost_force):
    ghost_len = ghost_force.shape[2]
    packed = jnp.stack(
        [
            jnp.stack([ghost_force[2], ghost_force[4], ghost_force[7]]),
            jnp.stack([ghost_force[0], ghost_force[3], ghost_force[5]]),
        ]
    ).reshape(2, -1)
    spread = padded(packed, (("yz", 0),), 1).reshape(4, 3, 3, ghost_len)
    from_below = spread[0]
    from_above = spread[3]
    packed = jnp.stack(
        [
            jnp.stack([from_below[2], ghost_force[6], from_above[2]]),
            jnp.stack([from_below[0], ghost_force[1], from_above[0]]),
        ]
    ).reshape(2, -1)
    spread = padded(packed, (("gx", 0),), 1).reshape(4, 3, 3, ghost_len)
    from_low = spread[0]
    from_high = spread[3]
    return jnp.stack(
        [
            from_low[0],
            from_low[1],
            from_low[2],
            from_below[1],
            from_above[1],
            from_high[0],
            from_high[1],
            from_high[2],
        ]
    )


def prepare_weights(radial_weight, species_embed, env_weight, latent_weight, readout, atom_n):
    latent = readout.shape[0]
    half = BF16(0.5)
    radial_t = radial_weight.T * half
    embed_t = jnp.concatenate([species_embed[1].T, species_embed[0].T], axis=1) * half
    radial_pad = BASIS_PAD - radial_weight.shape[0]
    readout_row = readout[None, :]
    zeros = jnp.zeros((BASIS_PAD - 1, latent), BF16)
    folded = (latent_weight[0].astype(F32) * (0.5 * readout_row.astype(F32))).astype(BF16)
    latent_t = latent_weight[0].T * half
    return (
        embed_t,
        jnp.pad(radial_t, ((0, 0), (0, radial_pad))),
        jnp.concatenate([latent_t[:, :latent], env_weight[0].T, readout_row, zeros], axis=0),
        latent_t[:, latent:],
        folded,
        jnp.concatenate([env_weight[0], readout[:, None], zeros.T], axis=1),
        jnp.broadcast_to(readout.astype(F32)[:, None], (latent, 128)),
        jnp.pad(radial_weight * half, ((0, radial_pad), (0, 0))),
        atom_n,
    )


def body(
    positions,
    velocities,
    forces_start,
    species,
    live_atoms,
    send_list,
    neighbours,
    neighbour_count,
    radial_weight,
    species_embed,
    env_weight,
    latent_weight,
    readout,
):
    atom_n = positions.shape[1]
    ghost_len = send_list.shape[1]
    species_float = species.astype(jnp.float32)
    inverse = inverse_mass(species)
    weights = prepare_weights(
        radial_weight, species_embed, env_weight, latent_weight, readout, atom_n
    )
    pairs = compact_pairs(live_atoms, neighbour_count, neighbours)
    send_pick = (
        send_list.reshape(-1)[:, None] == jnp.arange(atom_n, dtype=jnp.int32)[None, :]
    ).astype(jnp.float32)

    def evaluate(coords):
        sources = jnp.concatenate([coords, species_float[None]], axis=0)
        payload = pick_columns(sources, send_pick).reshape(4, 8, ghost_len).transpose(1, 0, 2)
        ghosts = forward_gx_first(payload)
        ext_pos = jnp.concatenate(
            [coords, ghosts[:, 0:3].transpose(1, 0, 2).reshape(3, -1)], axis=1
        )
        ext_species = jnp.concatenate([species_float, ghosts[:, 3].reshape(-1)])
        forces = pair_forces(pairs, ext_pos, ext_species.astype(jnp.int32)[None, :], weights)
        ghost_force = forces[:, atom_n:].reshape(3, 8, -1).transpose(1, 0, 2)
        returned = return_gx_first(ghost_force)
        back = jnp.dot(
            returned.transpose(1, 0, 2).reshape(3, -1),
            send_pick,
            precision=lax.Precision.HIGHEST,
            preferred_element_type=jnp.float32,
        )
        return forces[:, :atom_n] + back

    half = velocities + 0.5 * STEP * inverse * forces_start
    moved = positions + STEP * half
    forces_mid = evaluate(moved)
    velocities_mid = half + 0.5 * STEP * inverse * forces_mid
    half_two = velocities_mid + 0.5 * STEP * inverse * forces_mid
    positions_end = moved + STEP * half_two
    forces_end = evaluate(positions_end)
    velocities_end = half_two + 0.5 * STEP * inverse * forces_end
    return (positions_end, velocities_end, forces_end)


def solution(mesh):
    placed = (
        P(None, ("gx", "yz")),
        P(None, ("gx", "yz")),
        P(None, ("gx", "yz")),
        P(("gx", "yz")),
        P(("gx", "yz")),
        P(None, ("gx", "yz")),
        P(("gx", "yz"), None),
        P(("gx", "yz")),
        P(),
        P(),
        P(),
        P(),
        P(),
    )
    return jax.shard_map(
        body,
        mesh=mesh,
        in_specs=placed,
        out_specs=(P(None, ("gx", "yz")), P(None, ("gx", "yz")), P(None, ("gx", "yz"))),
        check_vma=False,
    )
```

```python
import jax
import jax.numpy as jnp
from jax import lax
from jax.experimental import pallas as pl
from jax.experimental.pallas import tpu as pltpu
from jax.sharding import PartitionSpec as P

SPECIES = 8
SLOTS = 128
RADIUS = 6.0
STEP = 0.25
COUPLING = 4.0
MASSES = (1.008, 12.011, 14.007, 15.999, 32.06, 22.99, 35.45, 30.97)

LANES = 512
GATHERED = 4
BASIS_PAD = 16

F32 = jnp.float32
BF16 = jnp.bfloat16


def mm(left, right):
    return jnp.dot(left, right, preferred_element_type=F32)


def mm_nt(left, right):
    return lax.dot_general(left, right, (((1,), (1,)), ((), ())), preferred_element_type=F32)


def split3(values):
    high = values.astype(BF16)
    rest = values - high.astype(F32)
    mid = rest.astype(BF16)
    low = (rest - mid.astype(F32)).astype(BF16)
    return jnp.concatenate([high.astype(F32), mid.astype(F32), low.astype(F32)], axis=0).astype(BF16)


def one_hot(ids, rows):
    row_ids = lax.broadcasted_iota(jnp.int32, (rows, ids.shape[1]), 0)
    return jnp.where(row_ids == ids, 1.0, 0.0).astype(BF16)


def compact_kernel(live_ref, count_ref, slots_ref, neigh_ref, centre_ref, total_ref):
    atom_n = count_ref.shape[1]
    slot_n = slots_ref.shape[0]
    blocks, lanes = neigh_ref.shape
    atom_row = lax.broadcasted_iota(jnp.int32, (1, atom_n), 1)
    used = jnp.where(atom_row < live_ref[0], count_ref[...], 0).astype(F32)
    row_i = lax.broadcasted_iota(jnp.int32, (atom_n, atom_n), 0)
    col_i = lax.broadcasted_iota(jnp.int32, (atom_n, atom_n), 1)
    end = jnp.sum(jnp.where(col_i <= row_i, used, 0.0), axis=1, keepdims=True)
    own = jnp.sum(jnp.where(col_i == row_i, used, 0.0), axis=1, keepdims=True)
    total = jnp.sum(used)
    total_ref[0] = total.astype(jnp.int32)
    lane = lax.broadcasted_iota(jnp.int32, (1, lanes), 1)

    def one_block(block, carry):
        place = (lane + block * lanes).astype(F32)
        past = end <= place
        centre = jnp.sum(jnp.where(past, 1.0, 0.0), axis=0, keepdims=True)
        start = jnp.sum(jnp.where(past, own, 0.0), axis=0, keepdims=True)
        slot = (place - start).astype(jnp.int32)
        centre_id = centre.astype(jnp.int32)
        rows = mm(slots_ref[...], one_hot(centre_id, atom_n))
        slot_ids = lax.broadcasted_iota(jnp.int32, (slot_n, lanes), 0)
        neigh = jnp.sum(jnp.where(slot_ids == slot, rows, 0.0), axis=0, keepdims=True)
        valid = place < total
        neigh_ref[pl.ds(block, 1), :] = jnp.where(valid, neigh.astype(jnp.int32), -1)
        centre_ref[pl.ds(block, 1), :] = jnp.where(valid, centre_id, -1)
        return carry

    lax.fori_loop(0, blocks, one_block, 0)


def compact_pairs(live_atoms, neighbour_count, neighbours):
    atom_n, slot_n = neighbours.shape
    blocks = (atom_n * slot_n // LANES // GATHERED + 1) * GATHERED
    smem = pl.BlockSpec(memory_space=pltpu.SMEM)
    vmem = pl.BlockSpec(memory_space=pltpu.VMEM)
    return pl.pallas_call(
        compact_kernel,
        out_shape=(
            jax.ShapeDtypeStruct((blocks, LANES), jnp.int32),
            jax.ShapeDtypeStruct((blocks, LANES), jnp.int32),
            jax.ShapeDtypeStruct((1,), jnp.int32),
        ),
        in_specs=[smem, vmem, vmem],
        out_specs=(vmem, vmem, smem),
        compiler_params=pltpu.CompilerParams(vmem_limit_bytes=16 * 2**20),
        name="compact_pairs",
    )(live_atoms, neighbour_count.reshape(1, atom_n), neighbours.T.astype(BF16))


def silu_pair(half_in):
    bent = jnp.tanh(half_in)
    part = half_in * bent
    return half_in + part, (1.0 + bent) * (1.0 + (half_in - part))


def force_kernel(
    total_ref,
    neigh_ref,
    centre_ref,
    pos_ref,
    kind_ref,
    embed_ref,
    radial_ref,
    on_hidden_ref,
    on_inner_ref,
    on_bent_ref,
    on_weight_ref,
    readout_ref,
    radial_back_ref,
    out_ref,
    hot_s,
    use_s,
    u_s,
    inside_s,
    slope_s,
    raw_s,
    part_s,
    ain_s,
    energy_s,
    c_s,
    dc_s,
    f_s,
):
    blocks, lanes = neigh_ref.shape
    ext_n = pos_ref.shape[1]
    atom_n = use_s.shape[1] // 3
    basis_n = SPECIES
    latent, features = on_inner_ref.shape
    count = (total_ref[0] + lanes - 1) // lanes
    scale = COUPLING * SLOTS ** (-0.5)

    pos8 = jnp.concatenate([pos_ref[...], jnp.zeros((5, ext_n), F32)], axis=0) * (1.0 / RADIUS)
    pos_parts = split3(jnp.concatenate([pos8, -pos8[:, :atom_n]], axis=1))
    row8 = lax.broadcasted_iota(jnp.int32, (SPECIES, ext_n), 0)
    kinds = jnp.where(row8 == kind_ref[...], 1.0, 0.0)
    none = jnp.zeros((SPECIES, ext_n), F32)
    neigh_embed = mm(embed_ref[...], jnp.concatenate([kinds, none], axis=0).astype(BF16))
    own_embed = mm(
        embed_ref[...],
        jnp.concatenate([none, kinds], axis=0)[:, :atom_n].astype(BF16),
    )
    weight_in = jnp.concatenate(
        [neigh_embed, own_embed, radial_ref[...].astype(F32)], axis=1
    ).astype(BF16)

    mid_row = lax.broadcasted_iota(jnp.int32, (BASIS_PAD, lanes), 0).astype(F32)
    mids = (mid_row + 0.5) / basis_n
    sharp = 2.0 * basis_n * basis_n

    c_s[...] = jnp.zeros_like(c_s)
    dc_s[...] = jnp.zeros_like(dc_s)
    f_s[...] = jnp.zeros_like(f_s)
    for empty in (hot_s, use_s, u_s, inside_s):
        empty[0] = jnp.zeros(empty.shape[1:], empty.dtype)

    def gather(block):
        slot = block + 1
        centre = centre_ref[pl.ds(block, 1), :]
        hot_j = one_hot(neigh_ref[pl.ds(block, 1), :], ext_n)
        hot_c = one_hot(centre, atom_n)
        hot = jnp.concatenate([hot_j, hot_c], axis=0)
        parts = mm(pos_parts, hot)
        vec = parts[0:8] + parts[8:16] + parts[16:24]
        square = jnp.sum(vec * vec, axis=0, keepdims=True)
        apart = square - mids
        basis = jnp.exp(-sharp * apart * apart)
        u_s[slot] = vec
        inside_s[slot] = jnp.where(centre >= 0, jnp.maximum(1.0 - square, 0.0), 0.0)
        use_s[slot] = jnp.concatenate(
            [hot_c * vec[k : k + 1].astype(BF16) for k in range(3)], axis=0
        )
        hot_s[slot] = jnp.concatenate([hot, basis.astype(BF16)], axis=0)

    def gather_some(step, carry):
        for more in range(GATHERED):
            gather(step * GATHERED + more)
        return carry

    lax.fori_loop(0, count // GATHERED + 1, gather_some, 0)

    def pipelined(start, finish, empty):
        def step(slot, carry):
            finish(slot, *carry)
            return start(slot + 1)

        lax.fori_loop(0, count + 1, step, empty)

    no_act = jnp.zeros((latent, lanes), BF16)

    def first_start(slot):
        hidden, slope = silu_pair(mm(weight_in, hot_s[slot]))
        slope_s[slot] = slope.astype(BF16)
        return (hidden.astype(BF16),)

    def first_finish(slot, hidden):
        taken = mm(on_hidden_ref[...], hidden)
        inside = inside_s[slot]
        part_s[slot] = taken[:latent]
        raw = taken[latent : latent + features]
        raw_s[slot] = raw
        energy_s[slot] = taken[latent + features : latent + features + 8]
        c_s[...] += mm_nt((raw * (inside * inside)).astype(BF16), use_s[slot])

    pipelined(first_start, first_finish, (no_act,))
    c_all = c_s[...] * scale
    c_b = c_all.astype(BF16)

    def second_start(slot):
        inside = inside_s[slot]
        inner = raw_s[slot] * (inside * inside) * mm(c_b, use_s[slot])
        later = part_s[slot] + mm(on_inner_ref[...], inner.astype(BF16))
        gain, bent = silu_pair(later)
        readout = jnp.concatenate([readout_ref[...]] * (lanes // 128), axis=1)
        energy_s[slot] += jnp.sum(gain * readout, axis=0, keepdims=True)
        return (bent.astype(BF16),)

    def second_finish(slot, bent):
        inside = inside_s[slot]
        env = inside * inside
        taken = mm(on_bent_ref[...], bent)
        part_s[slot] = taken[:latent]
        a_in = taken[latent:] * env
        ain_s[slot] = a_in
        dc_s[...] += mm_nt((a_in * (raw_s[slot] * env)).astype(BF16), use_s[slot])

    pipelined(second_start, second_finish, (no_act,))
    c_dc = jnp.concatenate([c_all, dc_s[...] * scale], axis=0).astype(BF16)
    both = jnp.concatenate([c_all.T, dc_s[...].T * scale], axis=1).astype(BF16)

    def third_start(slot):
        along = mm(c_dc, use_s[slot])
        d_weight = ain_s[slot] * along[:features] + along[features:]
        d_env = jnp.sum(d_weight * raw_s[slot], axis=0, keepdims=True) + energy_s[slot][0:1]
        ones = jnp.ones((BASIS_PAD, lanes), BF16)
        d_hidden = part_s[slot] + mm(
            on_weight_ref[...], jnp.concatenate([d_weight.astype(BF16), ones], axis=0)
        )
        return (d_hidden * slope_s[slot].astype(F32)).astype(BF16), d_env

    def third_finish(slot, d_pre, d_env):
        hot = hot_s[slot, : ext_n + atom_n]
        vec = u_s[slot]
        inside = inside_s[slot]
        env = inside * inside
        square = jnp.sum(vec * vec, axis=0, keepdims=True)
        apart = square - mids
        basis = jnp.exp(-sharp * apart * apart)
        d_basis = mm(radial_back_ref[...], d_pre)
        d_square = env * jnp.sum(d_basis * basis * apart, axis=0, keepdims=True) * (-2.0 * sharp)
        d_square = d_square - 2.0 * inside * d_env
        weight = raw_s[slot] * env
        d_all = mm(both, jnp.concatenate([ain_s[slot] * weight, weight], axis=0).astype(BF16))
        hot_c = hot[ext_n:].astype(F32)
        picked = [
            jnp.sum(d_all[k * atom_n : (k + 1) * atom_n] * hot_c, axis=0, keepdims=True)
            for k in range(3)
        ]
        d_vec = jnp.concatenate(picked + [jnp.zeros((5, lanes), F32)], axis=0)
        d_vec = (d_vec + 2.0 * d_square * vec) * (1.0 / RADIUS)
        f_s[...] += mm_nt(split3(d_vec), hot)

    pipelined(third_start, third_finish, (no_act, jnp.zeros((1, lanes), F32)))
    summed = f_s[0:8] + f_s[8:16] + f_s[16:24]
    on_centre = summed[0:3, ext_n:]
    on_neigh = summed[0:3, :ext_n]
    out_ref[...] = jnp.concatenate([on_centre - on_neigh[:, :atom_n], -on_neigh[:, atom_n:]], axis=1)


def pair_forces(pairs, ext_pos, ext_kind, weights):
    neigh, centre, total = pairs
    blocks, lanes = neigh.shape
    ext_n = ext_pos.shape[1]
    latent, features = weights[3].shape
    atom_n = weights[-1]
    smem = pl.BlockSpec(memory_space=pltpu.SMEM)
    vmem = pl.BlockSpec(memory_space=pltpu.VMEM)
    operands = (total, neigh, centre, ext_pos, ext_kind) + tuple(weights[:-1])
    pair_rows = blocks * lanes
    slots = blocks + 1
    return pl.pallas_call(
        force_kernel,
        out_shape=jax.ShapeDtypeStruct((3, ext_n), F32),
        in_specs=[smem] + [vmem] * (len(operands) - 1),
        out_specs=vmem,
        scratch_shapes=[
            pltpu.VMEM((slots, ext_n + atom_n + BASIS_PAD, lanes), BF16),
            pltpu.VMEM((slots, 3 * atom_n, lanes), BF16),
            pltpu.VMEM((slots, 8, lanes), F32),
            pltpu.VMEM((slots, 1, lanes), F32),
            pltpu.VMEM((slots, latent, lanes), BF16),
            pltpu.VMEM((slots, features, lanes), F32),
            pltpu.VMEM((slots, latent, lanes), F32),
            pltpu.VMEM((slots, features, lanes), F32),
            pltpu.VMEM((slots, 8, lanes), F32),
            pltpu.VMEM((features, 3 * atom_n), F32),
            pltpu.VMEM((features, 3 * atom_n), F32),
            pltpu.VMEM((24, ext_n + atom_n), F32),
        ],
        compiler_params=pltpu.CompilerParams(vmem_limit_bytes=56 * 2**20),
        cost_estimate=pl.CostEstimate(
            flops=pair_rows * latent * 2700, bytes_accessed=4 * 2**20, transcendentals=0
        ),
        name="pair_forces",
    )(*operands)


def padded(cells, sides, width):
    for axis, dim in sides:
        count = lax.axis_size(axis)
        head = lax.slice_in_dim(cells, 0, width, axis=dim)
        tail = lax.slice_in_dim(cells, cells.shape[dim] - width, cells.shape[dim], axis=dim)
        cells = jnp.concatenate(
            [
                lax.ppermute(tail, axis, [(i, (i + 1) % count) for i in range(count)]),
                cells,
                lax.ppermute(head, axis, [((i + 1) % count, i) for i in range(count)]),
            ],
            axis=dim,
        )
    return cells


def inverse_mass(species):
    inv_total = jnp.zeros(species.shape, jnp.float32)
    for spec_id in range(len(MASSES)):
        inv_total = inv_total + jnp.where(
            species == spec_id, jnp.float32(1.0 / MASSES[spec_id]), jnp.float32(0.0)
        )
    return inv_total


def pick_columns(values, select):
    return lax.dot_general(
        values,
        select,
        (((1,), (1,)), ((), ())),
        precision=lax.Precision.HIGHEST,
        preferred_element_type=jnp.float32,
    )


def forward_gx_first(payload):
    ghost_len = payload.shape[2]
    packed = jnp.stack([payload[0:3], payload[5:8]]).reshape(2, -1)
    spread = padded(packed, (("gx", 0),), 1).reshape(4, 3, 4, ghost_len)
    from_low = spread[0]
    from_high = spread[3]
    packed = jnp.stack(
        [
            jnp.stack([from_high[0], payload[3], from_low[0]]),
            jnp.stack([from_high[2], payload[4], from_low[2]]),
        ]
    ).reshape(2, -1)
    spread = padded(packed, (("yz", 0),), 1).reshape(4, 3, 4, ghost_len)
    from_below = spread[0]
    from_above = spread[3]
    return jnp.stack(
        [
            from_above[0],
            from_high[1],
            from_below[0],
            from_above[1],
            from_below[1],
            from_above[2],
            from_low[1],
            from_below[2],
        ]
    )


def return_gx_first(ghost_force):
    ghost_len = ghost_force.shape[2]
    packed = jnp.stack(
        [
            jnp.stack([ghost_force[2], ghost_force[4], ghost_force[7]]),
            jnp.stack([ghost_force[0], ghost_force[3], ghost_force[5]]),
        ]
    ).reshape(2, -1)
    spread = padded(packed, (("yz", 0),), 1).reshape(4, 3, 3, ghost_len)
    from_below = spread[0]
    from_above = spread[3]
    packed = jnp.stack(
        [
            jnp.stack([from_below[2], ghost_force[6], from_above[2]]),
            jnp.stack([from_below[0], ghost_force[1], from_above[0]]),
        ]
    ).reshape(2, -1)
    spread = padded(packed, (("gx", 0),), 1).reshape(4, 3, 3, ghost_len)
    from_low = spread[0]
    from_high = spread[3]
    return jnp.stack(
        [
            from_low[0],
            from_low[1],
            from_low[2],
            from_below[1],
            from_above[1],
            from_high[0],
            from_high[1],
            from_high[2],
        ]
    )


def prepare_weights(radial_weight, species_embed, env_weight, latent_weight, readout, atom_n):
    latent = readout.shape[0]
    half = BF16(0.5)
    radial_t = radial_weight.T * half
    embed_t = jnp.concatenate([species_embed[1].T, species_embed[0].T], axis=1) * half
    radial_pad = BASIS_PAD - radial_weight.shape[0]
    readout_row = readout[None, :]
    zeros = jnp.zeros((BASIS_PAD - 1, latent), BF16)
    folded = (latent_weight[0].astype(F32) * (0.5 * readout_row.astype(F32))).astype(BF16)
    latent_t = latent_weight[0].T * half
    return (
        embed_t,
        jnp.pad(radial_t, ((0, 0), (0, radial_pad))),
        jnp.concatenate([latent_t[:, :latent], env_weight[0].T, readout_row, zeros], axis=0),
        latent_t[:, latent:],
        folded,
        jnp.concatenate([env_weight[0], readout[:, None], zeros.T], axis=1),
        jnp.broadcast_to(readout.astype(F32)[:, None], (latent, 128)),
        jnp.pad(radial_weight * half, ((0, radial_pad), (0, 0))),
        atom_n,
    )


def body(
    positions,
    velocities,
    forces_start,
    species,
    live_atoms,
    send_list,
    neighbours,
    neighbour_count,
    radial_weight,
    species_embed,
    env_weight,
    latent_weight,
    readout,
):
    atom_n = positions.shape[1]
    ghost_len = send_list.shape[1]
    species_float = species.astype(jnp.float32)
    inverse = inverse_mass(species)
    weights = prepare_weights(
        radial_weight, species_embed, env_weight, latent_weight, readout, atom_n
    )
    pairs = compact_pairs(live_atoms, neighbour_count, neighbours)
    send_pick = (
        send_list.reshape(-1)[:, None] == jnp.arange(atom_n, dtype=jnp.int32)[None, :]
    ).astype(jnp.float32)

    def evaluate(coords):
        sources = jnp.concatenate([coords, species_float[None]], axis=0)
        payload = pick_columns(sources, send_pick).reshape(4, 8, ghost_len).transpose(1, 0, 2)
        ghosts = forward_gx_first(payload)
        ext_pos = jnp.concatenate(
            [coords, ghosts[:, 0:3].transpose(1, 0, 2).reshape(3, -1)], axis=1
        )
        ext_species = jnp.concatenate([species_float, ghosts[:, 3].reshape(-1)])
        forces = pair_forces(pairs, ext_pos, ext_species.astype(jnp.int32)[None, :], weights)
        ghost_force = forces[:, atom_n:].reshape(3, 8, -1).transpose(1, 0, 2)
        returned = return_gx_first(ghost_force)
        back = jnp.dot(
            returned.transpose(1, 0, 2).reshape(3, -1),
            send_pick,
            precision=lax.Precision.HIGHEST,
            preferred_element_type=jnp.float32,
        )
        return forces[:, :atom_n] + back

    half = velocities + 0.5 * STEP * inverse * forces_start
    moved = positions + STEP * half
    forces_mid = evaluate(moved)
    velocities_mid = half + 0.5 * STEP * inverse * forces_mid
    half_two = velocities_mid + 0.5 * STEP * inverse * forces_mid
    positions_end = moved + STEP * half_two
    forces_end = evaluate(positions_end)
    velocities_end = half_two + 0.5 * STEP * inverse * forces_end
    return (positions_end, velocities_end, forces_end)


def solution(mesh):
    placed = (
        P(None, ("gx", "yz")),
        P(None, ("gx", "yz")),
        P(None, ("gx", "yz")),
        P(("gx", "yz")),
        P(("gx", "yz")),
        P(None, ("gx", "yz")),
        P(("gx", "yz"), None),
        P(("gx", "yz")),
        P(),
        P(),
        P(),
        P(),
        P(),
    )
    return jax.shard_map(
        body,
        mesh=mesh,
        in_specs=placed,
        out_specs=(P(None, ("gx", "yz")), P(None, ("gx", "yz")), P(None, ("gx", "yz"))),
        check_vma=False,
    )
```

```python
import functools

import jax
import jax.numpy as jnp
from jax import lax
from jax.experimental import pallas as pl
from jax.experimental.pallas import tpu as pltpu
from jax.sharding import PartitionSpec as P

SPECIES = 8
SLOTS = 128
RADIUS = 6.0
STEP = 0.25
COUPLING = 4.0
MASSES = (1.008, 12.011, 14.007, 15.999, 32.06, 22.99, 35.45, 30.97)

LANES = 1024
FORWARD_DIRECT = False
BACK_DIRECT = True
GATHERED = 2
DIRECTIONS = ((-1, -1), (-1, 0), (-1, 1), (0, -1), (0, 1), (1, -1), (1, 0), (1, 1))
BASIS_PAD = 16

F32 = jnp.float32
BF16 = jnp.bfloat16


def mm(left, right):
    return jnp.dot(left, right, preferred_element_type=F32)


def mm_nt(left, right):
    return lax.dot_general(left, right, (((1,), (1,)), ((), ())), preferred_element_type=F32)


def split3(values):
    high = values.astype(BF16)
    rest = values - high.astype(F32)
    mid = rest.astype(BF16)
    low = (rest - mid.astype(F32)).astype(BF16)
    return jnp.concatenate([high.astype(F32), mid.astype(F32), low.astype(F32)], axis=0).astype(BF16)


def one_hot(ids, rows):
    row_ids = lax.broadcasted_iota(jnp.int32, (rows, ids.shape[1]), 0)
    return jnp.where(row_ids == ids, 1.0, 0.0).astype(BF16)


SMEM = pl.BlockSpec(memory_space=pltpu.SMEM)
VMEM = pl.BlockSpec(memory_space=pltpu.VMEM)


def identity(size):
    row = lax.broadcasted_iota(jnp.int32, (size, size), 0)
    col = lax.broadcasted_iota(jnp.int32, (size, size), 1)
    return jnp.where(row == col, 1.0, 0.0).astype(BF16)


def padded_rows(values, rows):
    have, lanes = values.shape
    return jnp.concatenate([values, jnp.zeros((rows - have, lanes), values.dtype)], axis=0)


def sum_parts(parts):
    rows = parts.shape[0] // 3
    return parts[:rows] + parts[rows : 2 * rows] + parts[2 * rows :]


def by_direction(rows):
    return jnp.concatenate([rows[k : k + 1] for k in range(len(DIRECTIONS))], axis=1)


def put(out_refs, place_ref, blocks):
    ghost_n = blocks.shape[1] // len(DIRECTIONS)
    if len(out_refs) == 1:
        out_refs[0][...] = jnp.zeros_like(out_refs[0])
    for k in range(len(DIRECTIONS)):
        block = blocks[:, k * ghost_n : (k + 1) * ghost_n]
        if len(out_refs) == 1:
            out_refs[0][place_ref[k]] = block
        else:
            out_refs[k][...] = block


def take(in_refs, place_ref):
    if len(in_refs) == 1:
        got = [in_refs[0][place_ref[k]] for k in range(len(DIRECTIONS))]
    else:
        got = [ref[...] for ref in in_refs]
    return jnp.concatenate(got, axis=1)


def pick_ghosts(values, send_ref, atom_n):
    return sum_parts(mm(split3(values), one_hot(by_direction(send_ref[...]), atom_n)))


def start_kernel(
    place_ref, pos_ref, vel_ref, force_ref, species_ref, send_ref, moved_ref, half_ref, inv_ref, *out_refs
):
    species = species_ref[...]
    inverse = jnp.zeros(species.shape, F32)
    for spec_id, mass in enumerate(MASSES):
        inverse = jnp.where(species == spec_id, F32(1.0 / mass), inverse)
    half = vel_ref[...] + 0.5 * STEP * inverse * force_ref[...]
    moved = pos_ref[...] + STEP * half
    inv_ref[...] = inverse
    half_ref[...] = half
    moved_ref[...] = moved
    sources = padded_rows(jnp.concatenate([moved, species.astype(F32)], axis=0), 8)
    put(out_refs, place_ref, pick_ghosts(sources, send_ref, species.shape[1])[0:4])


def total_force(place_ref, own_ref, send_ref, in_refs):
    own = own_ref[...]
    back = padded_rows(take(in_refs, place_ref), 8)
    pick = one_hot(by_direction(send_ref[...]), own.shape[1])
    return own + sum_parts(mm_nt(split3(back), pick))[0:3]


def middle_kernel(
    back_ref, place_ref, own_ref, send_ref, half_ref, moved_ref, inv_ref, *refs, in_count
):
    in_refs, (half_two_ref, end_ref), out_refs = refs[:in_count], refs[in_count : in_count + 2], refs[in_count + 2 :]
    forces = total_force(back_ref, own_ref, send_ref, in_refs)
    kick = 0.5 * STEP * inv_ref[...] * forces
    half_two = half_ref[...] + kick + kick
    end = moved_ref[...] + STEP * half_two
    half_two_ref[...] = half_two
    end_ref[...] = end
    put(out_refs, place_ref, pick_ghosts(padded_rows(end, 8), send_ref, end.shape[1])[0:3])


def last_kernel(back_ref, own_ref, send_ref, half_two_ref, inv_ref, *refs):
    in_refs, (vel_ref, force_ref) = refs[:-2], refs[-2:]
    forces = total_force(back_ref, own_ref, send_ref, in_refs)
    force_ref[...] = forces
    vel_ref[...] = half_two_ref[...] + 0.5 * STEP * inv_ref[...] * forces


def prepare_kernel(
    live_ref,
    count_ref,
    slots_ref,
    radial_ref,
    embed_ref,
    env_t_ref,
    latent_ref,
    readout_ref,
    neigh_ref,
    centre_ref,
    total_ref,
    embed_t_ref,
    radial_t_ref,
    on_hidden_ref,
    on_inner_ref,
    on_bent_ref,
    on_weight_ref,
    readout_t_ref,
    radial_back_ref,
):
    features, latent = env_t_ref.shape
    slots_t = mm_nt(identity(slots_ref.shape[1]), slots_ref[...].astype(F32).astype(BF16)).astype(BF16)
    list_pairs(live_ref, count_ref, slots_t, neigh_ref, centre_ref, total_ref)

    eye = identity(latent)
    half = BF16(0.5)
    latent_w = latent_ref[...]
    readout = readout_ref[...]
    none = jnp.zeros((BASIS_PAD - 8, latent), BF16)
    readout16 = padded_rows(readout.astype(F32), BASIS_PAD).astype(BF16)
    radial16 = jnp.concatenate([radial_ref[...] * half, none], axis=0)
    latent_t = mm_nt(eye, latent_w * half).astype(BF16)
    on_hidden_ref[...] = jnp.concatenate([latent_t[:, :latent], env_t_ref[...], readout16], axis=0)
    on_inner_ref[...] = latent_t[:, latent:]
    on_bent_ref[...] = (latent_w.astype(F32) * (0.5 * readout.astype(F32))).astype(BF16)
    on_weight_ref[...] = mm_nt(eye, jnp.concatenate([env_t_ref[...], readout16], axis=0)).astype(BF16)
    readout_t_ref[...] = mm_nt(eye, jnp.broadcast_to(readout.astype(F32), (128, latent)).astype(BF16))
    radial_back_ref[...] = radial16
    radial_t_ref[...] = mm_nt(eye, radial16).astype(BF16)
    embed_t_ref[...] = mm_nt(eye, jnp.concatenate([embed_ref[1], embed_ref[0]], axis=0) * half).astype(BF16)


def list_pairs(live_ref, count_ref, slots_t, neigh_ref, centre_ref, total_ref):
    atom_n = count_ref.shape[1]
    slot_n = slots_t.shape[0]
    blocks, lanes = neigh_ref.shape
    atom_row = lax.broadcasted_iota(jnp.int32, (1, atom_n), 1)
    used = jnp.where(atom_row < live_ref[0], count_ref[...], 0).astype(F32)
    row_i = lax.broadcasted_iota(jnp.int32, (atom_n, atom_n), 0)
    col_i = lax.broadcasted_iota(jnp.int32, (atom_n, atom_n), 1)
    end = jnp.sum(jnp.where(col_i <= row_i, used, 0.0), axis=1, keepdims=True)
    own = jnp.sum(jnp.where(col_i == row_i, used, 0.0), axis=1, keepdims=True)
    total = jnp.sum(used)
    total_ref[0] = total.astype(jnp.int32)
    lane = lax.broadcasted_iota(jnp.int32, (1, lanes), 1)

    def one_block(block, carry):
        place = (lane + block * lanes).astype(F32)
        past = end <= place
        centre = jnp.sum(jnp.where(past, 1.0, 0.0), axis=0, keepdims=True)
        start = jnp.sum(jnp.where(past, own, 0.0), axis=0, keepdims=True)
        slot = (place - start).astype(jnp.int32)
        centre_id = centre.astype(jnp.int32)
        rows = mm(slots_t, one_hot(centre_id, atom_n))
        slot_ids = lax.broadcasted_iota(jnp.int32, (slot_n, lanes), 0)
        neigh = jnp.sum(jnp.where(slot_ids == slot, rows, 0.0), axis=0, keepdims=True)
        valid = place < total
        neigh_ref[pl.ds(block, 1), :] = jnp.where(valid, neigh.astype(jnp.int32), -1)
        centre_ref[pl.ds(block, 1), :] = jnp.where(valid, centre_id, -1)
        return carry

    lax.fori_loop(0, blocks, one_block, 0)


def prepare(live_atoms, neighbour_count, neighbours, radial_weight, species_embed, env_weight, latent_weight, readout):
    atom_n, slot_n = neighbours.shape
    latent, features = env_weight.shape[1:]
    blocks = atom_n * slot_n // LANES
    shapes = (
        ((blocks, LANES), jnp.int32),
        ((blocks, LANES), jnp.int32),
        ((1,), jnp.int32),
        ((latent, 16), BF16),
        ((latent, BASIS_PAD), BF16),
        ((latent + features + BASIS_PAD, latent), BF16),
        ((latent, features), BF16),
        ((latent + features, latent), BF16),
        ((latent, features + BASIS_PAD), BF16),
        ((latent, 128), F32),
        ((BASIS_PAD, latent), BF16),
    )
    out = pl.pallas_call(
        prepare_kernel,
        out_shape=[jax.ShapeDtypeStruct(*shape) for shape in shapes],
        in_specs=[SMEM] + [VMEM] * 7,
        out_specs=[VMEM, VMEM, SMEM] + [VMEM] * 8,
        compiler_params=pltpu.CompilerParams(vmem_limit_bytes=24 * 2**20),
        cost_estimate=pl.CostEstimate(flops=2 * 10**9, bytes_accessed=4 * 2**20, transcendentals=0),
        name="prepare",
    )(
        live_atoms,
        neighbour_count.reshape(1, atom_n),
        neighbours,
        radial_weight,
        species_embed,
        env_weight[0].T,
        latent_weight[0],
        readout[None, :],
    )
    return out[:3], out[3:]


def silu_pair(half_in):
    bent = jnp.tanh(half_in)
    part = half_in * bent
    return half_in + part, (1.0 + bent) * (1.0 + (half_in - part))


def force_kernel(
    place_ref,
    back_ref,
    total_ref,
    neigh_ref,
    centre_ref,
    own_ref,
    own_kind_ref,
    embed_ref,
    radial_ref,
    on_hidden_ref,
    on_inner_ref,
    on_bent_ref,
    on_weight_ref,
    readout_ref,
    radial_back_ref,
    *refs,
    in_count,
    first_call,
):
    in_refs, refs = refs[:in_count], refs[in_count:]
    if first_call:
        kind_out_ref, own_out_ref = refs[:2]
        out_refs = refs[2:-12]
    else:
        ghost_kind_ref, own_out_ref = refs[:2]
        out_refs = refs[2:-12]
    hot_s, use_s, u_s, inside_s, slope_s, raw_s, part_s, ain_s, energy_s, c_s, dc_s, f_s = refs[-12:]
    blocks, lanes = neigh_ref.shape
    atom_n = own_ref.shape[1]
    ghosts = take(in_refs, place_ref)
    ext_n = atom_n + ghosts.shape[1]
    if first_call:
        ghost_kind = ghosts[3:4].astype(jnp.int32)
        kind_out_ref[...] = ghost_kind
    else:
        ghost_kind = ghost_kind_ref[...]
    kind = jnp.concatenate([own_kind_ref[...], ghost_kind], axis=1)
    pos = jnp.concatenate([own_ref[...], ghosts[0:3]], axis=1)
    basis_n = SPECIES
    latent, features = on_inner_ref.shape
    count = (total_ref[0] + lanes - 1) // lanes
    scale = COUPLING * SLOTS ** (-0.5)

    pos8 = padded_rows(pos, 8) * (1.0 / RADIUS)
    pos_parts = split3(jnp.concatenate([pos8, -pos8[:, :atom_n]], axis=1))
    row8 = lax.broadcasted_iota(jnp.int32, (SPECIES, ext_n), 0)
    kinds = jnp.where(row8 == kind, 1.0, 0.0)
    none = jnp.zeros((SPECIES, ext_n), F32)
    neigh_embed = mm(embed_ref[...], jnp.concatenate([kinds, none], axis=0).astype(BF16))
    own_embed = mm(
        embed_ref[...],
        jnp.concatenate([none, kinds], axis=0)[:, :atom_n].astype(BF16),
    )
    weight_in = jnp.concatenate(
        [neigh_embed, own_embed, radial_ref[...].astype(F32)], axis=1
    ).astype(BF16)

    mid_row = lax.broadcasted_iota(jnp.int32, (BASIS_PAD, lanes), 0).astype(F32)
    mids = (mid_row + 0.5) / basis_n
    sharp = 2.0 * basis_n * basis_n

    c_s[...] = jnp.zeros_like(c_s)
    dc_s[...] = jnp.zeros_like(dc_s)
    f_s[...] = jnp.zeros_like(f_s)

    def gather(block):
        centre = centre_ref[pl.ds(block, 1), :]
        hot_j = one_hot(neigh_ref[pl.ds(block, 1), :], ext_n)
        hot_c = one_hot(centre, atom_n)
        hot = jnp.concatenate([hot_j, hot_c], axis=0)
        parts = mm(pos_parts, hot)
        vec = parts[0:8] + parts[8:16] + parts[16:24]
        square = jnp.sum(vec * vec, axis=0, keepdims=True)
        apart = square - mids
        basis = jnp.exp(-sharp * apart * apart)
        u_s[block] = vec
        inside_s[block] = jnp.where(centre >= 0, jnp.maximum(1.0 - square, 0.0), 0.0)
        use_s[block] = jnp.concatenate(
            [hot_c * vec[k : k + 1].astype(BF16) for k in range(3)], axis=0
        )
        hot_s[block] = jnp.concatenate([hot, basis.astype(BF16)], axis=0)

    def gather_some(step, carry):
        for more in range(GATHERED):
            gather(step * GATHERED + more)
        return carry

    lax.fori_loop(0, (count + GATHERED - 1) // GATHERED, gather_some, 0)

    def first(block, carry):
        inside = inside_s[block]
        use = use_s[block]
        pre = mm(weight_in, hot_s[block])
        hidden, slope = silu_pair(pre)
        slope_s[block] = slope.astype(BF16)
        taken = mm(on_hidden_ref[...], hidden.astype(BF16))
        part_s[block] = taken[:latent]
        raw = taken[latent : latent + features]
        raw_s[block] = raw
        energy_s[block] = taken[latent + features : latent + features + 8]
        c_s[...] += mm_nt((raw * (inside * inside)).astype(BF16), use)
        return carry

    lax.fori_loop(0, count, first, 0)
    c_all = c_s[...] * scale
    c_b = c_all.astype(BF16)

    def second(block, carry):
        inside = inside_s[block]
        use = use_s[block]
        env = inside * inside
        weight = raw_s[block] * env
        inner = weight * mm(c_b, use)
        later = part_s[block] + mm(on_inner_ref[...], inner.astype(BF16))
        gain, bent = silu_pair(later)
        readout = jnp.concatenate([readout_ref[...]] * (lanes // 128), axis=1)
        energy_s[block] += jnp.sum(gain * readout, axis=0, keepdims=True)
        taken = mm(on_bent_ref[...], bent.astype(BF16))
        part_s[block] = taken[:latent]
        a_in = taken[latent:] * env
        ain_s[block] = a_in
        dc_s[...] += mm_nt((a_in * weight).astype(BF16), use)
        return carry

    lax.fori_loop(0, count, second, 0)
    c_dc = jnp.concatenate([c_all, dc_s[...] * scale], axis=0).astype(BF16)
    both = jnp.concatenate([c_all.T, dc_s[...].T * scale], axis=1).astype(BF16)

    def third(block, carry):
        vec = u_s[block]
        inside = inside_s[block]
        square = jnp.sum(vec * vec, axis=0, keepdims=True)
        apart = square - mids
        basis = jnp.exp(-sharp * apart * apart)
        use = use_s[block]
        hot = hot_s[block, : ext_n + atom_n]
        env = inside * inside
        raw = raw_s[block]
        weight = raw * env
        a_in = ain_s[block]
        along = mm(c_dc, use)
        d_weight = a_in * along[:features] + along[features:]
        d_env = jnp.sum(d_weight * raw, axis=0, keepdims=True) + energy_s[block][0:1]
        ones = jnp.ones((BASIS_PAD, lanes), BF16)
        d_hidden = part_s[block] + mm(
            on_weight_ref[...], jnp.concatenate([d_weight.astype(BF16), ones], axis=0)
        )
        d_pre = (d_hidden * slope_s[block].astype(F32)).astype(BF16)
        d_basis = mm(radial_back_ref[...], d_pre)
        d_square = env * jnp.sum(d_basis * basis * apart, axis=0, keepdims=True) * (-2.0 * sharp)
        d_square = d_square - 2.0 * inside * d_env
        d_all = mm(both, jnp.concatenate([a_in * weight, weight], axis=0).astype(BF16))
        hot_c = hot[ext_n:].astype(F32)
        picked = [
            jnp.sum(d_all[k * atom_n : (k + 1) * atom_n] * hot_c, axis=0, keepdims=True)
            for k in range(3)
        ]
        d_vec = jnp.concatenate(picked + [jnp.zeros((5, lanes), F32)], axis=0)
        d_vec = (d_vec + 2.0 * d_square * vec) * (1.0 / RADIUS)
        f_s[...] += mm_nt(split3(d_vec), hot)
        return carry

    lax.fori_loop(0, count, third, 0)
    summed = f_s[0:8] + f_s[8:16] + f_s[16:24]
    on_centre = summed[0:3, ext_n:]
    on_neigh = summed[0:3, :ext_n]
    own_out_ref[...] = on_centre - on_neigh[:, :atom_n]
    put(out_refs, back_ref, -on_neigh[:, atom_n:])


def exchange_shapes(devices, rows, ghost_n, direct):
    if direct:
        return [jax.ShapeDtypeStruct((rows, ghost_n), F32)] * len(DIRECTIONS)
    return [jax.ShapeDtypeStruct((devices, rows, ghost_n), F32)]


def pair_forces(places, pairs, own_pos, own_kind, ghost_kind, incoming, weights, devices, direct):
    neigh, centre, total = pairs
    blocks, lanes = neigh.shape
    latent, features = weights[3].shape
    atom_n = own_pos.shape[1]
    ghost_n = incoming[0].shape[-1]
    ghost_all = ghost_n * len(DIRECTIONS)
    ext_n = atom_n + ghost_all
    first_call = ghost_kind is None
    operands = [*places, total, neigh, centre, own_pos, own_kind, *weights, *incoming]
    out_shape = [jax.ShapeDtypeStruct((3, atom_n), F32)] + exchange_shapes(devices, 3, ghost_n, direct)
    if first_call:
        out_shape = [jax.ShapeDtypeStruct((1, ghost_all), jnp.int32)] + out_shape
    else:
        operands.append(ghost_kind)
    pair_rows = blocks * lanes
    return pl.pallas_call(
        functools.partial(force_kernel, in_count=len(incoming), first_call=first_call),
        out_shape=out_shape,
        in_specs=[SMEM] * 3 + [VMEM] * (len(operands) - 3),
        out_specs=[VMEM] * len(out_shape),
        scratch_shapes=[
            pltpu.VMEM((blocks, ext_n + atom_n + BASIS_PAD, lanes), BF16),
            pltpu.VMEM((blocks, 3 * atom_n, lanes), BF16),
            pltpu.VMEM((blocks, 8, lanes), F32),
            pltpu.VMEM((blocks, 1, lanes), F32),
            pltpu.VMEM((blocks, latent, lanes), BF16),
            pltpu.VMEM((blocks, features, lanes), F32),
            pltpu.VMEM((blocks, latent, lanes), F32),
            pltpu.VMEM((blocks, features, lanes), F32),
            pltpu.VMEM((blocks, 8, lanes), F32),
            pltpu.VMEM((features, 3 * atom_n), F32),
            pltpu.VMEM((features, 3 * atom_n), F32),
            pltpu.VMEM((24, ext_n + atom_n), F32),
        ],
        compiler_params=pltpu.CompilerParams(vmem_limit_bytes=48 * 2**20),
        cost_estimate=pl.CostEstimate(
            flops=pair_rows * latent * 2700, bytes_accessed=4 * 2**20, transcendentals=0
        ),
        name="pair_forces",
    )(*operands)


def small_call(kernel, name, smem_n, operands, out_shape):
    return pl.pallas_call(
        kernel,
        out_shape=out_shape,
        in_specs=[SMEM] * smem_n + [VMEM] * (len(operands) - smem_n),
        out_specs=[VMEM] * len(out_shape),
        compiler_params=pltpu.CompilerParams(vmem_limit_bytes=16 * 2**20),
        name=name,
    )(*operands)


def neighbour_devices(step):
    gx_n, yz_n = lax.axis_size("gx"), lax.axis_size("yz")
    gx, yz = lax.axis_index("gx"), lax.axis_index("yz")
    step_gx = jnp.array([a for a, _ in DIRECTIONS], jnp.int32) * step
    step_yz = jnp.array([b for _, b in DIRECTIONS], jnp.int32) * step
    return ((gx + step_gx + gx_n) % gx_n) * yz_n + (yz + step_yz + yz_n) % yz_n


def exchange(blocks, step):
    axes = ("gx", "yz")
    if len(blocks) == 1:
        return [lax.all_to_all(blocks[0], axes, 0, 0, tiled=True)]
    gx_n, yz_n = lax.axis_size("gx"), lax.axis_size("yz")
    got = []
    for (a, b), block in zip(DIRECTIONS, blocks):
        pairs = [
            (p * yz_n + q, (p + step * a) % gx_n * yz_n + (q + step * b) % yz_n)
            for p in range(gx_n)
            for q in range(yz_n)
        ]
        got.append(lax.ppermute(block, axes, pairs))
    return got


def body(
    positions,
    velocities,
    forces_start,
    species,
    live_atoms,
    send_list,
    neighbours,
    neighbour_count,
    radial_weight,
    species_embed,
    env_weight,
    latent_weight,
    readout,
):
    atom_n = positions.shape[1]
    ghost_n = send_list.shape[1]
    devices = lax.axis_size("gx") * lax.axis_size("yz")
    ahead, behind = neighbour_devices(1), neighbour_devices(-1)
    kinds = species.reshape(1, atom_n)
    atoms = jax.ShapeDtypeStruct((3, atom_n), F32)
    row = jax.ShapeDtypeStruct((1, atom_n), F32)

    moved, half, inverse, *sent = small_call(
        start_kernel,
        "start",
        1,
        [ahead, positions, velocities, forces_start, kinds, send_list],
        [atoms, atoms, row] + exchange_shapes(devices, 4, ghost_n, FORWARD_DIRECT),
    )
    got = exchange(sent, 1)
    pairs, weights = prepare(
        live_atoms, neighbour_count, neighbours, radial_weight, species_embed, env_weight, latent_weight, readout
    )
    places = (behind, behind)
    ghost_kind, own, *sent = pair_forces(
        places, pairs, moved, kinds, None, got, weights, devices, BACK_DIRECT
    )
    got = exchange(sent, -1)
    half_two, positions_end, *sent = small_call(
        functools.partial(middle_kernel, in_count=len(got)),
        "middle",
        2,
        [ahead, ahead, own, send_list, half, moved, inverse, *got],
        [atoms, atoms] + exchange_shapes(devices, 3, ghost_n, FORWARD_DIRECT),
    )
    got = exchange(sent, 1)
    own, *sent = pair_forces(
        places, pairs, positions_end, kinds, ghost_kind, got, weights, devices, BACK_DIRECT
    )
    got = exchange(sent, -1)
    velocities_end, forces_end = small_call(
        last_kernel, "last", 1, [ahead, own, send_list, half_two, inverse, *got], [atoms, atoms]
    )
    return (positions_end, velocities_end, forces_end)


def solution(mesh):
    placed = (
        P(None, ("gx", "yz")),
        P(None, ("gx", "yz")),
        P(None, ("gx", "yz")),
        P(("gx", "yz")),
        P(("gx", "yz")),
        P(None, ("gx", "yz")),
        P(("gx", "yz"), None),
        P(("gx", "yz")),
        P(),
        P(),
        P(),
        P(),
        P(),
    )
    return jax.shard_map(
        body,
        mesh=mesh,
        in_specs=placed,
        out_specs=(P(None, ("gx", "yz")), P(None, ("gx", "yz")), P(None, ("gx", "yz"))),
        check_vma=False,
    )
```

```python
import functools

import jax
import jax.numpy as jnp
from jax import lax
from jax.experimental import pallas as pl
from jax.experimental.pallas import tpu as pltpu
from jax.sharding import PartitionSpec as P

SPECIES = 8
SLOTS = 128
RADIUS = 6.0
STEP = 0.25
COUPLING = 4.0
MASSES = (1.008, 12.011, 14.007, 15.999, 32.06, 22.99, 35.45, 30.97)

LANES = 1664
DIRECTIONS = ((-1, -1), (-1, 0), (-1, 1), (0, -1), (0, 1), (1, -1), (1, 0), (1, 1))
BASIS_PAD = 16

F32 = jnp.float32
BF16 = jnp.bfloat16


def mm(left, right):
    return jnp.dot(left, right, preferred_element_type=F32)


def mm_nt(left, right):
    return lax.dot_general(left, right, (((1,), (1,)), ((), ())), preferred_element_type=F32)


def split3(values):
    high = values.astype(BF16)
    rest = values - high.astype(F32)
    mid = rest.astype(BF16)
    low = (rest - mid.astype(F32)).astype(BF16)
    return jnp.concatenate([high.astype(F32), mid.astype(F32), low.astype(F32)], axis=0).astype(BF16)


def one_hot(ids, rows):
    row_ids = lax.broadcasted_iota(jnp.int32, (rows, ids.shape[1]), 0)
    return jnp.where(row_ids == ids, 1.0, 0.0).astype(BF16)


SMEM = pl.BlockSpec(memory_space=pltpu.SMEM)
VMEM = pl.BlockSpec(memory_space=pltpu.VMEM)


def identity(size):
    row = lax.broadcasted_iota(jnp.int32, (size, size), 0)
    col = lax.broadcasted_iota(jnp.int32, (size, size), 1)
    return jnp.where(row == col, 1.0, 0.0).astype(BF16)


def padded_rows(values, rows):
    have, lanes = values.shape
    return jnp.concatenate([values, jnp.zeros((rows - have, lanes), values.dtype)], axis=0)


def sum_parts(parts):
    rows = parts.shape[0] // 3
    return parts[:rows] + parts[rows : 2 * rows] + parts[2 * rows :]


def by_direction(rows):
    return jnp.concatenate([rows[k : k + 1] for k in range(len(DIRECTIONS))], axis=1)


def put(out_ref, place_ref, blocks):
    ghost_n = blocks.shape[1] // len(DIRECTIONS)
    out_ref[...] = jnp.zeros_like(out_ref)
    for k in range(len(DIRECTIONS)):
        out_ref[place_ref[k]] = blocks[:, k * ghost_n : (k + 1) * ghost_n]


def take(in_ref, place_ref):
    return jnp.concatenate([in_ref[place_ref[k]] for k in range(len(DIRECTIONS))], axis=1)


def pick_ghosts(values, send_ref, atom_n):
    return sum_parts(mm(split3(values), one_hot(by_direction(send_ref[...]), atom_n)))


def start_kernel(
    place_ref, pos_ref, vel_ref, force_ref, species_ref, send_ref, moved_ref, half_ref, inv_ref, out_ref
):
    species = species_ref[...]
    inverse = jnp.zeros(species.shape, F32)
    for spec_id, mass in enumerate(MASSES):
        inverse = jnp.where(species == spec_id, F32(1.0 / mass), inverse)
    half = vel_ref[...] + 0.5 * STEP * inverse * force_ref[...]
    moved = pos_ref[...] + STEP * half
    inv_ref[...] = inverse
    half_ref[...] = half
    moved_ref[...] = moved
    sources = padded_rows(jnp.concatenate([moved, species.astype(F32)], axis=0), 8)
    put(out_ref, place_ref, pick_ghosts(sources, send_ref, species.shape[1])[0:4])


def total_force(place_ref, own_ref, send_ref, in_ref):
    own = own_ref[...]
    back = padded_rows(take(in_ref, place_ref), 8)
    pick = one_hot(by_direction(send_ref[...]), own.shape[1])
    return own + sum_parts(mm_nt(split3(back), pick))[0:3]


def middle_kernel(
    back_ref, place_ref, own_ref, send_ref, half_ref, moved_ref, inv_ref, in_ref, half_two_ref, end_ref, out_ref
):
    forces = total_force(back_ref, own_ref, send_ref, in_ref)
    kick = 0.5 * STEP * inv_ref[...] * forces
    half_two = half_ref[...] + kick + kick
    end = moved_ref[...] + STEP * half_two
    half_two_ref[...] = half_two
    end_ref[...] = end
    put(out_ref, place_ref, pick_ghosts(padded_rows(end, 8), send_ref, end.shape[1])[0:3])


def last_kernel(back_ref, own_ref, send_ref, half_two_ref, inv_ref, in_ref, vel_ref, force_ref):
    forces = total_force(back_ref, own_ref, send_ref, in_ref)
    force_ref[...] = forces
    vel_ref[...] = half_two_ref[...] + 0.5 * STEP * inv_ref[...] * forces


def prepare_kernel(
    live_ref,
    count_ref,
    slots_ref,
    radial_ref,
    embed_ref,
    env_t_ref,
    latent_ref,
    readout_ref,
    neigh_ref,
    centre_ref,
    total_ref,
    embed_t_ref,
    radial_t_ref,
    on_hidden_ref,
    on_inner_ref,
    on_bent_ref,
    on_weight_ref,
    readout_t_ref,
    radial_back_ref,
):
    features, latent = env_t_ref.shape
    slots_t = mm_nt(identity(slots_ref.shape[1]), slots_ref[...].astype(F32).astype(BF16)).astype(BF16)
    list_pairs(live_ref, count_ref, slots_t, neigh_ref, centre_ref, total_ref)

    eye = identity(latent)
    half = BF16(0.5)
    latent_w = latent_ref[...]
    readout = readout_ref[...]
    none = jnp.zeros((BASIS_PAD - 8, latent), BF16)
    readout16 = padded_rows(readout.astype(F32), BASIS_PAD).astype(BF16)
    radial16 = jnp.concatenate([radial_ref[...] * half, none], axis=0)
    latent_t = mm_nt(eye, latent_w * half).astype(BF16)
    on_hidden_ref[...] = jnp.concatenate([latent_t[:, :latent], env_t_ref[...], readout16], axis=0)
    on_inner_ref[...] = latent_t[:, latent:]
    on_bent_ref[...] = (latent_w.astype(F32) * (0.5 * readout.astype(F32))).astype(BF16)
    on_weight_ref[...] = mm_nt(eye, jnp.concatenate([env_t_ref[...], readout16], axis=0)).astype(BF16)
    readout_t_ref[...] = mm_nt(eye, jnp.broadcast_to(readout.astype(F32), (128, latent)).astype(BF16))
    radial_back_ref[...] = radial16
    radial_t_ref[...] = mm_nt(eye, radial16).astype(BF16)
    embed_t_ref[...] = mm_nt(eye, jnp.concatenate([embed_ref[1], embed_ref[0]], axis=0) * half).astype(BF16)


def list_pairs(live_ref, count_ref, slots_t, neigh_ref, centre_ref, total_ref):
    atom_n = count_ref.shape[1]
    slot_n = slots_t.shape[0]
    blocks, lanes = neigh_ref.shape
    atom_row = lax.broadcasted_iota(jnp.int32, (1, atom_n), 1)
    used = jnp.where(atom_row < live_ref[0], count_ref[...], 0).astype(F32)
    row_i = lax.broadcasted_iota(jnp.int32, (atom_n, atom_n), 0)
    col_i = lax.broadcasted_iota(jnp.int32, (atom_n, atom_n), 1)
    end = jnp.sum(jnp.where(col_i <= row_i, used, 0.0), axis=1, keepdims=True)
    own = jnp.sum(jnp.where(col_i == row_i, used, 0.0), axis=1, keepdims=True)
    total = jnp.sum(used)
    total_ref[0] = total.astype(jnp.int32)
    lane = lax.broadcasted_iota(jnp.int32, (1, lanes), 1)

    def one_block(block, carry):
        place = (lane + block * lanes).astype(F32)
        past = end <= place
        centre = jnp.sum(jnp.where(past, 1.0, 0.0), axis=0, keepdims=True)
        start = jnp.sum(jnp.where(past, own, 0.0), axis=0, keepdims=True)
        slot = (place - start).astype(jnp.int32)
        centre_id = centre.astype(jnp.int32)
        rows = mm(slots_t, one_hot(centre_id, atom_n))
        slot_ids = lax.broadcasted_iota(jnp.int32, (slot_n, lanes), 0)
        neigh = jnp.sum(jnp.where(slot_ids == slot, rows, 0.0), axis=0, keepdims=True)
        valid = place < total
        neigh_ref[pl.ds(block, 1), :] = jnp.where(valid, neigh.astype(jnp.int32), -1)
        centre_ref[pl.ds(block, 1), :] = jnp.where(valid, centre_id, -1)
        return carry

    lax.fori_loop(0, blocks, one_block, 0)


def prepare(live_atoms, neighbour_count, neighbours, radial_weight, species_embed, env_weight, latent_weight, readout):
    atom_n, slot_n = neighbours.shape
    latent, features = env_weight.shape[1:]
    blocks = pl.cdiv(atom_n * slot_n, LANES)
    shapes = (
        ((blocks, LANES), jnp.int32),
        ((blocks, LANES), jnp.int32),
        ((1,), jnp.int32),
        ((latent, 16), BF16),
        ((latent, BASIS_PAD), BF16),
        ((latent + features + BASIS_PAD, latent), BF16),
        ((latent, features), BF16),
        ((latent + features, latent), BF16),
        ((latent, features + BASIS_PAD), BF16),
        ((latent, 128), F32),
        ((BASIS_PAD, latent), BF16),
    )
    out = pl.pallas_call(
        prepare_kernel,
        out_shape=[jax.ShapeDtypeStruct(*shape) for shape in shapes],
        in_specs=[SMEM] + [VMEM] * 7,
        out_specs=[VMEM, VMEM, SMEM] + [VMEM] * 8,
        compiler_params=pltpu.CompilerParams(vmem_limit_bytes=24 * 2**20),
        cost_estimate=pl.CostEstimate(flops=2 * 10**9, bytes_accessed=4 * 2**20, transcendentals=0),
        name="prepare",
    )(
        live_atoms,
        neighbour_count.reshape(1, atom_n),
        neighbours,
        radial_weight,
        species_embed,
        env_weight[0].T,
        latent_weight[0],
        readout[None, :],
    )
    return out[:3], out[3:]


def silu_pair(half_in):
    bent = jnp.tanh(half_in)
    part = half_in * bent
    return half_in + part, (1.0 + bent) * (1.0 + (half_in - part))


def force_kernel(
    place_ref,
    back_ref,
    total_ref,
    neigh_ref,
    centre_ref,
    own_ref,
    own_kind_ref,
    embed_ref,
    radial_ref,
    on_hidden_ref,
    on_inner_ref,
    on_bent_ref,
    on_weight_ref,
    readout_ref,
    radial_back_ref,
    in_ref,
    *refs,
    first_call,
):
    kind_ref, own_out_ref, out_ref, *scratch = refs
    hot_s, use_s, u_s, slope_s, raw_s, part_s, ain_s, energy_s, c_s, dc_s, f_s = scratch
    blocks, lanes = neigh_ref.shape
    atom_n = own_ref.shape[1]
    ghosts = take(in_ref, place_ref)
    ext_n = atom_n + ghosts.shape[1]
    if first_call:
        ghost_kind = ghosts[3:4].astype(jnp.int32)
        kind_ref[...] = ghost_kind
    else:
        ghost_kind = kind_ref[...]
    kind = jnp.concatenate([own_kind_ref[...], ghost_kind], axis=1)
    pos = jnp.concatenate([own_ref[...], ghosts[0:3]], axis=1)
    basis_n = SPECIES
    latent, features = on_inner_ref.shape
    count = (total_ref[0] + lanes - 1) // lanes
    scale = COUPLING * SLOTS ** (-0.5)

    pos8 = padded_rows(pos, 8) * (1.0 / RADIUS)
    pos_parts = split3(jnp.concatenate([pos8, -pos8[:, :atom_n]], axis=1))
    row8 = lax.broadcasted_iota(jnp.int32, (SPECIES, ext_n), 0)
    kinds = jnp.where(row8 == kind, 1.0, 0.0)
    none = jnp.zeros((SPECIES, ext_n), F32)
    neigh_embed = mm(embed_ref[...], jnp.concatenate([kinds, none], axis=0).astype(BF16))
    own_embed = mm(
        embed_ref[...],
        jnp.concatenate([none, kinds], axis=0)[:, :atom_n].astype(BF16),
    )
    weight_in = jnp.concatenate(
        [neigh_embed, own_embed, radial_ref[...].astype(F32)], axis=1
    ).astype(BF16)

    mid_row = lax.broadcasted_iota(jnp.int32, (BASIS_PAD, lanes), 0).astype(F32)
    mids = (mid_row + 0.5) / basis_n
    sharp = 2.0 * basis_n * basis_n

    c_s[...] = jnp.zeros_like(c_s)
    dc_s[...] = jnp.zeros_like(dc_s)
    f_s[...] = jnp.zeros_like(f_s)

    def geometry(block):
        vec = u_s[block]
        square = jnp.sum(vec * vec, axis=0, keepdims=True)
        inside = jnp.maximum(1.0 - square, 0.0)
        inside = jnp.where(centre_ref[pl.ds(block, 1), :] >= 0, inside, 0.0)
        apart = square - mids
        return vec, inside, apart, jnp.exp(-sharp * apart * apart)

    def first(block, carry):
        hot_j = one_hot(neigh_ref[pl.ds(block, 1), :], ext_n)
        hot_c = one_hot(centre_ref[pl.ds(block, 1), :], atom_n)
        hot = jnp.concatenate([hot_j, hot_c], axis=0)
        hot_s[block] = hot
        u_s[block] = sum_parts(mm(pos_parts, hot))
        vec, inside, _, basis = geometry(block)
        use = jnp.concatenate([hot_c * vec[k : k + 1].astype(BF16) for k in range(3)], axis=0)
        use_s[block] = use
        pre = mm(weight_in, jnp.concatenate([hot, basis.astype(BF16)], axis=0))
        hidden, slope = silu_pair(pre)
        slope_s[block] = slope.astype(BF16)
        taken = mm(on_hidden_ref[...], hidden.astype(BF16))
        part_s[block] = taken[:latent]
        raw = taken[latent : latent + features]
        raw_s[block] = raw
        energy_s[block] = taken[latent + features : latent + features + 8]
        c_s[...] += mm_nt((raw * (inside * inside)).astype(BF16), use)
        return carry

    lax.fori_loop(0, count, first, 0)
    c_all = c_s[...] * scale
    c_b = c_all.astype(BF16)

    def second(block, carry):
        _, inside, _, _ = geometry(block)
        use = use_s[block]
        env = inside * inside
        weight = raw_s[block] * env
        inner = weight * mm(c_b, use)
        later = part_s[block] + mm(on_inner_ref[...], inner.astype(BF16))
        gain, bent = silu_pair(later)
        readout = jnp.concatenate([readout_ref[...]] * (lanes // 128), axis=1)
        energy_s[block] += jnp.sum(gain * readout, axis=0, keepdims=True)
        taken = mm(on_bent_ref[...], bent.astype(BF16))
        part_s[block] = taken[:latent]
        a_in = taken[latent:] * env
        ain_s[block] = a_in
        dc_s[...] += mm_nt((a_in * weight).astype(BF16), use)
        return carry

    lax.fori_loop(0, count, second, 0)
    c_dc = jnp.concatenate([c_all, dc_s[...] * scale], axis=0).astype(BF16)
    both = jnp.concatenate([c_all.T, dc_s[...].T * scale], axis=1).astype(BF16)

    def third(block, carry):
        vec, inside, apart, basis = geometry(block)
        use = use_s[block]
        hot = hot_s[block]
        env = inside * inside
        raw = raw_s[block]
        weight = raw * env
        a_in = ain_s[block]
        along = mm(c_dc, use)
        d_weight = a_in * along[:features] + along[features:]
        d_env = jnp.sum(d_weight * raw, axis=0, keepdims=True) + energy_s[block][0:1]
        ones = jnp.ones((BASIS_PAD, lanes), BF16)
        d_hidden = part_s[block] + mm(
            on_weight_ref[...], jnp.concatenate([d_weight.astype(BF16), ones], axis=0)
        )
        d_pre = (d_hidden * slope_s[block].astype(F32)).astype(BF16)
        d_basis = mm(radial_back_ref[...], d_pre)
        d_square = env * jnp.sum(d_basis * basis * apart, axis=0, keepdims=True) * (-2.0 * sharp)
        d_square = d_square - 2.0 * inside * d_env
        d_all = mm(both, jnp.concatenate([a_in * weight, weight], axis=0).astype(BF16))
        hot_c = hot[ext_n:].astype(F32)
        picked = [
            jnp.sum(d_all[k * atom_n : (k + 1) * atom_n] * hot_c, axis=0, keepdims=True)
            for k in range(3)
        ]
        d_vec = jnp.concatenate(picked + [jnp.zeros((5, lanes), F32)], axis=0)
        d_vec = (d_vec + 2.0 * d_square * vec) * (1.0 / RADIUS)
        f_s[...] += mm_nt(split3(d_vec), hot)
        return carry

    lax.fori_loop(0, count, third, 0)
    summed = f_s[0:8] + f_s[8:16] + f_s[16:24]
    on_centre = summed[0:3, ext_n:]
    on_neigh = summed[0:3, :ext_n]
    own_out_ref[...] = on_centre - on_neigh[:, :atom_n]
    put(out_ref, back_ref, -on_neigh[:, atom_n:])


def exchange_shape(devices, rows, ghost_n):
    return [jax.ShapeDtypeStruct((devices, rows, ghost_n), F32)]


def pair_forces(places, pairs, own_pos, own_kind, ghost_kind, incoming, weights, devices):
    neigh, centre, total = pairs
    blocks, lanes = neigh.shape
    latent, features = weights[3].shape
    atom_n = own_pos.shape[1]
    ghost_n = incoming.shape[-1]
    ghost_all = ghost_n * len(DIRECTIONS)
    ext_n = atom_n + ghost_all
    first_call = ghost_kind is None
    operands = [*places, total, neigh, centre, own_pos, own_kind, *weights, incoming]
    out_shape = [jax.ShapeDtypeStruct((3, atom_n), F32)] + exchange_shape(devices, 3, ghost_n)
    if first_call:
        out_shape = [jax.ShapeDtypeStruct((1, ghost_all), jnp.int32)] + out_shape
    else:
        operands.append(ghost_kind)
    pair_rows = blocks * lanes
    return pl.pallas_call(
        functools.partial(force_kernel, first_call=first_call),
        out_shape=out_shape,
        in_specs=[SMEM] * 3 + [VMEM] * (len(operands) - 3),
        out_specs=[VMEM] * len(out_shape),
        scratch_shapes=[
            pltpu.VMEM((blocks, ext_n + atom_n, lanes), BF16),
            pltpu.VMEM((blocks, 3 * atom_n, lanes), BF16),
            pltpu.VMEM((blocks, 8, lanes), F32),
            pltpu.VMEM((blocks, latent, lanes), BF16),
            pltpu.VMEM((blocks, features, lanes), F32),
            pltpu.VMEM((blocks, latent, lanes), F32),
            pltpu.VMEM((blocks, features, lanes), F32),
            pltpu.VMEM((blocks, 8, lanes), F32),
            pltpu.VMEM((features, 3 * atom_n), F32),
            pltpu.VMEM((features, 3 * atom_n), F32),
            pltpu.VMEM((24, ext_n + atom_n), F32),
        ],
        compiler_params=pltpu.CompilerParams(vmem_limit_bytes=48 * 2**20),
        cost_estimate=pl.CostEstimate(
            flops=pair_rows * latent * 2700, bytes_accessed=4 * 2**20, transcendentals=0
        ),
        name="pair_forces",
    )(*operands)


def small_call(kernel, name, smem_n, operands, out_shape):
    return pl.pallas_call(
        kernel,
        out_shape=out_shape,
        in_specs=[SMEM] * smem_n + [VMEM] * (len(operands) - smem_n),
        out_specs=[VMEM] * len(out_shape),
        compiler_params=pltpu.CompilerParams(vmem_limit_bytes=16 * 2**20),
        name=name,
    )(*operands)


def neighbour_devices(step):
    gx_n, yz_n = lax.axis_size("gx"), lax.axis_size("yz")
    gx, yz = lax.axis_index("gx"), lax.axis_index("yz")
    step_gx = jnp.array([a for a, _ in DIRECTIONS], jnp.int32) * step
    step_yz = jnp.array([b for _, b in DIRECTIONS], jnp.int32) * step
    return ((gx + step_gx + gx_n) % gx_n) * yz_n + (yz + step_yz + yz_n) % yz_n


def exchange(blocks):
    return lax.all_to_all(blocks, ("gx", "yz"), 0, 0, tiled=True)


def body(
    positions,
    velocities,
    forces_start,
    species,
    live_atoms,
    send_list,
    neighbours,
    neighbour_count,
    radial_weight,
    species_embed,
    env_weight,
    latent_weight,
    readout,
):
    atom_n = positions.shape[1]
    ghost_n = send_list.shape[1]
    devices = lax.axis_size("gx") * lax.axis_size("yz")
    ahead, behind = neighbour_devices(1), neighbour_devices(-1)
    kinds = species.reshape(1, atom_n)
    atoms = jax.ShapeDtypeStruct((3, atom_n), F32)
    row = jax.ShapeDtypeStruct((1, atom_n), F32)

    moved, half, inverse, sent = small_call(
        start_kernel,
        "start",
        1,
        [ahead, positions, velocities, forces_start, kinds, send_list],
        [atoms, atoms, row] + exchange_shape(devices, 4, ghost_n),
    )
    got = exchange(sent)
    pairs, weights = prepare(
        live_atoms, neighbour_count, neighbours, radial_weight, species_embed, env_weight, latent_weight, readout
    )
    places = (behind, behind)
    ghost_kind, own, sent = pair_forces(
        places, pairs, moved, kinds, None, got, weights, devices
    )
    got = exchange(sent)
    half_two, positions_end, sent = small_call(
        middle_kernel,
        "middle",
        2,
        [ahead, ahead, own, send_list, half, moved, inverse, got],
        [atoms, atoms] + exchange_shape(devices, 3, ghost_n),
    )
    got = exchange(sent)
    own, sent = pair_forces(
        places, pairs, positions_end, kinds, ghost_kind, got, weights, devices
    )
    got = exchange(sent)
    velocities_end, forces_end = small_call(
        last_kernel, "last", 1, [ahead, own, send_list, half_two, inverse, got], [atoms, atoms]
    )
    return (positions_end, velocities_end, forces_end)


def solution(mesh):
    placed = (
        P(None, ("gx", "yz")),
        P(None, ("gx", "yz")),
        P(None, ("gx", "yz")),
        P(("gx", "yz")),
        P(("gx", "yz")),
        P(None, ("gx", "yz")),
        P(("gx", "yz"), None),
        P(("gx", "yz")),
        P(),
        P(),
        P(),
        P(),
        P(),
    )
    return jax.shard_map(
        body,
        mesh=mesh,
        in_specs=placed,
        out_specs=(P(None, ("gx", "yz")), P(None, ("gx", "yz")), P(None, ("gx", "yz"))),
        check_vma=False,
    )
```

```python
import functools

import jax
import jax.numpy as jnp
from jax import lax
from jax.experimental import pallas as pl
from jax.experimental.pallas import tpu as pltpu
from jax.sharding import PartitionSpec as P

SPECIES = 8
SLOTS = 128
RADIUS = 6.0
STEP = 0.25
COUPLING = 4.0
MASSES = (1.008, 12.011, 14.007, 15.999, 32.06, 22.99, 35.45, 30.97)

LANES = 1024
DIRECTIONS = ((-1, -1), (-1, 0), (-1, 1), (0, -1), (0, 1), (1, -1), (1, 0), (1, 1))
BASIS_PAD = 16

F32 = jnp.float32
BF16 = jnp.bfloat16


def mm(left, right):
    return jnp.dot(left, right, preferred_element_type=F32)


def mm_nt(left, right):
    return lax.dot_general(left, right, (((1,), (1,)), ((), ())), preferred_element_type=F32)


def split3(values):
    high = values.astype(BF16)
    rest = values - high.astype(F32)
    mid = rest.astype(BF16)
    low = (rest - mid.astype(F32)).astype(BF16)
    return jnp.concatenate([high.astype(F32), mid.astype(F32), low.astype(F32)], axis=0).astype(BF16)


def one_hot(ids, rows):
    row_ids = lax.broadcasted_iota(jnp.int32, (rows, ids.shape[1]), 0)
    return jnp.where(row_ids == ids, 1.0, 0.0).astype(BF16)


SMEM = pl.BlockSpec(memory_space=pltpu.SMEM)
VMEM = pl.BlockSpec(memory_space=pltpu.VMEM)


def identity(size):
    row = lax.broadcasted_iota(jnp.int32, (size, size), 0)
    col = lax.broadcasted_iota(jnp.int32, (size, size), 1)
    return jnp.where(row == col, 1.0, 0.0).astype(BF16)


def padded_rows(values, rows):
    have, lanes = values.shape
    return jnp.concatenate([values, jnp.zeros((rows - have, lanes), values.dtype)], axis=0)


def sum_parts(parts):
    rows = parts.shape[0] // 3
    return parts[:rows] + parts[rows : 2 * rows] + parts[2 * rows :]


def by_direction(rows):
    return jnp.concatenate([rows[k : k + 1] for k in range(len(DIRECTIONS))], axis=1)


def put(out_ref, place_ref, blocks):
    ghost_n = blocks.shape[1] // len(DIRECTIONS)
    out_ref[...] = jnp.zeros_like(out_ref)
    for k in range(len(DIRECTIONS)):
        out_ref[place_ref[k]] = blocks[:, k * ghost_n : (k + 1) * ghost_n]


def take(in_ref, place_ref):
    return jnp.concatenate([in_ref[place_ref[k]] for k in range(len(DIRECTIONS))], axis=1)


def pick_ghosts(values, send_ref, atom_n):
    return sum_parts(mm(split3(values), one_hot(by_direction(send_ref[...]), atom_n)))


def inverse_mass(species):
    inverse = jnp.zeros(species.shape, F32)
    for spec_id, mass in enumerate(MASSES):
        inverse = jnp.where(species == spec_id, F32(1.0 / mass), inverse)
    return inverse


def start_kernel(
    place_ref, pos_ref, vel_ref, force_ref, species_ref, send_ref, moved_ref, half_ref, out_ref
):
    species = species_ref[...]
    inverse = inverse_mass(species)
    half = vel_ref[...] + 0.5 * STEP * inverse * force_ref[...]
    moved = pos_ref[...] + STEP * half
    half_ref[...] = half
    moved_ref[...] = moved
    spare = jnp.zeros((1, species.shape[1]), F32)
    sources = jnp.concatenate([moved, species.astype(F32), half, spare], axis=0)
    picked = pick_ghosts(sources, send_ref, species.shape[1])
    sends = jnp.concatenate([send_ref[...].astype(F32)] * len(DIRECTIONS), axis=1)
    put(out_ref, place_ref, jnp.concatenate([picked, sends], axis=0))


def total_force(own, back, sends):
    pick = one_hot(by_direction(sends), own.shape[1])
    return own + sum_parts(mm_nt(split3(padded_rows(back, 8)), pick))[0:3]


def domain_force(all_ref, owner, around_ref, first, sends, atom_n):
    ghost_n = sends.shape[1]
    back = []
    for k in range(len(DIRECTIONS)):
        start = atom_n + k * ghost_n
        back.append(all_ref[around_ref[first + k]][:, start : start + ghost_n])
    return total_force(all_ref[owner][:, :atom_n], jnp.concatenate(back, axis=1), sends)


def step_on(moved, half, kinds, forces):
    kick = 0.5 * STEP * inverse_mass(kinds) * forces
    half_two = half + kick + kick
    return half_two, moved + STEP * half_two


def last_kernel(place_ref, own_ref, send_ref, half_two_ref, species_ref, in_ref, vel_ref, force_ref):
    forces = total_force(own_ref[...], take(in_ref, place_ref), send_ref[...])
    force_ref[...] = forces
    vel_ref[...] = half_two_ref[...] + 0.5 * STEP * inverse_mass(species_ref[...]) * forces


def prepare_kernel(
    live_ref,
    count_ref,
    slots_ref,
    radial_ref,
    embed_ref,
    env_t_ref,
    latent_ref,
    readout_ref,
    neigh_ref,
    centre_ref,
    total_ref,
    embed_t_ref,
    radial_t_ref,
    on_hidden_ref,
    on_inner_ref,
    on_bent_ref,
    on_weight_ref,
    readout_t_ref,
    radial_back_ref,
):
    features, latent = env_t_ref.shape
    slots_t = mm_nt(identity(slots_ref.shape[1]), slots_ref[...].astype(F32).astype(BF16)).astype(BF16)
    list_pairs(live_ref, count_ref, slots_t, neigh_ref, centre_ref, total_ref)

    eye = identity(latent)
    half = BF16(0.5)
    latent_w = latent_ref[...]
    readout = readout_ref[...]
    none = jnp.zeros((BASIS_PAD - 8, latent), BF16)
    readout16 = padded_rows(readout.astype(F32), BASIS_PAD).astype(BF16)
    radial16 = jnp.concatenate([radial_ref[...] * half, none], axis=0)
    latent_t = mm_nt(eye, latent_w * half).astype(BF16)
    on_hidden_ref[...] = jnp.concatenate([latent_t[:, :latent], env_t_ref[...], readout16], axis=0)
    on_inner_ref[...] = latent_t[:, latent:]
    on_bent_ref[...] = (latent_w.astype(F32) * (0.5 * readout.astype(F32))).astype(BF16)
    on_weight_ref[...] = mm_nt(eye, jnp.concatenate([env_t_ref[...], readout16], axis=0)).astype(BF16)
    readout_t_ref[...] = mm_nt(eye, jnp.broadcast_to(readout.astype(F32), (128, latent)).astype(BF16))
    radial_back_ref[...] = radial16
    radial_t_ref[...] = mm_nt(eye, radial16).astype(BF16)
    embed_t_ref[...] = mm_nt(eye, jnp.concatenate([embed_ref[1], embed_ref[0]], axis=0) * half).astype(BF16)


def list_pairs(live_ref, count_ref, slots_t, neigh_ref, centre_ref, total_ref):
    atom_n = count_ref.shape[1]
    slot_n = slots_t.shape[0]
    blocks, lanes = neigh_ref.shape
    atom_row = lax.broadcasted_iota(jnp.int32, (1, atom_n), 1)
    used = jnp.where(atom_row < live_ref[0], count_ref[...], 0).astype(F32)
    row_i = lax.broadcasted_iota(jnp.int32, (atom_n, atom_n), 0)
    col_i = lax.broadcasted_iota(jnp.int32, (atom_n, atom_n), 1)
    end = jnp.sum(jnp.where(col_i <= row_i, used, 0.0), axis=1, keepdims=True)
    own = jnp.sum(jnp.where(col_i == row_i, used, 0.0), axis=1, keepdims=True)
    total = jnp.sum(used)
    total_ref[0] = total.astype(jnp.int32)
    lane = lax.broadcasted_iota(jnp.int32, (1, lanes), 1)

    def one_block(block, carry):
        place = (lane + block * lanes).astype(F32)
        past = end <= place
        centre = jnp.sum(jnp.where(past, 1.0, 0.0), axis=0, keepdims=True)
        start = jnp.sum(jnp.where(past, own, 0.0), axis=0, keepdims=True)
        slot = (place - start).astype(jnp.int32)
        centre_id = centre.astype(jnp.int32)
        rows = mm(slots_t, one_hot(centre_id, atom_n))
        slot_ids = lax.broadcasted_iota(jnp.int32, (slot_n, lanes), 0)
        neigh = jnp.sum(jnp.where(slot_ids == slot, rows, 0.0), axis=0, keepdims=True)
        valid = place < total
        neigh_ref[pl.ds(block, 1), :] = jnp.where(valid, neigh.astype(jnp.int32), -1)
        centre_ref[pl.ds(block, 1), :] = jnp.where(valid, centre_id, -1)
        return carry

    lax.fori_loop(0, blocks, one_block, 0)


def prepare(live_atoms, neighbour_count, neighbours, radial_weight, species_embed, env_weight, latent_weight, readout):
    atom_n, slot_n = neighbours.shape
    latent, features = env_weight.shape[1:]
    blocks = pl.cdiv(atom_n * slot_n, LANES)
    shapes = (
        ((blocks, LANES), jnp.int32),
        ((blocks, LANES), jnp.int32),
        ((1,), jnp.int32),
        ((latent, 16), BF16),
        ((latent, BASIS_PAD), BF16),
        ((latent + features + BASIS_PAD, latent), BF16),
        ((latent, features), BF16),
        ((latent + features, latent), BF16),
        ((latent, features + BASIS_PAD), BF16),
        ((latent, 128), F32),
        ((BASIS_PAD, latent), BF16),
    )
    out = pl.pallas_call(
        prepare_kernel,
        out_shape=[jax.ShapeDtypeStruct(*shape) for shape in shapes],
        in_specs=[SMEM] + [VMEM] * 7,
        out_specs=[VMEM, VMEM, SMEM] + [VMEM] * 8,
        compiler_params=pltpu.CompilerParams(vmem_limit_bytes=24 * 2**20),
        cost_estimate=pl.CostEstimate(flops=2 * 10**9, bytes_accessed=4 * 2**20, transcendentals=0),
        name="prepare",
    )(
        live_atoms,
        neighbour_count.reshape(1, atom_n),
        neighbours,
        radial_weight,
        species_embed,
        env_weight[0].T,
        latent_weight[0],
        readout[None, :],
    )
    return out[:3], out[3:]


def silu_pair(half_in):
    bent = jnp.tanh(half_in)
    part = half_in * bent
    return half_in + part, (1.0 + bent) * (1.0 + (half_in - part))


def force_kernel(
    place_ref,
    total_ref,
    around_ref,
    neigh_ref,
    centre_ref,
    moved_ref,
    own_kind_ref,
    embed_ref,
    radial_ref,
    on_hidden_ref,
    on_inner_ref,
    on_bent_ref,
    on_weight_ref,
    readout_ref,
    radial_back_ref,
    in_ref,
    *refs,
    second_call,
):
    *refs, hot_s, use_s, u_s, slope_s, raw_s, part_s, ain_s, energy_s, c_s, dc_s, f_s = refs
    blocks, lanes = neigh_ref.shape
    atom_n = moved_ref.shape[1]
    ghosts = take(in_ref, place_ref)
    ghost_n = ghosts.shape[1] // len(DIRECTIONS)
    ext_n = atom_n + ghosts.shape[1]
    ghost_kind = ghosts[3:4].astype(jnp.int32)
    own_kind = own_kind_ref[...]
    if second_call:
        half_ref, send_ref, all_ref, half_two_ref, end_ref, own_out_ref, out_ref = refs
        on_ghosts = []
        for k in range(len(DIRECTIONS)):
            owner = place_ref[k]
            sends = ghosts[8:16, k * ghost_n : (k + 1) * ghost_n].astype(jnp.int32)
            whole = domain_force(all_ref, owner, around_ref, k * 8, sends, atom_n)
            picked = mm(split3(padded_rows(whole, 8)), one_hot(sends[k : k + 1], atom_n))
            on_ghosts.append(sum_parts(picked)[0:3])
        _, ghost_pos = step_on(
            ghosts[0:3], ghosts[4:7], ghost_kind, jnp.concatenate(on_ghosts, axis=1)
        )
        here = len(DIRECTIONS)
        whole = domain_force(all_ref, place_ref[here], around_ref, here * 8, send_ref[...], atom_n)
        half_two, own_pos = step_on(moved_ref[...], half_ref[...], own_kind, whole)
        half_two_ref[...] = half_two
        end_ref[...] = own_pos
    else:
        (out_ref,) = refs
        own_pos, ghost_pos = moved_ref[...], ghosts[0:3]
    kind = jnp.concatenate([own_kind, ghost_kind], axis=1)
    pos = jnp.concatenate([own_pos, ghost_pos], axis=1)
    basis_n = SPECIES
    latent, features = on_inner_ref.shape
    count = (total_ref[0] + lanes - 1) // lanes
    scale = COUPLING * SLOTS ** (-0.5)

    pos8 = padded_rows(pos, 8) * (1.0 / RADIUS)
    pos_parts = split3(jnp.concatenate([pos8, -pos8[:, :atom_n]], axis=1))
    row8 = lax.broadcasted_iota(jnp.int32, (SPECIES, ext_n), 0)
    kinds = jnp.where(row8 == kind, 1.0, 0.0)
    none = jnp.zeros((SPECIES, ext_n), F32)
    neigh_embed = mm(embed_ref[...], jnp.concatenate([kinds, none], axis=0).astype(BF16))
    own_embed = mm(
        embed_ref[...],
        jnp.concatenate([none, kinds], axis=0)[:, :atom_n].astype(BF16),
    )
    weight_in = jnp.concatenate(
        [neigh_embed, own_embed, radial_ref[...].astype(F32)], axis=1
    ).astype(BF16)

    mid_row = lax.broadcasted_iota(jnp.int32, (BASIS_PAD, lanes), 0).astype(F32)
    mids = (mid_row + 0.5) / basis_n
    sharp = 2.0 * basis_n * basis_n

    c_s[...] = jnp.zeros_like(c_s)
    dc_s[...] = jnp.zeros_like(dc_s)
    f_s[...] = jnp.zeros_like(f_s)

    def geometry(block):
        vec = u_s[block]
        square = jnp.sum(vec * vec, axis=0, keepdims=True)
        inside = jnp.maximum(1.0 - square, 0.0)
        inside = jnp.where(centre_ref[pl.ds(block, 1), :] >= 0, inside, 0.0)
        apart = square - mids
        return vec, inside, apart, jnp.exp(-sharp * apart * apart)

    def first(block, carry):
        hot_j = one_hot(neigh_ref[pl.ds(block, 1), :], ext_n)
        hot_c = one_hot(centre_ref[pl.ds(block, 1), :], atom_n)
        hot = jnp.concatenate([hot_j, hot_c], axis=0)
        hot_s[block] = hot
        u_s[block] = sum_parts(mm(pos_parts, hot))
        vec, inside, _, basis = geometry(block)
        use = jnp.concatenate([hot_c * vec[k : k + 1].astype(BF16) for k in range(3)], axis=0)
        use_s[block] = use
        pre = mm(weight_in, jnp.concatenate([hot, basis.astype(BF16)], axis=0))
        hidden, slope = silu_pair(pre.astype(BF16))
        slope_s[block] = slope
        taken = mm(on_hidden_ref[...], hidden)
        part_s[block] = taken[:latent]
        raw = taken[latent : latent + features]
        raw_s[block] = raw
        energy_s[block] = taken[latent + features : latent + features + 8]
        c_s[...] += mm_nt((raw * (inside * inside)).astype(BF16), use)
        return carry

    lax.fori_loop(0, count, first, 0)
    c_all = c_s[...] * scale
    c_b = c_all.astype(BF16)

    def second(block, carry):
        _, inside, _, _ = geometry(block)
        use = use_s[block]
        env = inside * inside
        weight = raw_s[block] * env
        inner = weight * mm(c_b, use)
        later = part_s[block] + mm(on_inner_ref[...], inner.astype(BF16))
        gain, bent = silu_pair(later.astype(BF16))
        readout = jnp.concatenate([readout_ref[...]] * (lanes // 128), axis=1)
        energy_s[block] += jnp.sum(gain.astype(F32) * readout, axis=0, keepdims=True)
        taken = mm(on_bent_ref[...], bent)
        part_s[block] = taken[:latent]
        a_in = taken[latent:] * env
        ain_s[block] = a_in
        dc_s[...] += mm_nt((a_in * weight).astype(BF16), use)
        return carry

    lax.fori_loop(0, count, second, 0)
    c_dc = jnp.concatenate([c_all, dc_s[...] * scale], axis=0).astype(BF16)
    both = jnp.concatenate([c_all.T, dc_s[...].T * scale], axis=1).astype(BF16)

    def third(block, carry):
        vec, inside, apart, basis = geometry(block)
        use = use_s[block]
        hot = hot_s[block]
        env = inside * inside
        raw = raw_s[block]
        weight = raw * env
        a_in = ain_s[block]
        along = mm(c_dc, use)
        d_weight = a_in * along[:features] + along[features:]
        d_env = jnp.sum(d_weight * raw, axis=0, keepdims=True) + energy_s[block][0:1]
        ones = jnp.ones((BASIS_PAD, lanes), BF16)
        d_hidden = part_s[block] + mm(
            on_weight_ref[...], jnp.concatenate([d_weight.astype(BF16), ones], axis=0)
        )
        d_pre = d_hidden.astype(BF16) * slope_s[block]
        d_basis = mm(radial_back_ref[...], d_pre)
        d_square = env * jnp.sum(d_basis * basis * apart, axis=0, keepdims=True) * (-2.0 * sharp)
        d_square = d_square - 2.0 * inside * d_env
        d_all = mm(both, jnp.concatenate([a_in * weight, weight], axis=0).astype(BF16))
        hot_c = hot[ext_n:].astype(F32)
        picked = [
            jnp.sum(d_all[k * atom_n : (k + 1) * atom_n] * hot_c, axis=0, keepdims=True)
            for k in range(3)
        ]
        d_vec = jnp.concatenate(picked + [jnp.zeros((5, lanes), F32)], axis=0)
        d_vec = (d_vec + 2.0 * d_square * vec) * (1.0 / RADIUS)
        f_s[...] += mm_nt(split3(d_vec), hot)
        return carry

    lax.fori_loop(0, count, third, 0)
    summed = f_s[0:8] + f_s[8:16] + f_s[16:24]
    on_centre = summed[0:3, ext_n:]
    on_neigh = summed[0:3, :ext_n]
    own = on_centre - on_neigh[:, :atom_n]
    if second_call:
        own_out_ref[...] = own
        put(out_ref, place_ref, -on_neigh[:, atom_n:])
    else:
        every = jnp.concatenate([own, -on_neigh[:, atom_n:]], axis=1)
        out_ref[...] = jnp.broadcast_to(every[None], out_ref.shape)


def pair_forces(places, pairs, own_pos, own_kind, weights, incoming, second=()):
    place, around = places
    neigh, centre, total = pairs
    blocks, lanes = neigh.shape
    latent, features = weights[3].shape
    atom_n = own_pos.shape[1]
    devices, _, ghost_n = incoming.shape
    ext_n = atom_n + ghost_n * len(DIRECTIONS)
    operands = [place, total, around, neigh, centre, own_pos, own_kind, *weights, incoming, *second]
    if second:
        out_shape = [jax.ShapeDtypeStruct((3, atom_n), F32)] * 3
        out_shape.append(jax.ShapeDtypeStruct((devices, 3, ghost_n), F32))
    else:
        out_shape = [jax.ShapeDtypeStruct((devices, 3, ext_n), F32)]
    pair_rows = blocks * lanes
    return pl.pallas_call(
        functools.partial(force_kernel, second_call=bool(second)),
        out_shape=out_shape,
        in_specs=[SMEM] * 3 + [VMEM] * (len(operands) - 3),
        out_specs=[VMEM] * len(out_shape),
        scratch_shapes=[
            pltpu.VMEM((blocks, ext_n + atom_n, lanes), BF16),
            pltpu.VMEM((blocks, 3 * atom_n, lanes), BF16),
            pltpu.VMEM((blocks, 8, lanes), F32),
            pltpu.VMEM((blocks, latent, lanes), BF16),
            pltpu.VMEM((blocks, features, lanes), F32),
            pltpu.VMEM((blocks, latent, lanes), F32),
            pltpu.VMEM((blocks, features, lanes), F32),
            pltpu.VMEM((blocks, 8, lanes), F32),
            pltpu.VMEM((features, 3 * atom_n), F32),
            pltpu.VMEM((features, 3 * atom_n), F32),
            pltpu.VMEM((24, ext_n + atom_n), F32),
        ],
        compiler_params=pltpu.CompilerParams(vmem_limit_bytes=48 * 2**20),
        cost_estimate=pl.CostEstimate(
            flops=pair_rows * latent * 2700, bytes_accessed=4 * 2**20, transcendentals=0
        ),
        name="pair_forces",
    )(*operands)


def small_call(kernel, name, smem_n, operands, out_shape):
    return pl.pallas_call(
        kernel,
        out_shape=out_shape,
        in_specs=[SMEM] * smem_n + [VMEM] * (len(operands) - smem_n),
        out_specs=[VMEM] * len(out_shape),
        compiler_params=pltpu.CompilerParams(vmem_limit_bytes=16 * 2**20),
        name=name,
    )(*operands)


def devices_at(shift_gx, shift_yz):
    gx_n, yz_n = lax.axis_size("gx"), lax.axis_size("yz")
    gx = (lax.axis_index("gx") + jnp.asarray(shift_gx, jnp.int32) + gx_n) % gx_n
    yz = (lax.axis_index("yz") + jnp.asarray(shift_yz, jnp.int32) + yz_n) % yz_n
    return gx * yz_n + yz


def exchange(blocks):
    return lax.all_to_all(blocks, ("gx", "yz"), 0, 0, tiled=True)


def body(
    positions,
    velocities,
    forces_start,
    species,
    live_atoms,
    send_list,
    neighbours,
    neighbour_count,
    radial_weight,
    species_embed,
    env_weight,
    latent_weight,
    readout,
):
    atom_n = positions.shape[1]
    ghost_n = send_list.shape[1]
    devices = lax.axis_size("gx") * lax.axis_size("yz")
    ahead = devices_at([a for a, _ in DIRECTIONS], [b for _, b in DIRECTIONS])
    sources = [(-a, -b) for a, b in DIRECTIONS] + [(0, 0)]
    behind = devices_at([a for a, _ in sources], [b for _, b in sources])
    around = devices_at(
        [a + c for a, _ in sources for c, _ in DIRECTIONS], [b + d for _, b in sources for _, d in DIRECTIONS]
    )
    kinds = species.reshape(1, atom_n)
    atoms = jax.ShapeDtypeStruct((3, atom_n), F32)

    moved, half, sent = small_call(
        start_kernel,
        "start",
        1,
        [ahead, positions, velocities, forces_start, kinds, send_list],
        [atoms, atoms, jax.ShapeDtypeStruct((devices, 16, ghost_n), F32)],
    )
    got = exchange(sent)
    pairs, weights = prepare(
        live_atoms, neighbour_count, neighbours, radial_weight, species_embed, env_weight, latent_weight, readout
    )
    places = (behind, around)
    (sent,) = pair_forces(places, pairs, moved, kinds, weights, got)
    every = exchange(sent)
    half_two, positions_end, own, sent = pair_forces(
        places, pairs, moved, kinds, weights, got, (half, send_list, every)
    )
    back = exchange(sent)
    velocities_end, forces_end = small_call(
        last_kernel, "last", 1, [ahead, own, send_list, half_two, kinds, back], [atoms, atoms]
    )
    return (positions_end, velocities_end, forces_end)


def solution(mesh):
    placed = (
        P(None, ("gx", "yz")),
        P(None, ("gx", "yz")),
        P(None, ("gx", "yz")),
        P(("gx", "yz")),
        P(("gx", "yz")),
        P(None, ("gx", "yz")),
        P(("gx", "yz"), None),
        P(("gx", "yz")),
        P(),
        P(),
        P(),
        P(),
        P(),
    )
    return jax.shard_map(
        body,
        mesh=mesh,
        in_specs=placed,
        out_specs=(P(None, ("gx", "yz")), P(None, ("gx", "yz")), P(None, ("gx", "yz"))),
        check_vma=False,
    )
```

```python
import functools

import jax
import jax.numpy as jnp
from jax import lax
from jax.experimental import pallas as pl
from jax.experimental.pallas import tpu as pltpu
from jax.sharding import PartitionSpec as P

SPECIES = 8
SLOTS = 128
RADIUS = 6.0
STEP = 0.25
COUPLING = 4.0
MASSES = (1.008, 12.011, 14.007, 15.999, 32.06, 22.99, 35.45, 30.97)

LANES = 1024
DIRECTIONS = ((-1, -1), (-1, 0), (-1, 1), (0, -1), (0, 1), (1, -1), (1, 0), (1, 1))
BASIS_PAD = 16

F32 = jnp.float32
BF16 = jnp.bfloat16


def mm(left, right):
    return jnp.dot(left, right, preferred_element_type=F32)


def mm_nt(left, right):
    return lax.dot_general(left, right, (((1,), (1,)), ((), ())), preferred_element_type=F32)


def split3(values):
    high = values.astype(BF16)
    rest = values - high.astype(F32)
    mid = rest.astype(BF16)
    low = (rest - mid.astype(F32)).astype(BF16)
    return jnp.concatenate([high.astype(F32), mid.astype(F32), low.astype(F32)], axis=0).astype(BF16)


def one_hot(ids, rows):
    row_ids = lax.broadcasted_iota(jnp.int32, (rows, ids.shape[1]), 0)
    return jnp.where(row_ids == ids, 1.0, 0.0).astype(BF16)


SMEM = pl.BlockSpec(memory_space=pltpu.SMEM)
VMEM = pl.BlockSpec(memory_space=pltpu.VMEM)


def identity(size):
    row = lax.broadcasted_iota(jnp.int32, (size, size), 0)
    col = lax.broadcasted_iota(jnp.int32, (size, size), 1)
    return jnp.where(row == col, 1.0, 0.0).astype(BF16)


def padded_rows(values, rows):
    have, lanes = values.shape
    return jnp.concatenate([values, jnp.zeros((rows - have, lanes), values.dtype)], axis=0)


def sum_parts(parts):
    rows = parts.shape[0] // 3
    return parts[:rows] + parts[rows : 2 * rows] + parts[2 * rows :]


def by_direction(rows):
    return jnp.concatenate([rows[k : k + 1] for k in range(len(DIRECTIONS))], axis=1)


def put(out_ref, place_ref, blocks):
    ghost_n = blocks.shape[1] // len(DIRECTIONS)
    out_ref[...] = jnp.zeros_like(out_ref)
    for k in range(len(DIRECTIONS)):
        out_ref[place_ref[k]] = blocks[:, k * ghost_n : (k + 1) * ghost_n]


def take(in_ref, place_ref):
    return jnp.concatenate([in_ref[place_ref[k]] for k in range(len(DIRECTIONS))], axis=1)


def inverse_mass(species):
    inverse = jnp.zeros(species.shape, F32)
    for spec_id, mass in enumerate(MASSES):
        inverse = jnp.where(species == spec_id, F32(1.0 / mass), inverse)
    return inverse


def start_kernel(pos_ref, vel_ref, force_ref, species_ref, send_ref, moved_ref, half_ref, out_ref):
    species = species_ref[...]
    inverse = inverse_mass(species)
    half = vel_ref[...] + 0.5 * STEP * inverse * force_ref[...]
    moved = pos_ref[...] + STEP * half
    half_ref[...] = half
    moved_ref[...] = moved
    spare = jnp.zeros((1, species.shape[1]), F32)
    sends = send_ref[...].astype(F32)
    sends = jnp.concatenate([sends, jnp.zeros((8, species.shape[1] - sends.shape[1]), F32)], axis=1)
    out_ref[...] = jnp.concatenate([moved, species.astype(F32), half, spare, sends], axis=0)


def total_force(own, back, sends):
    pick = one_hot(by_direction(sends), own.shape[1])
    return own + sum_parts(mm_nt(split3(padded_rows(back, 8)), pick))[0:3]


def domain_force(all_ref, owner, around_ref, first, sends, atom_n):
    ghost_n = sends.shape[1]
    back = []
    for k in range(len(DIRECTIONS)):
        start = atom_n + k * ghost_n
        back.append(all_ref[around_ref[first + k]][:, start : start + ghost_n])
    return total_force(all_ref[owner][:, :atom_n], jnp.concatenate(back, axis=1), sends)


def step_on(moved, half, kinds, forces):
    kick = 0.5 * STEP * inverse_mass(kinds) * forces
    half_two = half + kick + kick
    return half_two, moved + STEP * half_two


def last_kernel(place_ref, own_ref, send_ref, half_two_ref, species_ref, in_ref, vel_ref, force_ref):
    forces = total_force(own_ref[...], take(in_ref, place_ref), send_ref[...])
    force_ref[...] = forces
    vel_ref[...] = half_two_ref[...] + 0.5 * STEP * inverse_mass(species_ref[...]) * forces


def prepare_kernel(
    live_ref,
    count_ref,
    slots_ref,
    radial_ref,
    embed_ref,
    env_t_ref,
    latent_ref,
    readout_ref,
    neigh_ref,
    centre_ref,
    total_ref,
    into_ref,
    on_hidden_ref,
    on_inner_ref,
    on_bent_ref,
    on_weight_ref,
    readout_t_ref,
    radial_back_ref,
):
    features, latent = env_t_ref.shape
    slots_t = mm_nt(identity(slots_ref.shape[1]), slots_ref[...].astype(F32).astype(BF16)).astype(BF16)
    list_pairs(live_ref, count_ref, slots_t, neigh_ref, centre_ref, total_ref)

    eye = identity(latent)
    half = BF16(0.5)
    latent_w = latent_ref[...]
    readout = readout_ref[...]
    none = jnp.zeros((BASIS_PAD - 8, latent), BF16)
    readout16 = padded_rows(readout.astype(F32), BASIS_PAD).astype(BF16)
    radial16 = jnp.concatenate([radial_ref[...] * half, none], axis=0)
    latent_t = mm_nt(eye, latent_w * half).astype(BF16)
    on_hidden_ref[...] = jnp.concatenate([latent_t[:, :latent], env_t_ref[...], readout16], axis=0)
    on_inner_ref[...] = latent_t[:, latent:]
    on_bent_ref[...] = (latent_w.astype(F32) * (0.5 * readout.astype(F32))).astype(BF16)
    on_weight_ref[...] = mm_nt(eye, jnp.concatenate([env_t_ref[...], readout16], axis=0)).astype(BF16)
    readout_t_ref[...] = mm_nt(eye, jnp.broadcast_to(readout.astype(F32), (128, latent)).astype(BF16))
    radial_back_ref[...] = radial16
    into = jnp.concatenate([embed_ref[1] * half, embed_ref[0] * half, radial16], axis=0)
    into_ref[...] = mm_nt(eye, into).astype(BF16)


def list_pairs(live_ref, count_ref, slots_t, neigh_ref, centre_ref, total_ref):
    atom_n = count_ref.shape[1]
    slot_n = slots_t.shape[0]
    blocks, lanes = neigh_ref.shape
    atom_row = lax.broadcasted_iota(jnp.int32, (1, atom_n), 1)
    used = jnp.where(atom_row < live_ref[0], count_ref[...], 0).astype(F32)
    row_i = lax.broadcasted_iota(jnp.int32, (atom_n, atom_n), 0)
    col_i = lax.broadcasted_iota(jnp.int32, (atom_n, atom_n), 1)
    end = jnp.sum(jnp.where(col_i <= row_i, used, 0.0), axis=1, keepdims=True)
    own = jnp.sum(jnp.where(col_i == row_i, used, 0.0), axis=1, keepdims=True)
    total = jnp.sum(used)
    total_ref[0] = total.astype(jnp.int32)
    lane = lax.broadcasted_iota(jnp.int32, (1, lanes), 1)

    def one_block(block, carry):
        place = (lane + block * lanes).astype(F32)
        past = end <= place
        centre = jnp.sum(jnp.where(past, 1.0, 0.0), axis=0, keepdims=True)
        start = jnp.sum(jnp.where(past, own, 0.0), axis=0, keepdims=True)
        slot = (place - start).astype(jnp.int32)
        centre_id = centre.astype(jnp.int32)
        rows = mm(slots_t, one_hot(centre_id, atom_n))
        slot_ids = lax.broadcasted_iota(jnp.int32, (slot_n, lanes), 0)
        neigh = jnp.sum(jnp.where(slot_ids == slot, rows, 0.0), axis=0, keepdims=True)
        valid = place < total
        neigh_ref[pl.ds(block, 1), :] = jnp.where(valid, neigh.astype(jnp.int32), -1)
        centre_ref[pl.ds(block, 1), :] = jnp.where(valid, centre_id, -1)
        return carry

    lax.fori_loop(0, blocks, one_block, 0)


def prepare(live_atoms, neighbour_count, neighbours, radial_weight, species_embed, env_weight, latent_weight, readout):
    atom_n, slot_n = neighbours.shape
    latent, features = env_weight.shape[1:]
    blocks = pl.cdiv(atom_n * slot_n, LANES)
    shapes = (
        ((blocks, LANES), jnp.int32),
        ((blocks, LANES), jnp.int32),
        ((1,), jnp.int32),
        ((latent, 2 * SPECIES + BASIS_PAD), BF16),
        ((latent + features + BASIS_PAD, latent), BF16),
        ((latent, features), BF16),
        ((latent + features, latent), BF16),
        ((latent, features + BASIS_PAD), BF16),
        ((latent, 128), F32),
        ((BASIS_PAD, latent), BF16),
    )
    out = pl.pallas_call(
        prepare_kernel,
        out_shape=[jax.ShapeDtypeStruct(*shape) for shape in shapes],
        in_specs=[SMEM] + [VMEM] * 7,
        out_specs=[VMEM, VMEM, SMEM] + [VMEM] * 7,
        compiler_params=pltpu.CompilerParams(vmem_limit_bytes=24 * 2**20),
        cost_estimate=pl.CostEstimate(flops=2 * 10**9, bytes_accessed=4 * 2**20, transcendentals=0),
        name="prepare",
    )(
        live_atoms,
        neighbour_count.reshape(1, atom_n),
        neighbours,
        radial_weight,
        species_embed,
        env_weight[0].T,
        latent_weight[0],
        readout[None, :],
    )
    return out[:3], out[3:]


def silu_pair(half_in):
    bent = jnp.tanh(half_in)
    part = half_in * bent
    return half_in + part, (1.0 + bent) * (1.0 + (half_in - part))


def force_kernel(
    place_ref,
    total_ref,
    around_ref,
    neigh_ref,
    centre_ref,
    moved_ref,
    own_kind_ref,
    into_ref,
    on_hidden_ref,
    on_inner_ref,
    on_bent_ref,
    on_weight_ref,
    readout_ref,
    radial_back_ref,
    in_ref,
    *refs,
    second_call,
    out_ghost_n,
):
    *refs, hot_s, use_s, u_s, slope_s, raw_s, part_s, ain_s, energy_s, c_s, dc_s, f_s = refs
    blocks, lanes = neigh_ref.shape
    atom_n = moved_ref.shape[1]
    ghost_n = out_ghost_n
    ext_n = atom_n + ghost_n * len(DIRECTIONS)
    own_kind = own_kind_ref[...]
    from_owners = [in_ref[place_ref[k]] for k in range(len(DIRECTIONS))]
    sends = [owner[8:16, :ghost_n].astype(jnp.int32) for owner in from_owners]
    picks = [one_hot(sends[k][k : k + 1], atom_n) for k in range(len(DIRECTIONS))]
    ghosts = jnp.concatenate(
        [sum_parts(mm(split3(owner[0:8]), pick)) for owner, pick in zip(from_owners, picks)], axis=1
    )
    ghost_kind = ghosts[3:4].astype(jnp.int32)
    if second_call:
        half_ref, send_ref, all_ref, half_two_ref, end_ref, own_out_ref, out_ref = refs
        on_ghosts = []
        for k in range(len(DIRECTIONS)):
            whole = domain_force(all_ref, place_ref[k], around_ref, k * 8, sends[k], atom_n)
            on_ghosts.append(sum_parts(mm(split3(padded_rows(whole, 8)), picks[k]))[0:3])
        _, ghost_pos = step_on(
            ghosts[0:3], ghosts[4:7], ghost_kind, jnp.concatenate(on_ghosts, axis=1)
        )
        here = len(DIRECTIONS)
        whole = domain_force(all_ref, place_ref[here], around_ref, here * 8, send_ref[...], atom_n)
        half_two, own_pos = step_on(moved_ref[...], half_ref[...], own_kind, whole)
        half_two_ref[...] = half_two
        end_ref[...] = own_pos
    else:
        (out_ref,) = refs
        own_pos, ghost_pos = moved_ref[...], ghosts[0:3]
    kind = jnp.concatenate([own_kind, ghost_kind], axis=1)
    pos = jnp.concatenate([own_pos, ghost_pos], axis=1)
    basis_n = SPECIES
    latent, features = on_inner_ref.shape
    count = (total_ref[0] + lanes - 1) // lanes
    scale = COUPLING * SLOTS ** (-0.5)

    pos8 = padded_rows(pos, 8) * (1.0 / RADIUS)
    pos_parts = split3(jnp.concatenate([pos8, -pos8[:, :atom_n]], axis=1))
    row8 = lax.broadcasted_iota(jnp.int32, (SPECIES, ext_n), 0)
    kinds = jnp.where(row8 == kind, 1.0, 0.0)
    basis_in = identity(BASIS_PAD).astype(F32)
    selected = jnp.concatenate(
        [
            jnp.concatenate([kinds, jnp.zeros((SPECIES + BASIS_PAD, ext_n), F32)], axis=0),
            jnp.concatenate(
                [jnp.zeros((SPECIES, atom_n), F32), kinds[:, :atom_n], jnp.zeros((BASIS_PAD, atom_n), F32)], axis=0
            ),
            jnp.concatenate([jnp.zeros((2 * SPECIES, BASIS_PAD), F32), basis_in], axis=0),
        ],
        axis=1,
    )
    weight_in = mm(into_ref[...], selected.astype(BF16)).astype(BF16)

    mid_row = lax.broadcasted_iota(jnp.int32, (BASIS_PAD, lanes), 0).astype(F32)
    mids = (mid_row + 0.5) / basis_n
    sharp = 2.0 * basis_n * basis_n

    c_s[...] = jnp.zeros_like(c_s)
    dc_s[...] = jnp.zeros_like(dc_s)
    f_s[...] = jnp.zeros_like(f_s)

    def geometry(block):
        vec = u_s[block]
        square = jnp.sum(vec * vec, axis=0, keepdims=True)
        inside = jnp.maximum(1.0 - square, 0.0)
        inside = jnp.where(centre_ref[pl.ds(block, 1), :] >= 0, inside, 0.0)
        apart = square - mids
        return vec, inside, apart, jnp.exp(-sharp * apart * apart)

    def first(block, carry):
        hot_j = one_hot(neigh_ref[pl.ds(block, 1), :], ext_n)
        hot_c = one_hot(centre_ref[pl.ds(block, 1), :], atom_n)
        hot = jnp.concatenate([hot_j, hot_c], axis=0)
        hot_s[block] = hot
        u_s[block] = sum_parts(mm(pos_parts, hot))
        vec, inside, _, basis = geometry(block)
        use = jnp.concatenate([hot_c * vec[k : k + 1].astype(BF16) for k in range(3)], axis=0)
        use_s[block] = use
        pre = mm(weight_in, jnp.concatenate([hot, basis.astype(BF16)], axis=0))
        hidden, slope = silu_pair(pre)
        slope_s[block] = slope.astype(BF16)
        taken = mm(on_hidden_ref[...], hidden.astype(BF16))
        part_s[block] = taken[:latent]
        raw = taken[latent : latent + features]
        raw_s[block] = raw
        energy_s[block] = taken[latent + features : latent + features + 8]
        c_s[...] += mm_nt((raw * (inside * inside)).astype(BF16), use)
        return carry

    lax.fori_loop(0, count, first, 0)
    c_all = c_s[...] * scale
    c_b = c_all.astype(BF16)

    def second(block, carry):
        _, inside, _, _ = geometry(block)
        use = use_s[block]
        env = inside * inside
        weight = raw_s[block] * env
        inner = weight * mm(c_b, use)
        later = part_s[block] + mm(on_inner_ref[...], inner.astype(BF16))
        gain, bent = silu_pair(later)
        readout = jnp.concatenate([readout_ref[...]] * (lanes // 128), axis=1)
        energy_s[block] += jnp.sum(gain * readout, axis=0, keepdims=True)
        taken = mm(on_bent_ref[...], bent.astype(BF16))
        part_s[block] = taken[:latent]
        a_in = taken[latent:] * env
        ain_s[block] = a_in
        dc_s[...] += mm_nt((a_in * weight).astype(BF16), use)
        return carry

    lax.fori_loop(0, count, second, 0)
    c_dc = jnp.concatenate([c_all, dc_s[...] * scale], axis=0).astype(BF16)
    both = jnp.concatenate([c_all.T, dc_s[...].T * scale], axis=1).astype(BF16)

    def third(block, carry):
        vec, inside, apart, basis = geometry(block)
        use = use_s[block]
        hot = hot_s[block]
        env = inside * inside
        raw = raw_s[block]
        weight = raw * env
        a_in = ain_s[block]
        along = mm(c_dc, use)
        d_weight = a_in * along[:features] + along[features:]
        d_env = jnp.sum(d_weight * raw, axis=0, keepdims=True) + energy_s[block][0:1]
        ones = jnp.ones((BASIS_PAD, lanes), BF16)
        d_hidden = part_s[block] + mm(
            on_weight_ref[...], jnp.concatenate([d_weight.astype(BF16), ones], axis=0)
        )
        d_pre = (d_hidden * slope_s[block].astype(F32)).astype(BF16)
        d_basis = mm(radial_back_ref[...], d_pre)
        d_square = env * jnp.sum(d_basis * basis * apart, axis=0, keepdims=True) * (-2.0 * sharp)
        d_square = d_square - 2.0 * inside * d_env
        d_all = mm(both, jnp.concatenate([a_in * weight, weight], axis=0).astype(BF16))
        hot_c = hot[ext_n:].astype(F32)
        picked = [
            jnp.sum(d_all[k * atom_n : (k + 1) * atom_n] * hot_c, axis=0, keepdims=True)
            for k in range(3)
        ]
        d_vec = jnp.concatenate(picked + [jnp.zeros((5, lanes), F32)], axis=0)
        d_vec = (d_vec + 2.0 * d_square * vec) * (1.0 / RADIUS)
        f_s[...] += mm_nt(split3(d_vec), hot)
        return carry

    lax.fori_loop(0, count, third, 0)
    summed = f_s[0:8] + f_s[8:16] + f_s[16:24]
    on_centre = summed[0:3, ext_n:]
    on_neigh = summed[0:3, :ext_n]
    own = on_centre - on_neigh[:, :atom_n]
    if second_call:
        own_out_ref[...] = own
        put(out_ref, place_ref, -on_neigh[:, atom_n:])
    else:
        out_ref[...] = jnp.concatenate([own, -on_neigh[:, atom_n:]], axis=1)


def pair_forces(places, pairs, own_pos, own_kind, weights, incoming, ghost_n, second=()):
    place, around = places
    neigh, centre, total = pairs
    blocks, lanes = neigh.shape
    latent, features = weights[2].shape
    atom_n = own_pos.shape[1]
    devices = incoming.shape[0]
    ext_n = atom_n + ghost_n * len(DIRECTIONS)
    operands = [place, total, around, neigh, centre, own_pos, own_kind, *weights, incoming, *second]
    if second:
        out_shape = [jax.ShapeDtypeStruct((3, atom_n), F32)] * 3
        out_shape.append(jax.ShapeDtypeStruct((devices, 3, ghost_n), F32))
    else:
        out_shape = [jax.ShapeDtypeStruct((3, ext_n), F32)]
    pair_rows = blocks * lanes
    return pl.pallas_call(
        functools.partial(force_kernel, second_call=bool(second), out_ghost_n=ghost_n),
        out_shape=out_shape,
        in_specs=[SMEM] * 3 + [VMEM] * (len(operands) - 3),
        out_specs=[VMEM] * len(out_shape),
        scratch_shapes=[
            pltpu.VMEM((blocks, ext_n + atom_n, lanes), BF16),
            pltpu.VMEM((blocks, 3 * atom_n, lanes), BF16),
            pltpu.VMEM((blocks, 8, lanes), F32),
            pltpu.VMEM((blocks, latent, lanes), BF16),
            pltpu.VMEM((blocks, features, lanes), F32),
            pltpu.VMEM((blocks, latent, lanes), F32),
            pltpu.VMEM((blocks, features, lanes), F32),
            pltpu.VMEM((blocks, 8, lanes), F32),
            pltpu.VMEM((features, 3 * atom_n), F32),
            pltpu.VMEM((features, 3 * atom_n), F32),
            pltpu.VMEM((24, ext_n + atom_n), F32),
        ],
        compiler_params=pltpu.CompilerParams(vmem_limit_bytes=48 * 2**20),
        cost_estimate=pl.CostEstimate(
            flops=pair_rows * latent * 2700, bytes_accessed=4 * 2**20, transcendentals=0
        ),
        name="pair_forces",
    )(*operands)


def small_call(kernel, name, smem_n, operands, out_shape):
    return pl.pallas_call(
        kernel,
        out_shape=out_shape,
        in_specs=[SMEM] * smem_n + [VMEM] * (len(operands) - smem_n),
        out_specs=[VMEM] * len(out_shape),
        compiler_params=pltpu.CompilerParams(vmem_limit_bytes=16 * 2**20),
        name=name,
    )(*operands)


def devices_at(shift_gx, shift_yz):
    gx_n, yz_n = lax.axis_size("gx"), lax.axis_size("yz")
    gx = (lax.axis_index("gx") + jnp.asarray(shift_gx, jnp.int32) + gx_n) % gx_n
    yz = (lax.axis_index("yz") + jnp.asarray(shift_yz, jnp.int32) + yz_n) % yz_n
    return gx * yz_n + yz


def gather_all(block):
    return lax.all_gather(block, ("gx", "yz"))


def exchange(blocks):
    return lax.all_to_all(blocks, ("gx", "yz"), 0, 0, tiled=True)


def body(
    positions,
    velocities,
    forces_start,
    species,
    live_atoms,
    send_list,
    neighbours,
    neighbour_count,
    radial_weight,
    species_embed,
    env_weight,
    latent_weight,
    readout,
):
    atom_n = positions.shape[1]
    ghost_n = send_list.shape[1]
    ahead = devices_at([a for a, _ in DIRECTIONS], [b for _, b in DIRECTIONS])
    sources = [(-a, -b) for a, b in DIRECTIONS] + [(0, 0)]
    behind = devices_at([a for a, _ in sources], [b for _, b in sources])
    around = devices_at(
        [a + c for a, _ in sources for c, _ in DIRECTIONS], [b + d for _, b in sources for _, d in DIRECTIONS]
    )
    kinds = species.reshape(1, atom_n)
    atoms = jax.ShapeDtypeStruct((3, atom_n), F32)

    moved, half, sent = small_call(
        start_kernel,
        "start",
        0,
        [positions, velocities, forces_start, kinds, send_list],
        [atoms, atoms, jax.ShapeDtypeStruct((16, atom_n), F32)],
    )
    got = gather_all(sent)
    pairs, weights = prepare(
        live_atoms, neighbour_count, neighbours, radial_weight, species_embed, env_weight, latent_weight, readout
    )
    places = (behind, around)
    (sent,) = pair_forces(places, pairs, moved, kinds, weights, got, ghost_n)
    every = gather_all(sent)
    half_two, positions_end, own, sent = pair_forces(
        places, pairs, moved, kinds, weights, got, ghost_n, (half, send_list, every)
    )
    back = exchange(sent)
    velocities_end, forces_end = small_call(
        last_kernel, "last", 1, [ahead, own, send_list, half_two, kinds, back], [atoms, atoms]
    )
    return (positions_end, velocities_end, forces_end)


def solution(mesh):
    placed = (
        P(None, ("gx", "yz")),
        P(None, ("gx", "yz")),
        P(None, ("gx", "yz")),
        P(("gx", "yz")),
        P(("gx", "yz")),
        P(None, ("gx", "yz")),
        P(("gx", "yz"), None),
        P(("gx", "yz")),
        P(),
        P(),
        P(),
        P(),
        P(),
    )
    return jax.shard_map(
        body,
        mesh=mesh,
        in_specs=placed,
        out_specs=(P(None, ("gx", "yz")), P(None, ("gx", "yz")), P(None, ("gx", "yz"))),
        check_vma=False,
    )
```

```python
import functools

import jax
import jax.numpy as jnp
from jax import lax
from jax.experimental import pallas as pl
from jax.experimental.pallas import tpu as pltpu
from jax.sharding import PartitionSpec as P

SPECIES = 8
SLOTS = 128
RADIUS = 6.0
STEP = 0.25
COUPLING = 4.0
MASSES = (1.008, 12.011, 14.007, 15.999, 32.06, 22.99, 35.45, 30.97)

LANES = 1024
DIRECTIONS = ((-1, -1), (-1, 0), (-1, 1), (0, -1), (0, 1), (1, -1), (1, 0), (1, 1))
TILE = (8, 128)
BASIS_PAD = 16

F32 = jnp.float32
BF16 = jnp.bfloat16


def mm(left, right):
    return jnp.dot(left, right, preferred_element_type=F32)


def mm_nt(left, right):
    return lax.dot_general(left, right, (((1,), (1,)), ((), ())), preferred_element_type=F32)


def split3(values):
    high = values.astype(BF16)
    rest = values - high.astype(F32)
    mid = rest.astype(BF16)
    low = (rest - mid.astype(F32)).astype(BF16)
    return jnp.concatenate([high.astype(F32), mid.astype(F32), low.astype(F32)], axis=0).astype(BF16)


def one_hot(ids, rows):
    row_ids = lax.broadcasted_iota(jnp.int32, (rows, ids.shape[1]), 0)
    return jnp.where(row_ids == ids, 1.0, 0.0).astype(BF16)


SMEM = pl.BlockSpec(memory_space=pltpu.SMEM)
VMEM = pl.BlockSpec(memory_space=pltpu.VMEM)


def identity(size):
    row = lax.broadcasted_iota(jnp.int32, (size, size), 0)
    col = lax.broadcasted_iota(jnp.int32, (size, size), 1)
    return jnp.where(row == col, 1.0, 0.0).astype(BF16)


def padded_rows(values, rows):
    have, lanes = values.shape
    return jnp.concatenate([values, jnp.zeros((rows - have, lanes), values.dtype)], axis=0)


def sum_parts(parts):
    rows = parts.shape[0] // 3
    return parts[:rows] + parts[rows : 2 * rows] + parts[2 * rows :]


def by_direction(rows):
    return jnp.concatenate([rows[k : k + 1] for k in range(len(DIRECTIONS))], axis=1)


def put(out_ref, place_ref, blocks):
    ghost_n = blocks.shape[1] // len(DIRECTIONS)
    out_ref[...] = jnp.zeros_like(out_ref)
    for k in range(len(DIRECTIONS)):
        out_ref[place_ref[k]] = blocks[:, k * ghost_n : (k + 1) * ghost_n]


def take(in_ref, place_ref):
    return jnp.concatenate([in_ref[place_ref[k]] for k in range(len(DIRECTIONS))], axis=1)


def inverse_mass(species):
    inverse = jnp.zeros(species.shape, F32)
    for spec_id, mass in enumerate(MASSES):
        inverse = jnp.where(species == spec_id, F32(1.0 / mass), inverse)
    return inverse


def fetch(pairs, sems):
    copies = [pltpu.make_async_copy(src, dst, sems.at[n]) for n, (src, dst) in enumerate(pairs)]
    for copy in copies:
        copy.start()
    return copies


def start_kernel(
    place_ref, pos_hbm, vel_hbm, force_hbm, species_hbm, send_hbm, moved_ref, half_ref, out_ref, *scratch
):
    pos_ref, vel_ref, force_ref, species_ref, send_ref, sems = scratch
    copies = fetch(
        [
            (pos_hbm, pos_ref),
            (vel_hbm, vel_ref),
            (force_hbm, force_ref),
            (species_hbm, species_ref),
            (send_hbm, send_ref),
        ],
        sems,
    )
    out_ref[...] = jnp.zeros_like(out_ref)
    for copy in copies:
        copy.wait()
    species = species_ref[...]
    half = vel_ref[...] + 0.5 * STEP * inverse_mass(species) * force_ref[...]
    moved = pos_ref[...] + STEP * half
    half_ref[...] = half
    moved_ref[...] = moved
    spare = jnp.zeros((1, species.shape[1]), F32)
    sources = split3(jnp.concatenate([moved, species.astype(F32), half, spare], axis=0))
    sends = send_ref[...]
    picked = sum_parts(mm(sources, one_hot(by_direction(sends), species.shape[1])))
    sent = sends.astype(F32)
    ghost_n = sent.shape[1]
    rest = jnp.zeros((TILE[0], TILE[1] - 2 * ghost_n), F32)
    for k in range(len(DIRECTIONS)):
        block = picked[:, k * ghost_n : (k + 1) * ghost_n]
        out_ref[place_ref[k]] = jnp.concatenate([block, sent, rest], axis=1)


def total_force(own, back, sends):
    pick = one_hot(by_direction(sends), own.shape[1])
    return own + sum_parts(mm_nt(split3(padded_rows(back, 8)), pick))[0:3]


def domain_force(all_ref, owner, around_ref, first, sends, atom_n):
    ghost_n = sends.shape[1]
    back = []
    for k in range(len(DIRECTIONS)):
        start = k * ghost_n
        back.append(all_ref[around_ref[first + k]][0:3, start : start + ghost_n])
    return total_force(all_ref[owner][3:6, :atom_n], jnp.concatenate(back, axis=1), sends)


def step_on(moved, half, kinds, forces):
    kick = 0.5 * STEP * inverse_mass(kinds) * forces
    half_two = half + kick + kick
    return half_two, moved + STEP * half_two


def last_kernel(place_ref, own_ref, send_ref, half_two_ref, species_ref, in_ref, vel_ref, force_ref):
    forces = total_force(own_ref[...], take(in_ref, place_ref), send_ref[...])
    force_ref[...] = forces
    vel_ref[...] = half_two_ref[...] + 0.5 * STEP * inverse_mass(species_ref[...]) * forces


def prepare_kernel(
    live_ref,
    radial_ref,
    embed_ref,
    readout_ref,
    count_hbm,
    slots_hbm,
    env_t_hbm,
    latent_hbm,
    neigh_ref,
    centre_ref,
    total_ref,
    into_ref,
    on_hidden_ref,
    on_inner_ref,
    on_bent_ref,
    on_weight_ref,
    readout_t_ref,
    radial_back_ref,
    count_ref,
    slots_ref,
    env_t_ref,
    latent_ref,
    sems,
):
    copies = fetch(
        [
            (count_hbm, count_ref),
            (slots_hbm, slots_ref),
            (env_t_hbm, env_t_ref),
            (latent_hbm, latent_ref),
        ],
        sems,
    )
    features, latent = env_t_ref.shape
    for copy in copies[:2]:
        copy.wait()
    slots_t = mm_nt(identity(slots_ref.shape[1]), slots_ref[...].astype(F32).astype(BF16)).astype(BF16)
    list_pairs(live_ref, count_ref, slots_t, neigh_ref, centre_ref, total_ref)
    for copy in copies[2:]:
        copy.wait()

    eye = identity(latent)
    half = BF16(0.5)
    latent_w = latent_ref[...]
    readout = readout_ref[...]
    none = jnp.zeros((BASIS_PAD - 8, latent), BF16)
    readout16 = padded_rows(readout.astype(F32), BASIS_PAD).astype(BF16)
    radial16 = jnp.concatenate([radial_ref[...] * half, none], axis=0)
    latent_t = mm_nt(eye, latent_w * half).astype(BF16)
    on_hidden_ref[...] = jnp.concatenate([latent_t[:, :latent], env_t_ref[...], readout16], axis=0)
    on_inner_ref[...] = latent_t[:, latent:]
    on_bent_ref[...] = (latent_w.astype(F32) * (0.5 * readout.astype(F32))).astype(BF16)
    on_weight_ref[...] = mm_nt(eye, jnp.concatenate([env_t_ref[...], readout16], axis=0)).astype(BF16)
    readout_t_ref[...] = mm_nt(eye, jnp.broadcast_to(readout.astype(F32), (128, latent)).astype(BF16))
    radial_back_ref[...] = radial16
    into = jnp.concatenate([embed_ref[1] * half, embed_ref[0] * half, radial16], axis=0)
    into_ref[...] = mm_nt(eye, into).astype(BF16)


def list_pairs(live_ref, count_ref, slots_t, neigh_ref, centre_ref, total_ref):
    atom_n = count_ref.shape[1]
    slot_n = slots_t.shape[0]
    blocks, lanes = neigh_ref.shape
    atom_row = lax.broadcasted_iota(jnp.int32, (1, atom_n), 1)
    used = jnp.where(atom_row < live_ref[0], count_ref[...], 0).astype(F32)
    row_i = lax.broadcasted_iota(jnp.int32, (atom_n, atom_n), 0)
    col_i = lax.broadcasted_iota(jnp.int32, (atom_n, atom_n), 1)
    end = jnp.sum(jnp.where(col_i <= row_i, used, 0.0), axis=1, keepdims=True)
    own = jnp.sum(jnp.where(col_i == row_i, used, 0.0), axis=1, keepdims=True)
    total = jnp.sum(used)
    total_ref[0] = total.astype(jnp.int32)
    lane = lax.broadcasted_iota(jnp.int32, (1, lanes), 1)

    def one_block(block, carry):
        place = (lane + block * lanes).astype(F32)
        past = end <= place
        centre = jnp.sum(jnp.where(past, 1.0, 0.0), axis=0, keepdims=True)
        start = jnp.sum(jnp.where(past, own, 0.0), axis=0, keepdims=True)
        slot = (place - start).astype(jnp.int32)
        centre_id = centre.astype(jnp.int32)
        rows = mm(slots_t, one_hot(centre_id, atom_n))
        slot_ids = lax.broadcasted_iota(jnp.int32, (slot_n, lanes), 0)
        neigh = jnp.sum(jnp.where(slot_ids == slot, rows, 0.0), axis=0, keepdims=True)
        valid = place < total
        neigh_ref[pl.ds(block, 1), :] = jnp.where(valid, neigh.astype(jnp.int32), -1)
        centre_ref[pl.ds(block, 1), :] = jnp.where(valid, centre_id, -1)
        return carry

    lax.fori_loop(0, blocks, one_block, 0)


def prepare(live_atoms, neighbour_count, neighbours, radial_weight, species_embed, env_weight, latent_weight, readout):
    atom_n, slot_n = neighbours.shape
    latent, features = env_weight.shape[1:]
    blocks = pl.cdiv(atom_n * slot_n, LANES)
    shapes = (
        ((blocks, LANES), jnp.int32),
        ((blocks, LANES), jnp.int32),
        ((1,), jnp.int32),
        ((latent, 2 * SPECIES + BASIS_PAD), BF16),
        ((latent + features + BASIS_PAD, latent), BF16),
        ((latent, features), BF16),
        ((latent + features, latent), BF16),
        ((latent, features + BASIS_PAD), BF16),
        ((latent, 128), F32),
        ((BASIS_PAD, latent), BF16),
    )
    small = [radial_weight, species_embed, readout[None, :]]
    large = [neighbour_count.reshape(1, atom_n), neighbours, env_weight[0].T, latent_weight[0]]
    out = pl.pallas_call(
        prepare_kernel,
        out_shape=[jax.ShapeDtypeStruct(*shape) for shape in shapes],
        in_specs=[SMEM] + [VMEM] * len(small) + [pl.BlockSpec(memory_space=pl.ANY)] * len(large),
        out_specs=[VMEM, VMEM, SMEM] + [VMEM] * 7,
        scratch_shapes=fetch_scratch(large),
        compiler_params=pltpu.CompilerParams(vmem_limit_bytes=48 * 2**20),
        cost_estimate=pl.CostEstimate(flops=2 * 10**9, bytes_accessed=4 * 2**20, transcendentals=0),
        name="prepare",
    )(live_atoms, *small, *large)
    return out[:3], out[3:]


def silu_pair(half_in):
    bent = jnp.tanh(half_in)
    part = half_in * bent
    return half_in + part, (1.0 + bent) * (1.0 + (half_in - part))


def force_kernel(
    place_ref,
    total_ref,
    around_ref,
    neigh_ref,
    centre_ref,
    moved_ref,
    own_kind_ref,
    into_ref,
    on_hidden_ref,
    on_inner_ref,
    on_bent_ref,
    on_weight_ref,
    readout_ref,
    radial_back_ref,
    in_ref,
    *refs,
    second_call,
    out_ghost_n,
):
    *refs, hot_s, use_s, u_s, slope_s, raw_s, part_s, ain_s, energy_s, c_s, dc_s, f_s = refs
    blocks, lanes = neigh_ref.shape
    atom_n = moved_ref.shape[1]
    ghost_n = out_ghost_n
    ext_n = atom_n + ghost_n * len(DIRECTIONS)
    own_kind = own_kind_ref[...]
    from_owners = [in_ref[place_ref[k]] for k in range(len(DIRECTIONS))]
    ghosts = jnp.concatenate([owner[:, :ghost_n] for owner in from_owners], axis=1)
    ghost_kind = ghosts[3:4].astype(jnp.int32)
    if second_call:
        half_ref, send_ref, all_ref, half_two_ref, end_ref, own_out_ref, out_ref = refs
        on_ghosts = []
        for k in range(len(DIRECTIONS)):
            sends = from_owners[k][:, ghost_n : 2 * ghost_n].astype(jnp.int32)
            whole = domain_force(all_ref, place_ref[k], around_ref, k * 8, sends, atom_n)
            picked = mm(split3(padded_rows(whole, 8)), one_hot(sends[k : k + 1], atom_n))
            on_ghosts.append(sum_parts(picked)[0:3])
        _, ghost_pos = step_on(
            ghosts[0:3], ghosts[4:7], ghost_kind, jnp.concatenate(on_ghosts, axis=1)
        )
        here = len(DIRECTIONS)
        whole = domain_force(all_ref, place_ref[here], around_ref, here * 8, send_ref[...], atom_n)
        half_two, own_pos = step_on(moved_ref[...], half_ref[...], own_kind, whole)
        half_two_ref[...] = half_two
        end_ref[...] = own_pos
    else:
        (out_ref,) = refs
        own_pos, ghost_pos = moved_ref[...], ghosts[0:3]
    kind = jnp.concatenate([own_kind, ghost_kind], axis=1)
    pos = jnp.concatenate([own_pos, ghost_pos], axis=1)
    basis_n = SPECIES
    latent, features = on_inner_ref.shape
    count = (total_ref[0] + lanes - 1) // lanes
    scale = COUPLING * SLOTS ** (-0.5)

    pos8 = padded_rows(pos, 8) * (1.0 / RADIUS)
    pos_parts = split3(jnp.concatenate([pos8, -pos8[:, :atom_n]], axis=1))
    row8 = lax.broadcasted_iota(jnp.int32, (SPECIES, ext_n), 0)
    kinds = jnp.where(row8 == kind, 1.0, 0.0)
    basis_in = identity(BASIS_PAD).astype(F32)
    selected = jnp.concatenate(
        [
            jnp.concatenate([kinds, jnp.zeros((SPECIES + BASIS_PAD, ext_n), F32)], axis=0),
            jnp.concatenate(
                [jnp.zeros((SPECIES, atom_n), F32), kinds[:, :atom_n], jnp.zeros((BASIS_PAD, atom_n), F32)], axis=0
            ),
            jnp.concatenate([jnp.zeros((2 * SPECIES, BASIS_PAD), F32), basis_in], axis=0),
        ],
        axis=1,
    )
    weight_in = mm(into_ref[...], selected.astype(BF16)).astype(BF16)

    mid_row = lax.broadcasted_iota(jnp.int32, (BASIS_PAD, lanes), 0).astype(F32)
    mids = (mid_row + 0.5) / basis_n
    sharp = 2.0 * basis_n * basis_n

    c_s[...] = jnp.zeros_like(c_s)
    dc_s[...] = jnp.zeros_like(dc_s)
    f_s[...] = jnp.zeros_like(f_s)

    def geometry(block):
        vec = u_s[block]
        square = jnp.sum(vec * vec, axis=0, keepdims=True)
        inside = jnp.maximum(1.0 - square, 0.0)
        inside = jnp.where(centre_ref[pl.ds(block, 1), :] >= 0, inside, 0.0)
        apart = square - mids
        return vec, inside, apart, jnp.exp(-sharp * apart * apart)

    def first(block, carry):
        hot_j = one_hot(neigh_ref[pl.ds(block, 1), :], ext_n)
        hot_c = one_hot(centre_ref[pl.ds(block, 1), :], atom_n)
        hot = jnp.concatenate([hot_j, hot_c], axis=0)
        hot_s[block] = hot
        u_s[block] = sum_parts(mm(pos_parts, hot))
        vec, inside, _, basis = geometry(block)
        use = jnp.concatenate([hot_c * vec[k : k + 1].astype(BF16) for k in range(3)], axis=0)
        use_s[block] = use
        pre = mm(weight_in, jnp.concatenate([hot, basis.astype(BF16)], axis=0))
        hidden, slope = silu_pair(pre)
        slope_s[block] = slope.astype(BF16)
        taken = mm(on_hidden_ref[...], hidden.astype(BF16))
        part_s[block] = taken[:latent]
        raw = taken[latent : latent + features]
        raw_s[block] = raw
        energy_s[block] = taken[latent + features : latent + features + 8]
        c_s[...] += mm_nt((raw * (inside * inside)).astype(BF16), use)
        return carry

    lax.fori_loop(0, count, first, 0)
    c_all = c_s[...] * scale
    c_b = c_all.astype(BF16)

    def second(block, carry):
        _, inside, _, _ = geometry(block)
        use = use_s[block]
        env = inside * inside
        weight = raw_s[block] * env
        inner = weight * mm(c_b, use)
        later = part_s[block] + mm(on_inner_ref[...], inner.astype(BF16))
        gain, bent = silu_pair(later)
        readout = jnp.concatenate([readout_ref[...]] * (lanes // 128), axis=1)
        energy_s[block] += jnp.sum(gain * readout, axis=0, keepdims=True)
        taken = mm(on_bent_ref[...], bent.astype(BF16))
        part_s[block] = taken[:latent]
        a_in = taken[latent:] * env
        ain_s[block] = a_in
        dc_s[...] += mm_nt((a_in * weight).astype(BF16), use)
        return carry

    lax.fori_loop(0, count, second, 0)
    c_dc = jnp.concatenate([c_all, dc_s[...] * scale], axis=0).astype(BF16)
    both = jnp.concatenate([c_all.T, dc_s[...].T * scale], axis=1).astype(BF16)

    def third(block, carry):
        vec, inside, apart, basis = geometry(block)
        use = use_s[block]
        hot = hot_s[block]
        env = inside * inside
        raw = raw_s[block]
        weight = raw * env
        a_in = ain_s[block]
        along = mm(c_dc, use)
        d_weight = a_in * along[:features] + along[features:]
        d_env = jnp.sum(d_weight * raw, axis=0, keepdims=True) + energy_s[block][0:1]
        ones = jnp.ones((BASIS_PAD, lanes), BF16)
        d_hidden = part_s[block] + mm(
            on_weight_ref[...], jnp.concatenate([d_weight.astype(BF16), ones], axis=0)
        )
        d_pre = (d_hidden * slope_s[block].astype(F32)).astype(BF16)
        d_basis = mm(radial_back_ref[...], d_pre)
        d_square = env * jnp.sum(d_basis * basis * apart, axis=0, keepdims=True) * (-2.0 * sharp)
        d_square = d_square - 2.0 * inside * d_env
        d_all = mm(both, jnp.concatenate([a_in * weight, weight], axis=0).astype(BF16))
        hot_c = hot[ext_n:].astype(F32)
        picked = [
            jnp.sum(d_all[k * atom_n : (k + 1) * atom_n] * hot_c, axis=0, keepdims=True)
            for k in range(3)
        ]
        d_vec = jnp.concatenate(picked + [jnp.zeros((5, lanes), F32)], axis=0)
        d_vec = (d_vec + 2.0 * d_square * vec) * (1.0 / RADIUS)
        f_s[...] += mm_nt(split3(d_vec), hot)
        return carry

    lax.fori_loop(0, count, third, 0)
    summed = f_s[0:8] + f_s[8:16] + f_s[16:24]
    on_centre = summed[0:3, ext_n:]
    on_neigh = summed[0:3, :ext_n]
    own = on_centre - on_neigh[:, :atom_n]
    if second_call:
        own_out_ref[...] = own
        put(out_ref, place_ref, -on_neigh[:, atom_n:])
    else:
        ghost_all = ext_n - atom_n
        upper = jnp.concatenate([-on_neigh[:, atom_n:], jnp.zeros((3, TILE[1] - ghost_all), F32)], axis=1)
        lower = jnp.concatenate([own, jnp.zeros((3, TILE[1] - atom_n), F32)], axis=1)
        tile = jnp.concatenate([upper, lower, jnp.zeros((TILE[0] - 6, TILE[1]), F32)], axis=0)
        out_ref[...] = jnp.broadcast_to(tile[None], out_ref.shape)


def pair_forces(places, pairs, own_pos, own_kind, weights, incoming, ghost_n, second=()):
    place, around = places
    neigh, centre, total = pairs
    blocks, lanes = neigh.shape
    latent, features = weights[2].shape
    atom_n = own_pos.shape[1]
    devices = incoming.shape[0]
    ext_n = atom_n + ghost_n * len(DIRECTIONS)
    operands = [place, total, around, neigh, centre, own_pos, own_kind, *weights, incoming, *second]
    if second:
        out_shape = [jax.ShapeDtypeStruct((3, atom_n), F32)] * 3
        out_shape.append(jax.ShapeDtypeStruct((devices, 3, ghost_n), F32))
    else:
        out_shape = [jax.ShapeDtypeStruct((devices, *TILE), F32)]
    pair_rows = blocks * lanes
    return pl.pallas_call(
        functools.partial(force_kernel, second_call=bool(second), out_ghost_n=ghost_n),
        out_shape=out_shape,
        in_specs=[SMEM] * 3 + [VMEM] * (len(operands) - 3),
        out_specs=[VMEM] * len(out_shape),
        scratch_shapes=[
            pltpu.VMEM((blocks, ext_n + atom_n, lanes), BF16),
            pltpu.VMEM((blocks, 3 * atom_n, lanes), BF16),
            pltpu.VMEM((blocks, 8, lanes), F32),
            pltpu.VMEM((blocks, latent, lanes), BF16),
            pltpu.VMEM((blocks, features, lanes), F32),
            pltpu.VMEM((blocks, latent, lanes), F32),
            pltpu.VMEM((blocks, features, lanes), F32),
            pltpu.VMEM((blocks, 8, lanes), F32),
            pltpu.VMEM((features, 3 * atom_n), F32),
            pltpu.VMEM((features, 3 * atom_n), F32),
            pltpu.VMEM((24, ext_n + atom_n), F32),
        ],
        compiler_params=pltpu.CompilerParams(vmem_limit_bytes=48 * 2**20),
        cost_estimate=pl.CostEstimate(
            flops=pair_rows * latent * 2700, bytes_accessed=4 * 2**20, transcendentals=0
        ),
        name="pair_forces",
    )(*operands)


def fetch_scratch(operands):
    return [pltpu.VMEM(operand.shape, operand.dtype) for operand in operands] + [
        pltpu.SemaphoreType.DMA((len(operands),))
    ]


def small_call(kernel, name, smem_n, operands, out_shape, fetched=False):
    others = operands[smem_n:]
    place = pl.BlockSpec(memory_space=pl.ANY) if fetched else VMEM
    return pl.pallas_call(
        kernel,
        out_shape=out_shape,
        in_specs=[SMEM] * smem_n + [place] * len(others),
        out_specs=[VMEM] * len(out_shape),
        scratch_shapes=fetch_scratch(others) if fetched else [],
        compiler_params=pltpu.CompilerParams(vmem_limit_bytes=48 * 2**20),
        name=name,
    )(*operands)


def devices_at(shift_gx, shift_yz):
    gx_n, yz_n = lax.axis_size("gx"), lax.axis_size("yz")
    gx = (lax.axis_index("gx") + jnp.asarray(shift_gx, jnp.int32) + gx_n) % gx_n
    yz = (lax.axis_index("yz") + jnp.asarray(shift_yz, jnp.int32) + yz_n) % yz_n
    return gx * yz_n + yz


def exchange(blocks):
    return lax.all_to_all(blocks, ("gx", "yz"), 0, 0, tiled=True)


def body(
    positions,
    velocities,
    forces_start,
    species,
    live_atoms,
    send_list,
    neighbours,
    neighbour_count,
    radial_weight,
    species_embed,
    env_weight,
    latent_weight,
    readout,
):
    atom_n = positions.shape[1]
    ghost_n = send_list.shape[1]
    devices = lax.axis_size("gx") * lax.axis_size("yz")
    ahead = devices_at([a for a, _ in DIRECTIONS], [b for _, b in DIRECTIONS])
    sources = [(-a, -b) for a, b in DIRECTIONS] + [(0, 0)]
    behind = devices_at([a for a, _ in sources], [b for _, b in sources])
    around = devices_at(
        [a + c for a, _ in sources for c, _ in DIRECTIONS], [b + d for _, b in sources for _, d in DIRECTIONS]
    )
    kinds = species.reshape(1, atom_n)
    atoms = jax.ShapeDtypeStruct((3, atom_n), F32)

    moved, half, sent = small_call(
        start_kernel,
        "start",
        1,
        [ahead, positions, velocities, forces_start, kinds, send_list],
        [atoms, atoms, jax.ShapeDtypeStruct((devices, *TILE), F32)],
        fetched=True,
    )
    got = exchange(sent)
    pairs, weights = prepare(
        live_atoms, neighbour_count, neighbours, radial_weight, species_embed, env_weight, latent_weight, readout
    )
    places = (behind, around)
    (sent,) = pair_forces(places, pairs, moved, kinds, weights, got, ghost_n)
    every = exchange(sent)
    half_two, positions_end, own, sent = pair_forces(
        places, pairs, moved, kinds, weights, got, ghost_n, (half, send_list, every)
    )
    back = exchange(sent)
    velocities_end, forces_end = small_call(
        last_kernel, "last", 1, [ahead, own, send_list, half_two, kinds, back], [atoms, atoms]
    )
    return (positions_end, velocities_end, forces_end)


def solution(mesh):
    placed = (
        P(None, ("gx", "yz")),
        P(None, ("gx", "yz")),
        P(None, ("gx", "yz")),
        P(("gx", "yz")),
        P(("gx", "yz")),
        P(None, ("gx", "yz")),
        P(("gx", "yz"), None),
        P(("gx", "yz")),
        P(),
        P(),
        P(),
        P(),
        P(),
    )
    return jax.shard_map(
        body,
        mesh=mesh,
        in_specs=placed,
        out_specs=(P(None, ("gx", "yz")), P(None, ("gx", "yz")), P(None, ("gx", "yz"))),
        check_vma=False,
    )
```

```python
import functools

import jax
import jax.numpy as jnp
from jax import lax
from jax.experimental import pallas as pl
from jax.experimental.pallas import tpu as pltpu
from jax.sharding import PartitionSpec as P

SPECIES = 8
SLOTS = 128
RADIUS = 6.0
STEP = 0.25
COUPLING = 4.0
MASSES = (1.008, 12.011, 14.007, 15.999, 32.06, 22.99, 35.45, 30.97)

LANES = 1024
DIRECTIONS = ((-1, -1), (-1, 0), (-1, 1), (0, -1), (0, 1), (1, -1), (1, 0), (1, 1))
TILE = (4, 128)
BASIS_PAD = 16

F32 = jnp.float32
BF16 = jnp.bfloat16


def mm(left, right):
    return jnp.dot(left, right, preferred_element_type=F32)


def mm_nt(left, right):
    return lax.dot_general(left, right, (((1,), (1,)), ((), ())), preferred_element_type=F32)


def split3(values):
    high = values.astype(BF16)
    rest = values - high.astype(F32)
    mid = rest.astype(BF16)
    low = (rest - mid.astype(F32)).astype(BF16)
    return jnp.concatenate([high.astype(F32), mid.astype(F32), low.astype(F32)], axis=0).astype(BF16)


def one_hot(ids, rows):
    row_ids = lax.broadcasted_iota(jnp.int32, (rows, ids.shape[1]), 0)
    return jnp.where(row_ids == ids, 1.0, 0.0).astype(BF16)


SMEM = pl.BlockSpec(memory_space=pltpu.SMEM)
VMEM = pl.BlockSpec(memory_space=pltpu.VMEM)


def identity(size):
    row = lax.broadcasted_iota(jnp.int32, (size, size), 0)
    col = lax.broadcasted_iota(jnp.int32, (size, size), 1)
    return jnp.where(row == col, 1.0, 0.0).astype(BF16)


def padded_rows(values, rows):
    have, lanes = values.shape
    return jnp.concatenate([values, jnp.zeros((rows - have, lanes), values.dtype)], axis=0)


def sum_parts(parts):
    rows = parts.shape[0] // 3
    return parts[:rows] + parts[rows : 2 * rows] + parts[2 * rows :]


def by_direction(rows):
    return jnp.concatenate([rows[k : k + 1] for k in range(len(DIRECTIONS))], axis=1)


def device_at(shift_gx, shift_yz):
    gx_n, yz_n = lax.axis_size("gx"), lax.axis_size("yz")
    gx = lax.rem(lax.axis_index("gx") + (shift_gx % gx_n), gx_n)
    yz = lax.rem(lax.axis_index("yz") + (shift_yz % yz_n), yz_n)
    return gx * yz_n + yz


def towards(sign):
    return [device_at(sign * a, sign * b) for a, b in DIRECTIONS]


def put(out_ref, blocks):
    places = towards(-1)
    ghost_n = blocks.shape[1] // len(DIRECTIONS)
    out_ref[...] = jnp.zeros_like(out_ref)
    for k in range(len(DIRECTIONS)):
        out_ref[places[k]] = blocks[:, k * ghost_n : (k + 1) * ghost_n]


def take(in_ref):
    return jnp.concatenate([in_ref[place] for place in towards(1)], axis=1)


def inverse_mass(species):
    inverse = jnp.zeros(species.shape, F32)
    for spec_id, mass in enumerate(MASSES):
        inverse = jnp.where(species == spec_id, F32(1.0 / mass), inverse)
    return inverse


def start_kernel(pos_ref, vel_ref, force_ref, species_ref, send_ref, moved_ref, half_ref, out_ref):
    species = species_ref[...]
    half = vel_ref[...] + 0.5 * STEP * inverse_mass(species) * force_ref[...]
    moved = pos_ref[...] + STEP * half
    half_ref[...] = half
    moved_ref[...] = moved
    spare = jnp.zeros((1, species.shape[1]), F32)
    sources = split3(jnp.concatenate([moved, species.astype(F32), half, spare], axis=0))
    sends = send_ref[...]
    picked = sum_parts(mm(sources, one_hot(by_direction(sends), species.shape[1])))
    sent = sends.astype(F32)
    ghost_n = sent.shape[1]
    rest = jnp.zeros((TILE[0], TILE[1] - 4 * ghost_n), F32)
    out_ref[...] = jnp.zeros_like(out_ref)
    for k, place in enumerate(towards(1)):
        block = picked[:, k * ghost_n : (k + 1) * ghost_n]
        out_ref[place] = jnp.concatenate([block[:4], block[4:], sent[:4], sent[4:], rest], axis=1)


def total_force(own, back, sends):
    pick = one_hot(by_direction(sends), own.shape[1])
    return own + sum_parts(mm_nt(split3(padded_rows(back, 8)), pick))[0:3]


def forces_tile(own, on_ghosts):
    room = TILE[1] - on_ghosts.shape[1]
    upper = jnp.concatenate([on_ghosts, own[:, :room]], axis=1)
    last = [own[c : c + 1, room:] for c in range(3)]
    last.append(jnp.zeros((1, TILE[1] - 3 * (own.shape[1] - room)), F32))
    return jnp.concatenate([upper, jnp.concatenate(last, axis=1)], axis=0)


def domain_force(all_ref, shift_gx, shift_yz, sends, atom_n):
    ghost_n = sends.shape[1]
    back = []
    for k, (a, b) in enumerate(DIRECTIONS):
        place = device_at(shift_gx + a, shift_yz + b)
        back.append(all_ref[place][0:3, k * ghost_n : (k + 1) * ghost_n])
    tile = all_ref[device_at(shift_gx, shift_yz)]
    room = TILE[1] - len(DIRECTIONS) * ghost_n
    over = atom_n - room
    last = jnp.concatenate([tile[3:4, c * over : (c + 1) * over] for c in range(3)], axis=0)
    own = jnp.concatenate([tile[0:3, TILE[1] - room :], last], axis=1)
    return total_force(own, jnp.concatenate(back, axis=1), sends)


def step_on(moved, half, kinds, forces):
    kick = 0.5 * STEP * inverse_mass(kinds) * forces
    half_two = half + kick + kick
    return half_two, moved + STEP * half_two


def last_kernel(own_ref, send_ref, half_two_ref, species_ref, in_ref, vel_ref, force_ref):
    forces = total_force(own_ref[...], take(in_ref), send_ref[...])
    force_ref[...] = forces
    vel_ref[...] = half_two_ref[...] + 0.5 * STEP * inverse_mass(species_ref[...]) * forces


def prepare_kernel(
    live_ref,
    radial_ref,
    embed_ref,
    readout_ref,
    count_ref,
    slots_ref,
    env_t_ref,
    latent_ref,
    neigh_ref,
    centre_ref,
    total_ref,
    into_ref,
    on_hidden_ref,
    on_inner_ref,
    on_bent_ref,
    on_weight_ref,
    readout_t_ref,
    radial_back_ref,
):
    features, latent = env_t_ref.shape
    slots_t = mm_nt(identity(slots_ref.shape[1]), slots_ref[...].astype(F32).astype(BF16)).astype(BF16)
    list_pairs(live_ref, count_ref, slots_t, neigh_ref, centre_ref, total_ref)
    eye = identity(latent)
    half = BF16(0.5)
    latent_w = latent_ref[...]
    readout = readout_ref[...]
    none = jnp.zeros((BASIS_PAD - 8, latent), BF16)
    readout16 = padded_rows(readout.astype(F32), BASIS_PAD).astype(BF16)
    radial16 = jnp.concatenate([radial_ref[...] * half, none], axis=0)
    latent_t = mm_nt(eye, latent_w * half).astype(BF16)
    on_hidden_ref[...] = jnp.concatenate([latent_t[:, :latent], env_t_ref[...], readout16], axis=0)
    on_inner_ref[...] = latent_t[:, latent:]
    on_bent_ref[...] = (latent_w.astype(F32) * (0.5 * readout.astype(F32))).astype(BF16)
    on_weight_ref[...] = mm_nt(eye, jnp.concatenate([env_t_ref[...], readout16], axis=0)).astype(BF16)
    readout_t_ref[...] = mm_nt(eye, jnp.broadcast_to(readout.astype(F32), (128, latent)).astype(BF16))
    radial_back_ref[...] = radial16
    into = jnp.concatenate([embed_ref[1] * half, embed_ref[0] * half, radial16], axis=0)
    into_ref[...] = mm_nt(eye, into).astype(BF16)


def list_pairs(live_ref, count_ref, slots_t, neigh_ref, centre_ref, total_ref):
    atom_n = count_ref.shape[1]
    slot_n = slots_t.shape[0]
    blocks, lanes = neigh_ref.shape
    atom_row = lax.broadcasted_iota(jnp.int32, (1, atom_n), 1)
    used = jnp.where(atom_row < live_ref[...], count_ref[...], 0).astype(F32)
    row_i = lax.broadcasted_iota(jnp.int32, (atom_n, atom_n), 0)
    col_i = lax.broadcasted_iota(jnp.int32, (atom_n, atom_n), 1)
    end = jnp.sum(jnp.where(col_i <= row_i, used, 0.0), axis=1, keepdims=True)
    own = jnp.sum(jnp.where(col_i == row_i, used, 0.0), axis=1, keepdims=True)
    total = jnp.sum(used)
    total_ref[0] = total.astype(jnp.int32)
    lane = lax.broadcasted_iota(jnp.int32, (1, lanes), 1)

    def one_block(block, carry):
        place = (lane + block * lanes).astype(F32)
        past = end <= place
        centre = jnp.sum(jnp.where(past, 1.0, 0.0), axis=0, keepdims=True)
        start = jnp.sum(jnp.where(past, own, 0.0), axis=0, keepdims=True)
        slot = (place - start).astype(jnp.int32)
        centre_id = centre.astype(jnp.int32)
        rows = mm(slots_t, one_hot(centre_id, atom_n))
        slot_ids = lax.broadcasted_iota(jnp.int32, (slot_n, lanes), 0)
        neigh = jnp.sum(jnp.where(slot_ids == slot, rows, 0.0), axis=0, keepdims=True)
        valid = place < total
        neigh_ref[pl.ds(block, 1), :] = jnp.where(valid, neigh.astype(jnp.int32), -1)
        centre_ref[pl.ds(block, 1), :] = jnp.where(valid, centre_id, -1)
        return carry

    lax.fori_loop(0, blocks, one_block, 0)


def prepare(live_atoms, neighbour_count, neighbours, radial_weight, species_embed, env_weight, latent_weight, readout):
    atom_n, slot_n = neighbours.shape
    latent, features = env_weight.shape[1:]
    blocks = pl.cdiv(atom_n * slot_n, LANES)
    shapes = (
        ((blocks, LANES), jnp.int32),
        ((blocks, LANES), jnp.int32),
        ((1,), jnp.int32),
        ((latent, 2 * SPECIES + BASIS_PAD), BF16),
        ((latent + features + BASIS_PAD, latent), BF16),
        ((latent, features), BF16),
        ((latent + features, latent), BF16),
        ((latent, features + BASIS_PAD), BF16),
        ((latent, 128), F32),
        ((BASIS_PAD, latent), BF16),
    )
    operands = [
        live_atoms.reshape(1, 1),
        radial_weight,
        species_embed,
        readout[None, :],
        neighbour_count.reshape(1, atom_n),
        neighbours,
        env_weight[0].T,
        latent_weight[0],
    ]
    out = pl.pallas_call(
        prepare_kernel,
        out_shape=[jax.ShapeDtypeStruct(*shape) for shape in shapes],
        in_specs=[VMEM] * len(operands),
        out_specs=[VMEM, VMEM, SMEM] + [VMEM] * 7,
        compiler_params=pltpu.CompilerParams(vmem_limit_bytes=24 * 2**20),
        cost_estimate=pl.CostEstimate(flops=2 * 10**9, bytes_accessed=4 * 2**20, transcendentals=0),
        name="prepare",
    )(*operands)
    return out[:3], out[3:]


def silu_pair(half_in):
    bent = jnp.tanh(half_in)
    part = half_in * bent
    return half_in + part, (1.0 + bent) * (1.0 + (half_in - part))


def force_kernel(
    total_ref,
    neigh_ref,
    centre_ref,
    moved_ref,
    own_kind_ref,
    into_ref,
    on_hidden_ref,
    on_inner_ref,
    on_bent_ref,
    on_weight_ref,
    readout_ref,
    radial_back_ref,
    in_ref,
    *refs,
    second_call,
    out_ghost_n,
):
    *refs, hot_s, use_s, u_s, slope_s, raw_s, part_s, ain_s, energy_s, c_s, dc_s, f_s = refs
    blocks, lanes = neigh_ref.shape
    atom_n = moved_ref.shape[1]
    ghost_n = out_ghost_n
    ext_n = atom_n + ghost_n * len(DIRECTIONS)
    own_kind = own_kind_ref[...]
    from_owners = [in_ref[place] for place in towards(-1)]
    ghosts = jnp.concatenate(
        [
            jnp.concatenate([owner[:, n * ghost_n : (n + 1) * ghost_n] for owner in from_owners], axis=1)
            for n in range(2)
        ],
        axis=0,
    )
    ghost_kind = ghosts[3:4].astype(jnp.int32)
    if second_call:
        half_ref, send_ref, all_ref, half_two_ref, end_ref, own_out_ref, out_ref = refs
        on_ghosts = []
        for k, (a, b) in enumerate(DIRECTIONS):
            sends = jnp.concatenate(
                [from_owners[k][:, n * ghost_n : (n + 1) * ghost_n] for n in (2, 3)], axis=0
            ).astype(jnp.int32)
            whole = domain_force(all_ref, -a, -b, sends, atom_n)
            picked = mm(split3(padded_rows(whole, 8)), one_hot(sends[k : k + 1], atom_n))
            on_ghosts.append(sum_parts(picked)[0:3])
        _, ghost_pos = step_on(
            ghosts[0:3], ghosts[4:7], ghost_kind, jnp.concatenate(on_ghosts, axis=1)
        )
        whole = domain_force(all_ref, 0, 0, send_ref[...], atom_n)
        half_two, own_pos = step_on(moved_ref[...], half_ref[...], own_kind, whole)
        half_two_ref[...] = half_two
        end_ref[...] = own_pos
    else:
        (out_ref,) = refs
        own_pos, ghost_pos = moved_ref[...], ghosts[0:3]
    kind = jnp.concatenate([own_kind, ghost_kind], axis=1)
    pos = jnp.concatenate([own_pos, ghost_pos], axis=1)
    basis_n = SPECIES
    latent, features = on_inner_ref.shape
    count = (total_ref[0] + lanes - 1) // lanes
    scale = COUPLING * SLOTS ** (-0.5)

    pos8 = padded_rows(pos, 8) * (1.0 / RADIUS)
    pos_parts = split3(jnp.concatenate([pos8, -pos8[:, :atom_n]], axis=1))
    row8 = lax.broadcasted_iota(jnp.int32, (SPECIES, ext_n), 0)
    kinds = jnp.where(row8 == kind, 1.0, 0.0)
    basis_in = identity(BASIS_PAD).astype(F32)
    selected = jnp.concatenate(
        [
            jnp.concatenate([kinds, jnp.zeros((SPECIES + BASIS_PAD, ext_n), F32)], axis=0),
            jnp.concatenate(
                [jnp.zeros((SPECIES, atom_n), F32), kinds[:, :atom_n], jnp.zeros((BASIS_PAD, atom_n), F32)], axis=0
            ),
            jnp.concatenate([jnp.zeros((2 * SPECIES, BASIS_PAD), F32), basis_in], axis=0),
        ],
        axis=1,
    )
    weight_in = mm(into_ref[...], selected.astype(BF16)).astype(BF16)

    mid_row = lax.broadcasted_iota(jnp.int32, (BASIS_PAD, lanes), 0).astype(F32)
    mids = (mid_row + 0.5) / basis_n
    sharp = 2.0 * basis_n * basis_n

    c_s[...] = jnp.zeros_like(c_s)
    dc_s[...] = jnp.zeros_like(dc_s)
    f_s[...] = jnp.zeros_like(f_s)

    def geometry(block):
        vec = u_s[block]
        square = jnp.sum(vec * vec, axis=0, keepdims=True)
        inside = jnp.maximum(1.0 - square, 0.0)
        inside = jnp.where(centre_ref[pl.ds(block, 1), :] >= 0, inside, 0.0)
        apart = square - mids
        return vec, inside, apart, jnp.exp(-sharp * apart * apart)

    def first(block, carry):
        hot_j = one_hot(neigh_ref[pl.ds(block, 1), :], ext_n)
        hot_c = one_hot(centre_ref[pl.ds(block, 1), :], atom_n)
        hot = jnp.concatenate([hot_j, hot_c], axis=0)
        hot_s[block] = hot
        u_s[block] = sum_parts(mm(pos_parts, hot))
        vec, inside, _, basis = geometry(block)
        use = jnp.concatenate([hot_c * vec[k : k + 1].astype(BF16) for k in range(3)], axis=0)
        use_s[block] = use
        pre = mm(weight_in, jnp.concatenate([hot, basis.astype(BF16)], axis=0))
        hidden, slope = silu_pair(pre)
        slope_s[block] = slope.astype(BF16)
        taken = mm(on_hidden_ref[...], hidden.astype(BF16))
        part_s[block] = taken[:latent]
        raw = taken[latent : latent + features]
        raw_s[block] = raw
        energy_s[block] = taken[latent + features : latent + features + 8]
        c_s[...] += mm_nt((raw * (inside * inside)).astype(BF16), use)
        return carry

    lax.fori_loop(0, count, first, 0)
    c_all = c_s[...] * scale
    c_b = c_all.astype(BF16)

    def second(block, carry):
        _, inside, _, _ = geometry(block)
        use = use_s[block]
        env = inside * inside
        weight = raw_s[block] * env
        inner = weight * mm(c_b, use)
        later = part_s[block] + mm(on_inner_ref[...], inner.astype(BF16))
        gain, bent = silu_pair(later)
        readout = jnp.concatenate([readout_ref[...]] * (lanes // 128), axis=1)
        energy_s[block] += jnp.sum(gain * readout, axis=0, keepdims=True)
        taken = mm(on_bent_ref[...], bent.astype(BF16))
        part_s[block] = taken[:latent]
        a_in = taken[latent:] * env
        ain_s[block] = a_in
        dc_s[...] += mm_nt((a_in * weight).astype(BF16), use)
        return carry

    lax.fori_loop(0, count, second, 0)
    c_dc = jnp.concatenate([c_all, dc_s[...] * scale], axis=0).astype(BF16)
    both = jnp.concatenate([c_all.T, dc_s[...].T * scale], axis=1).astype(BF16)

    def third(block, carry):
        vec, inside, apart, basis = geometry(block)
        use = use_s[block]
        hot = hot_s[block]
        env = inside * inside
        raw = raw_s[block]
        weight = raw * env
        a_in = ain_s[block]
        along = mm(c_dc, use)
        d_weight = a_in * along[:features] + along[features:]
        d_env = jnp.sum(d_weight * raw, axis=0, keepdims=True) + energy_s[block][0:1]
        ones = jnp.ones((BASIS_PAD, lanes), BF16)
        d_hidden = part_s[block] + mm(
            on_weight_ref[...], jnp.concatenate([d_weight.astype(BF16), ones], axis=0)
        )
        d_pre = (d_hidden * slope_s[block].astype(F32)).astype(BF16)
        d_basis = mm(radial_back_ref[...], d_pre)
        d_square = env * jnp.sum(d_basis * basis * apart, axis=0, keepdims=True) * (-2.0 * sharp)
        d_square = d_square - 2.0 * inside * d_env
        d_all = mm(both, jnp.concatenate([a_in * weight, weight], axis=0).astype(BF16))
        hot_c = hot[ext_n:].astype(F32)
        picked = [
            jnp.sum(d_all[k * atom_n : (k + 1) * atom_n] * hot_c, axis=0, keepdims=True)
            for k in range(3)
        ]
        d_vec = jnp.concatenate(picked + [jnp.zeros((5, lanes), F32)], axis=0)
        d_vec = (d_vec + 2.0 * d_square * vec) * (1.0 / RADIUS)
        f_s[...] += mm_nt(split3(d_vec), hot)
        return carry

    lax.fori_loop(0, count, third, 0)
    summed = f_s[0:8] + f_s[8:16] + f_s[16:24]
    on_centre = summed[0:3, ext_n:]
    on_neigh = summed[0:3, :ext_n]
    own = on_centre - on_neigh[:, :atom_n]
    if second_call:
        own_out_ref[...] = own
        put(out_ref, -on_neigh[:, atom_n:])
    else:
        tile = forces_tile(own, -on_neigh[:, atom_n:])
        out_ref[...] = jnp.broadcast_to(tile[None], out_ref.shape)


def pair_forces(pairs, own_pos, own_kind, weights, incoming, ghost_n, second=()):
    neigh, centre, total = pairs
    blocks, lanes = neigh.shape
    latent, features = weights[2].shape
    atom_n = own_pos.shape[1]
    devices = incoming.shape[0]
    ext_n = atom_n + ghost_n * len(DIRECTIONS)
    operands = [total, neigh, centre, own_pos, own_kind, *weights, incoming, *second]
    if second:
        out_shape = [jax.ShapeDtypeStruct((3, atom_n), F32)] * 3
        out_shape.append(jax.ShapeDtypeStruct((devices, 3, ghost_n), F32))
    else:
        out_shape = [jax.ShapeDtypeStruct((devices, *TILE), F32)]
    pair_rows = blocks * lanes
    return pl.pallas_call(
        functools.partial(force_kernel, second_call=bool(second), out_ghost_n=ghost_n),
        out_shape=out_shape,
        in_specs=[SMEM] + [VMEM] * (len(operands) - 1),
        out_specs=[VMEM] * len(out_shape),
        scratch_shapes=[
            pltpu.VMEM((blocks, ext_n + atom_n, lanes), BF16),
            pltpu.VMEM((blocks, 3 * atom_n, lanes), BF16),
            pltpu.VMEM((blocks, 8, lanes), F32),
            pltpu.VMEM((blocks, latent, lanes), BF16),
            pltpu.VMEM((blocks, features, lanes), F32),
            pltpu.VMEM((blocks, latent, lanes), F32),
            pltpu.VMEM((blocks, features, lanes), F32),
            pltpu.VMEM((blocks, 8, lanes), F32),
            pltpu.VMEM((features, 3 * atom_n), F32),
            pltpu.VMEM((features, 3 * atom_n), F32),
            pltpu.VMEM((24, ext_n + atom_n), F32),
        ],
        compiler_params=pltpu.CompilerParams(vmem_limit_bytes=48 * 2**20),
        cost_estimate=pl.CostEstimate(
            flops=pair_rows * latent * 2700, bytes_accessed=4 * 2**20, transcendentals=0
        ),
        name="pair_forces",
    )(*operands)


def small_call(kernel, name, operands, out_shape):
    return pl.pallas_call(
        kernel,
        out_shape=out_shape,
        in_specs=[VMEM] * len(operands),
        out_specs=[VMEM] * len(out_shape),
        compiler_params=pltpu.CompilerParams(vmem_limit_bytes=16 * 2**20),
        name=name,
    )(*operands)


def exchange(blocks):
    return lax.all_to_all(blocks, ("gx", "yz"), 0, 0, tiled=True)


def body(
    positions,
    velocities,
    forces_start,
    species,
    live_atoms,
    send_list,
    neighbours,
    neighbour_count,
    radial_weight,
    species_embed,
    env_weight,
    latent_weight,
    readout,
):
    atom_n = positions.shape[1]
    ghost_n = send_list.shape[1]
    devices = lax.axis_size("gx") * lax.axis_size("yz")
    kinds = species.reshape(1, atom_n)
    atoms = jax.ShapeDtypeStruct((3, atom_n), F32)

    moved, half, sent = small_call(
        start_kernel,
        "start",
        [positions, velocities, forces_start, kinds, send_list],
        [atoms, atoms, jax.ShapeDtypeStruct((devices, *TILE), F32)],
    )
    got = exchange(sent)
    pairs, weights = prepare(
        live_atoms, neighbour_count, neighbours, radial_weight, species_embed, env_weight, latent_weight, readout
    )
    (sent,) = pair_forces(pairs, moved, kinds, weights, got, ghost_n)
    every = exchange(sent)
    half_two, positions_end, own, sent = pair_forces(
        pairs, moved, kinds, weights, got, ghost_n, (half, send_list, every)
    )
    back = exchange(sent)
    velocities_end, forces_end = small_call(
        last_kernel, "last", [own, send_list, half_two, kinds, back], [atoms, atoms]
    )
    return (positions_end, velocities_end, forces_end)


def solution(mesh):
    placed = (
        P(None, ("gx", "yz")),
        P(None, ("gx", "yz")),
        P(None, ("gx", "yz")),
        P(("gx", "yz")),
        P(("gx", "yz")),
        P(None, ("gx", "yz")),
        P(("gx", "yz"), None),
        P(("gx", "yz")),
        P(),
        P(),
        P(),
        P(),
        P(),
    )
    return jax.shard_map(
        body,
        mesh=mesh,
        in_specs=placed,
        out_specs=(P(None, ("gx", "yz")), P(None, ("gx", "yz")), P(None, ("gx", "yz"))),
        check_vma=False,
    )
```

```python
import functools

import jax
import jax.numpy as jnp
from jax import lax
from jax.experimental import pallas as pl
from jax.experimental.pallas import tpu as pltpu
from jax.sharding import PartitionSpec as P

SPECIES = 8
SLOTS = 128
RADIUS = 6.0
STEP = 0.25
COUPLING = 4.0
MASSES = (1.008, 12.011, 14.007, 15.999, 32.06, 22.99, 35.45, 30.97)

LANES = 1024
DIRECTIONS = ((-1, -1), (-1, 0), (-1, 1), (0, -1), (0, 1), (1, -1), (1, 0), (1, 1))
TILE = (4, 128)
BASIS_PAD = 16

F32 = jnp.float32
BF16 = jnp.bfloat16


def mm(left, right):
    return jnp.dot(left, right, preferred_element_type=F32)


def mm_nt(left, right):
    return lax.dot_general(left, right, (((1,), (1,)), ((), ())), preferred_element_type=F32)


def split3(values):
    high = values.astype(BF16)
    rest = values - high.astype(F32)
    mid = rest.astype(BF16)
    low = (rest - mid.astype(F32)).astype(BF16)
    return jnp.concatenate([high.astype(F32), mid.astype(F32), low.astype(F32)], axis=0).astype(BF16)


def one_hot(ids, rows):
    row_ids = lax.broadcasted_iota(jnp.int32, (rows, ids.shape[1]), 0)
    return jnp.where(row_ids == ids, 1.0, 0.0).astype(BF16)


SMEM = pl.BlockSpec(memory_space=pltpu.SMEM)
VMEM = pl.BlockSpec(memory_space=pltpu.VMEM)


def identity(size):
    row = lax.broadcasted_iota(jnp.int32, (size, size), 0)
    col = lax.broadcasted_iota(jnp.int32, (size, size), 1)
    return jnp.where(row == col, 1.0, 0.0).astype(BF16)


def padded_rows(values, rows):
    have, lanes = values.shape
    return jnp.concatenate([values, jnp.zeros((rows - have, lanes), values.dtype)], axis=0)


def sum_parts(parts):
    rows = parts.shape[0] // 3
    return parts[:rows] + parts[rows : 2 * rows] + parts[2 * rows :]


def by_direction(rows):
    return jnp.concatenate([rows[k : k + 1] for k in range(len(DIRECTIONS))], axis=1)


def device_at(shift_gx, shift_yz):
    gx_n, yz_n = lax.axis_size("gx"), lax.axis_size("yz")
    gx = lax.rem(lax.axis_index("gx") + (shift_gx % gx_n), gx_n)
    yz = lax.rem(lax.axis_index("yz") + (shift_yz % yz_n), yz_n)
    return gx * yz_n + yz


def towards(sign):
    return [device_at(sign * a, sign * b) for a, b in DIRECTIONS]


def put(out_ref, blocks):
    places = towards(-1)
    ghost_n = blocks.shape[1] // len(DIRECTIONS)
    out_ref[...] = jnp.zeros_like(out_ref)
    for k in range(len(DIRECTIONS)):
        out_ref[places[k]] = blocks[:, k * ghost_n : (k + 1) * ghost_n]


def take(in_ref):
    return jnp.concatenate([in_ref[place] for place in towards(1)], axis=1)


def inverse_mass(species):
    inverse = jnp.zeros(species.shape, F32)
    for spec_id, mass in enumerate(MASSES):
        inverse = jnp.where(species == spec_id, F32(1.0 / mass), inverse)
    return inverse


def start_kernel(
    ahead_ref,
    pos_ref,
    vel_ref,
    force_ref,
    species_ref,
    live_ref,
    count_ref,
    send_ref,
    moved_ref,
    half_ref,
    used_ref,
    out_ref,
):
    species = species_ref[...]
    slot = lax.broadcasted_iota(jnp.int32, species.shape, 1)
    used_ref[...] = jnp.where(slot < live_ref[...].reshape(1, 1), count_ref[...], 0).astype(F32)
    half = vel_ref[...] + 0.5 * STEP * inverse_mass(species) * force_ref[...]
    moved = pos_ref[...] + STEP * half
    half_ref[...] = half
    moved_ref[...] = moved
    spare = jnp.zeros((1, species.shape[1]), F32)
    sources = split3(jnp.concatenate([moved, species.astype(F32), half, spare], axis=0))
    sends = send_ref[...]
    picked = sum_parts(mm(sources, one_hot(by_direction(sends), species.shape[1])))
    sent = sends.astype(F32)
    ghost_n = sent.shape[1]
    rest = jnp.zeros((TILE[0], TILE[1] - 4 * ghost_n), F32)
    out_ref[...] = jnp.zeros_like(out_ref)
    for k in range(len(DIRECTIONS)):
        block = picked[:, k * ghost_n : (k + 1) * ghost_n]
        out_ref[ahead_ref[k]] = jnp.concatenate([block[:4], block[4:], sent[:4], sent[4:], rest], axis=1)


def total_force(own, back, sends):
    pick = one_hot(by_direction(sends), own.shape[1])
    return own + sum_parts(mm_nt(split3(padded_rows(back, 8)), pick))[0:3]


def forces_tile(own, on_ghosts):
    room = TILE[1] - on_ghosts.shape[1]
    upper = jnp.concatenate([on_ghosts, own[:, :room]], axis=1)
    last = [own[c : c + 1, room:] for c in range(3)]
    last.append(jnp.zeros((1, TILE[1] - 3 * (own.shape[1] - room)), F32))
    return jnp.concatenate([upper, jnp.concatenate(last, axis=1)], axis=0)


def domain_force(all_ref, shift_gx, shift_yz, sends, atom_n):
    ghost_n = sends.shape[1]
    back = []
    for k, (a, b) in enumerate(DIRECTIONS):
        place = device_at(shift_gx + a, shift_yz + b)
        back.append(all_ref[place][0:3, k * ghost_n : (k + 1) * ghost_n])
    tile = all_ref[device_at(shift_gx, shift_yz)]
    room = TILE[1] - len(DIRECTIONS) * ghost_n
    over = atom_n - room
    last = jnp.concatenate([tile[3:4, c * over : (c + 1) * over] for c in range(3)], axis=0)
    own = jnp.concatenate([tile[0:3, TILE[1] - room :], last], axis=1)
    return total_force(own, jnp.concatenate(back, axis=1), sends)


def step_on(moved, half, kinds, forces):
    kick = 0.5 * STEP * inverse_mass(kinds) * forces
    half_two = half + kick + kick
    return half_two, moved + STEP * half_two


def last_kernel(own_ref, send_ref, half_two_ref, species_ref, in_ref, vel_ref, force_ref):
    forces = total_force(own_ref[...], take(in_ref), send_ref[...])
    force_ref[...] = forces
    vel_ref[...] = half_two_ref[...] + 0.5 * STEP * inverse_mass(species_ref[...]) * forces


def weights_kernel(
    radial_ref,
    embed_ref,
    readout_ref,
    env_t_ref,
    latent_ref,
    into_ref,
    on_hidden_ref,
    on_inner_ref,
    on_bent_ref,
    on_weight_ref,
    readout_t_ref,
    radial_back_ref,
):
    latent = latent_ref.shape[1]
    eye = identity(latent)
    half = BF16(0.5)
    latent_w = latent_ref[...]
    readout = readout_ref[...]
    none = jnp.zeros((BASIS_PAD - 8, latent), BF16)
    readout16 = padded_rows(readout.astype(F32), BASIS_PAD).astype(BF16)
    radial16 = jnp.concatenate([radial_ref[...] * half, none], axis=0)
    latent_t = mm_nt(eye, latent_w * half).astype(BF16)
    on_hidden_ref[...] = jnp.concatenate([latent_t[:, :latent], env_t_ref[...], readout16], axis=0)
    on_inner_ref[...] = latent_t[:, latent:]
    on_bent_ref[...] = (latent_w.astype(F32) * (0.5 * readout.astype(F32))).astype(BF16)
    on_weight_ref[...] = mm_nt(eye, jnp.concatenate([env_t_ref[...], readout16], axis=0)).astype(BF16)
    readout_t_ref[...] = mm_nt(eye, jnp.broadcast_to(readout.astype(F32), (128, latent)).astype(BF16))
    radial_back_ref[...] = radial16
    into = jnp.concatenate([embed_ref[1] * half, embed_ref[0] * half, radial16], axis=0)
    into_ref[...] = mm_nt(eye, into).astype(BF16)


def list_kernel(used_ref, slots_ref, neigh_ref, centre_ref, total_ref):
    atom_n, slot_n = slots_ref.shape
    blocks, lanes = neigh_ref.shape
    slots_t = mm_nt(identity(slot_n), slots_ref[...].astype(F32).astype(BF16)).astype(BF16)
    used = used_ref[...]
    row_i = lax.broadcasted_iota(jnp.int32, (atom_n, atom_n), 0)
    col_i = lax.broadcasted_iota(jnp.int32, (atom_n, atom_n), 1)
    end = jnp.sum(jnp.where(col_i <= row_i, used, 0.0), axis=1, keepdims=True)
    own = jnp.sum(jnp.where(col_i == row_i, used, 0.0), axis=1, keepdims=True)
    total = jnp.sum(used)
    total_ref[0] = total.astype(jnp.int32)
    lane = lax.broadcasted_iota(jnp.int32, (1, lanes), 1)

    def one_block(block, carry):
        place = (lane + block * lanes).astype(F32)
        past = end <= place
        centre = jnp.sum(jnp.where(past, 1.0, 0.0), axis=0, keepdims=True)
        start = jnp.sum(jnp.where(past, own, 0.0), axis=0, keepdims=True)
        slot = (place - start).astype(jnp.int32)
        centre_id = centre.astype(jnp.int32)
        rows = mm(slots_t, one_hot(centre_id, atom_n))
        slot_ids = lax.broadcasted_iota(jnp.int32, (slot_n, lanes), 0)
        neigh = jnp.sum(jnp.where(slot_ids == slot, rows, 0.0), axis=0, keepdims=True)
        valid = place < total
        neigh_ref[pl.ds(block, 1), :] = jnp.where(valid, neigh.astype(jnp.int32), -1)
        centre_ref[pl.ds(block, 1), :] = jnp.where(valid, centre_id, -1)
        return carry

    lax.fori_loop(0, blocks, one_block, 0)


def list_pairs(used, neighbours):
    blocks = pl.cdiv(neighbours.size, LANES)
    pairs = jax.ShapeDtypeStruct((blocks, LANES), jnp.int32)
    return pl.pallas_call(
        list_kernel,
        out_shape=[pairs, pairs, jax.ShapeDtypeStruct((1,), jnp.int32)],
        in_specs=[VMEM] * 2,
        out_specs=[VMEM, VMEM, SMEM],
        compiler_params=pltpu.CompilerParams(vmem_limit_bytes=16 * 2**20),
        cost_estimate=pl.CostEstimate(flops=10**9, bytes_accessed=2**16, transcendentals=0),
        name="list_pairs",
    )(used, neighbours)


def prepare_weights(radial_weight, species_embed, env_weight, latent_weight, readout):
    latent, features = env_weight.shape[1:]
    shapes = (
        ((latent, 2 * SPECIES + BASIS_PAD), BF16),
        ((latent + features + BASIS_PAD, latent), BF16),
        ((latent, features), BF16),
        ((latent + features, latent), BF16),
        ((latent, features + BASIS_PAD), BF16),
        ((latent, 128), F32),
        ((BASIS_PAD, latent), BF16),
    )
    operands = [radial_weight, species_embed, readout[None, :], env_weight[0].T, latent_weight[0]]
    return pl.pallas_call(
        weights_kernel,
        out_shape=[jax.ShapeDtypeStruct(*shape) for shape in shapes],
        in_specs=[VMEM] * len(operands),
        out_specs=[VMEM] * len(shapes),
        compiler_params=pltpu.CompilerParams(vmem_limit_bytes=24 * 2**20),
        cost_estimate=pl.CostEstimate(flops=10**9, bytes_accessed=4 * 2**20, transcendentals=0),
        name="prepare_weights",
    )(*operands)


def silu_pair(half_in):
    bent = jnp.tanh(half_in)
    part = half_in * bent
    return half_in + part, (1.0 + bent) * (1.0 + (half_in - part))


def force_kernel(
    total_ref,
    neigh_ref,
    centre_ref,
    moved_ref,
    own_kind_ref,
    into_ref,
    on_hidden_ref,
    on_inner_ref,
    on_bent_ref,
    on_weight_ref,
    readout_ref,
    radial_back_ref,
    in_ref,
    *refs,
    second_call,
    out_ghost_n,
):
    *refs, hot_s, use_s, u_s, slope_s, raw_s, part_s, ain_s, energy_s, c_s, dc_s, f_s = refs
    blocks, lanes = neigh_ref.shape
    atom_n = moved_ref.shape[1]
    ghost_n = out_ghost_n
    ext_n = atom_n + ghost_n * len(DIRECTIONS)
    own_kind = own_kind_ref[...]
    from_owners = [in_ref[place] for place in towards(-1)]
    ghosts = jnp.concatenate(
        [
            jnp.concatenate([owner[:, n * ghost_n : (n + 1) * ghost_n] for owner in from_owners], axis=1)
            for n in range(2)
        ],
        axis=0,
    )
    ghost_kind = ghosts[3:4].astype(jnp.int32)
    if second_call:
        half_ref, send_ref, all_ref, half_two_ref, end_ref, own_out_ref, out_ref = refs
        on_ghosts = []
        for k, (a, b) in enumerate(DIRECTIONS):
            sends = jnp.concatenate(
                [from_owners[k][:, n * ghost_n : (n + 1) * ghost_n] for n in (2, 3)], axis=0
            ).astype(jnp.int32)
            whole = domain_force(all_ref, -a, -b, sends, atom_n)
            picked = mm(split3(padded_rows(whole, 8)), one_hot(sends[k : k + 1], atom_n))
            on_ghosts.append(sum_parts(picked)[0:3])
        _, ghost_pos = step_on(
            ghosts[0:3], ghosts[4:7], ghost_kind, jnp.concatenate(on_ghosts, axis=1)
        )
        whole = domain_force(all_ref, 0, 0, send_ref[...], atom_n)
        half_two, own_pos = step_on(moved_ref[...], half_ref[...], own_kind, whole)
        half_two_ref[...] = half_two
        end_ref[...] = own_pos
    else:
        (out_ref,) = refs
        own_pos, ghost_pos = moved_ref[...], ghosts[0:3]
    kind = jnp.concatenate([own_kind, ghost_kind], axis=1)
    pos = jnp.concatenate([own_pos, ghost_pos], axis=1)
    basis_n = SPECIES
    latent, features = on_inner_ref.shape
    count = (total_ref[0] + lanes - 1) // lanes
    scale = COUPLING * SLOTS ** (-0.5)

    pos8 = padded_rows(pos, 8) * (1.0 / RADIUS)
    pos_parts = split3(jnp.concatenate([pos8, -pos8[:, :atom_n]], axis=1))
    row8 = lax.broadcasted_iota(jnp.int32, (SPECIES, ext_n), 0)
    kinds = jnp.where(row8 == kind, 1.0, 0.0)
    basis_in = identity(BASIS_PAD).astype(F32)
    selected = jnp.concatenate(
        [
            jnp.concatenate([kinds, jnp.zeros((SPECIES + BASIS_PAD, ext_n), F32)], axis=0),
            jnp.concatenate(
                [jnp.zeros((SPECIES, atom_n), F32), kinds[:, :atom_n], jnp.zeros((BASIS_PAD, atom_n), F32)], axis=0
            ),
            jnp.concatenate([jnp.zeros((2 * SPECIES, BASIS_PAD), F32), basis_in], axis=0),
        ],
        axis=1,
    )
    weight_in = mm(into_ref[...], selected.astype(BF16)).astype(BF16)

    mid_row = lax.broadcasted_iota(jnp.int32, (BASIS_PAD, lanes), 0).astype(F32)
    mids = (mid_row + 0.5) / basis_n
    sharp = 2.0 * basis_n * basis_n

    c_s[...] = jnp.zeros_like(c_s)
    dc_s[...] = jnp.zeros_like(dc_s)
    f_s[...] = jnp.zeros_like(f_s)

    def geometry(block):
        vec = u_s[block]
        square = jnp.sum(vec * vec, axis=0, keepdims=True)
        inside = jnp.maximum(1.0 - square, 0.0)
        inside = jnp.where(centre_ref[pl.ds(block, 1), :] >= 0, inside, 0.0)
        apart = square - mids
        return vec, inside, apart, jnp.exp(-sharp * apart * apart)

    def first(block, carry):
        hot_j = one_hot(neigh_ref[pl.ds(block, 1), :], ext_n)
        hot_c = one_hot(centre_ref[pl.ds(block, 1), :], atom_n)
        hot = jnp.concatenate([hot_j, hot_c], axis=0)
        hot_s[block] = hot
        u_s[block] = sum_parts(mm(pos_parts, hot))
        vec, inside, _, basis = geometry(block)
        use = jnp.concatenate([hot_c * vec[k : k + 1].astype(BF16) for k in range(3)], axis=0)
        use_s[block] = use
        pre = mm(weight_in, jnp.concatenate([hot, basis.astype(BF16)], axis=0))
        hidden, slope = silu_pair(pre)
        slope_s[block] = slope.astype(BF16)
        taken = mm(on_hidden_ref[...], hidden.astype(BF16))
        part_s[block] = taken[:latent]
        raw = taken[latent : latent + features]
        raw_s[block] = raw
        energy_s[block] = taken[latent + features : latent + features + 8]
        c_s[...] += mm_nt((raw * (inside * inside)).astype(BF16), use)
        return carry

    lax.fori_loop(0, count, first, 0)
    c_all = c_s[...] * scale
    c_b = c_all.astype(BF16)

    def second(block, carry):
        _, inside, _, _ = geometry(block)
        use = use_s[block]
        env = inside * inside
        weight = raw_s[block] * env
        inner = weight * mm(c_b, use)
        later = part_s[block] + mm(on_inner_ref[...], inner.astype(BF16))
        gain, bent = silu_pair(later)
        readout = jnp.concatenate([readout_ref[...]] * (lanes // 128), axis=1)
        energy_s[block] += jnp.sum(gain * readout, axis=0, keepdims=True)
        taken = mm(on_bent_ref[...], bent.astype(BF16))
        part_s[block] = taken[:latent]
        a_in = taken[latent:] * env
        ain_s[block] = a_in
        dc_s[...] += mm_nt((a_in * weight).astype(BF16), use)
        return carry

    lax.fori_loop(0, count, second, 0)
    c_dc = jnp.concatenate([c_all, dc_s[...] * scale], axis=0).astype(BF16)
    both = jnp.concatenate([c_all.T, dc_s[...].T * scale], axis=1).astype(BF16)

    def third(block, carry):
        vec, inside, apart, basis = geometry(block)
        use = use_s[block]
        hot = hot_s[block]
        env = inside * inside
        raw = raw_s[block]
        weight = raw * env
        a_in = ain_s[block]
        along = mm(c_dc, use)
        d_weight = a_in * along[:features] + along[features:]
        d_env = jnp.sum(d_weight * raw, axis=0, keepdims=True) + energy_s[block][0:1]
        ones = jnp.ones((BASIS_PAD, lanes), BF16)
        d_hidden = part_s[block] + mm(
            on_weight_ref[...], jnp.concatenate([d_weight.astype(BF16), ones], axis=0)
        )
        d_pre = (d_hidden * slope_s[block].astype(F32)).astype(BF16)
        d_basis = mm(radial_back_ref[...], d_pre)
        d_square = env * jnp.sum(d_basis * basis * apart, axis=0, keepdims=True) * (-2.0 * sharp)
        d_square = d_square - 2.0 * inside * d_env
        d_all = mm(both, jnp.concatenate([a_in * weight, weight], axis=0).astype(BF16))
        hot_c = hot[ext_n:].astype(F32)
        picked = [
            jnp.sum(d_all[k * atom_n : (k + 1) * atom_n] * hot_c, axis=0, keepdims=True)
            for k in range(3)
        ]
        d_vec = jnp.concatenate(picked + [jnp.zeros((5, lanes), F32)], axis=0)
        d_vec = (d_vec + 2.0 * d_square * vec) * (1.0 / RADIUS)
        f_s[...] += mm_nt(split3(d_vec), hot)
        return carry

    lax.fori_loop(0, count, third, 0)
    summed = f_s[0:8] + f_s[8:16] + f_s[16:24]
    on_centre = summed[0:3, ext_n:]
    on_neigh = summed[0:3, :ext_n]
    own = on_centre - on_neigh[:, :atom_n]
    if second_call:
        own_out_ref[...] = own
        put(out_ref, -on_neigh[:, atom_n:])
    else:
        tile = forces_tile(own, -on_neigh[:, atom_n:])
        out_ref[...] = jnp.broadcast_to(tile[None], out_ref.shape)


def pair_forces(pairs, own_pos, own_kind, weights, incoming, ghost_n, second=()):
    neigh, centre, total = pairs
    blocks, lanes = neigh.shape
    latent, features = weights[2].shape
    atom_n = own_pos.shape[1]
    devices = incoming.shape[0]
    ext_n = atom_n + ghost_n * len(DIRECTIONS)
    operands = [total, neigh, centre, own_pos, own_kind, *weights, incoming, *second]
    if second:
        out_shape = [jax.ShapeDtypeStruct((3, atom_n), F32)] * 3
        out_shape.append(jax.ShapeDtypeStruct((devices, 3, ghost_n), F32))
    else:
        out_shape = [jax.ShapeDtypeStruct((devices, *TILE), F32)]
    pair_rows = blocks * lanes
    return pl.pallas_call(
        functools.partial(force_kernel, second_call=bool(second), out_ghost_n=ghost_n),
        out_shape=out_shape,
        in_specs=[SMEM] + [VMEM] * (len(operands) - 1),
        out_specs=[VMEM] * len(out_shape),
        scratch_shapes=[
            pltpu.VMEM((blocks, ext_n + atom_n, lanes), BF16),
            pltpu.VMEM((blocks, 3 * atom_n, lanes), BF16),
            pltpu.VMEM((blocks, 8, lanes), F32),
            pltpu.VMEM((blocks, latent, lanes), BF16),
            pltpu.VMEM((blocks, features, lanes), F32),
            pltpu.VMEM((blocks, latent, lanes), F32),
            pltpu.VMEM((blocks, features, lanes), F32),
            pltpu.VMEM((blocks, 8, lanes), F32),
            pltpu.VMEM((features, 3 * atom_n), F32),
            pltpu.VMEM((features, 3 * atom_n), F32),
            pltpu.VMEM((24, ext_n + atom_n), F32),
        ],
        compiler_params=pltpu.CompilerParams(vmem_limit_bytes=48 * 2**20),
        cost_estimate=pl.CostEstimate(
            flops=pair_rows * latent * 2700, bytes_accessed=4 * 2**20, transcendentals=0
        ),
        name="pair_forces",
    )(*operands)


def small_call(kernel, name, operands, out_shape, smem_n=0):
    return pl.pallas_call(
        kernel,
        out_shape=out_shape,
        in_specs=[SMEM] * smem_n + [VMEM] * (len(operands) - smem_n),
        out_specs=[VMEM] * len(out_shape),
        compiler_params=pltpu.CompilerParams(vmem_limit_bytes=16 * 2**20),
        name=name,
    )(*operands)


def devices_at(shift_gx, shift_yz):
    gx_n, yz_n = lax.axis_size("gx"), lax.axis_size("yz")
    gx = (lax.axis_index("gx") + jnp.asarray(shift_gx, jnp.int32) + gx_n) % gx_n
    yz = (lax.axis_index("yz") + jnp.asarray(shift_yz, jnp.int32) + yz_n) % yz_n
    return gx * yz_n + yz


def exchange(blocks):
    return lax.all_to_all(blocks, ("gx", "yz"), 0, 0, tiled=True)


def body(
    positions,
    velocities,
    forces_start,
    species,
    live_atoms,
    send_list,
    neighbours,
    neighbour_count,
    radial_weight,
    species_embed,
    env_weight,
    latent_weight,
    readout,
):
    atom_n = positions.shape[1]
    ghost_n = send_list.shape[1]
    devices = lax.axis_size("gx") * lax.axis_size("yz")
    atoms = jax.ShapeDtypeStruct((3, atom_n), F32)

    kinds = species.reshape(1, atom_n)
    ahead = devices_at([a for a, _ in DIRECTIONS], [b for _, b in DIRECTIONS])
    moved, half, used, sent = small_call(
        start_kernel,
        "start",
        [
            ahead,
            positions,
            velocities,
            forces_start,
            kinds,
            live_atoms,
            neighbour_count.reshape(1, atom_n),
            send_list,
        ],
        [atoms, atoms, jax.ShapeDtypeStruct((1, atom_n), F32), jax.ShapeDtypeStruct((devices, *TILE), F32)],
        smem_n=1,
    )
    got = exchange(sent)
    pairs = list_pairs(used, neighbours)
    weights = prepare_weights(radial_weight, species_embed, env_weight, latent_weight, readout)
    (sent,) = pair_forces(pairs, moved, kinds, weights, got, ghost_n)
    every = exchange(sent)
    half_two, positions_end, own, sent = pair_forces(
        pairs, moved, kinds, weights, got, ghost_n, (half, send_list, every)
    )
    back = exchange(sent)
    velocities_end, forces_end = small_call(
        last_kernel, "last", [own, send_list, half_two, kinds, back], [atoms, atoms]
    )
    return (positions_end, velocities_end, forces_end)


def solution(mesh):
    placed = (
        P(None, ("gx", "yz")),
        P(None, ("gx", "yz")),
        P(None, ("gx", "yz")),
        P(("gx", "yz")),
        P(("gx", "yz")),
        P(None, ("gx", "yz")),
        P(("gx", "yz"), None),
        P(("gx", "yz")),
        P(),
        P(),
        P(),
        P(),
        P(),
    )
    return jax.shard_map(
        body,
        mesh=mesh,
        in_specs=placed,
        out_specs=(P(None, ("gx", "yz")), P(None, ("gx", "yz")), P(None, ("gx", "yz"))),
        check_vma=False,
    )
```

```python
import functools

import jax
import jax.numpy as jnp
from jax import lax
from jax.experimental import pallas as pl
from jax.experimental.pallas import tpu as pltpu
from jax.sharding import PartitionSpec as P

SPECIES = 8
SLOTS = 128
RADIUS = 6.0
STEP = 0.25
COUPLING = 4.0
MASSES = (1.008, 12.011, 14.007, 15.999, 32.06, 22.99, 35.45, 30.97)

LANES = 1024
TAIL = 640
LISTED = 2
DIRECTIONS = ((-1, -1), (-1, 0), (-1, 1), (0, -1), (0, 1), (1, -1), (1, 0), (1, 1))
TILE = (4, 128)
BASIS_PAD = 16

F32 = jnp.float32
BF16 = jnp.bfloat16


def mm(left, right):
    return jnp.dot(left, right, preferred_element_type=F32)


def mm_nt(left, right):
    return lax.dot_general(left, right, (((1,), (1,)), ((), ())), preferred_element_type=F32)


def split3(values):
    high = values.astype(BF16)
    rest = values - high.astype(F32)
    mid = rest.astype(BF16)
    low = (rest - mid.astype(F32)).astype(BF16)
    return jnp.concatenate([high.astype(F32), mid.astype(F32), low.astype(F32)], axis=0).astype(BF16)


def one_hot(ids, rows):
    row_ids = lax.broadcasted_iota(jnp.int32, (rows, ids.shape[1]), 0)
    return jnp.where(row_ids == ids, 1.0, 0.0).astype(BF16)


SMEM = pl.BlockSpec(memory_space=pltpu.SMEM)
VMEM = pl.BlockSpec(memory_space=pltpu.VMEM)


def identity(size):
    row = lax.broadcasted_iota(jnp.int32, (size, size), 0)
    col = lax.broadcasted_iota(jnp.int32, (size, size), 1)
    return jnp.where(row == col, 1.0, 0.0).astype(BF16)


def padded_rows(values, rows):
    have, lanes = values.shape
    return jnp.concatenate([values, jnp.zeros((rows - have, lanes), values.dtype)], axis=0)


def sum_parts(parts):
    rows = parts.shape[0] // 3
    return parts[:rows] + parts[rows : 2 * rows] + parts[2 * rows :]


def by_direction(rows):
    return jnp.concatenate([rows[k : k + 1] for k in range(len(DIRECTIONS))], axis=1)


def device_at(shift_gx, shift_yz):
    gx_n, yz_n = lax.axis_size("gx"), lax.axis_size("yz")
    gx = lax.rem(lax.axis_index("gx") + (shift_gx % gx_n), gx_n)
    yz = lax.rem(lax.axis_index("yz") + (shift_yz % yz_n), yz_n)
    return gx * yz_n + yz


def towards(sign):
    return [device_at(sign * a, sign * b) for a, b in DIRECTIONS]


def put(out_ref, blocks):
    places = towards(-1)
    ghost_n = blocks.shape[1] // len(DIRECTIONS)
    out_ref[...] = jnp.zeros_like(out_ref)
    for k in range(len(DIRECTIONS)):
        out_ref[places[k]] = blocks[:, k * ghost_n : (k + 1) * ghost_n]


def take(in_ref):
    return jnp.concatenate([in_ref[place] for place in towards(1)], axis=1)


def inverse_mass(species):
    inverse = jnp.zeros(species.shape, F32)
    for spec_id, mass in enumerate(MASSES):
        inverse = jnp.where(species == spec_id, F32(1.0 / mass), inverse)
    return inverse


def start_kernel(
    ahead_ref,
    pos_ref,
    vel_ref,
    force_ref,
    species_ref,
    live_ref,
    count_ref,
    send_ref,
    moved_ref,
    half_ref,
    used_ref,
    out_ref,
):
    species = species_ref[...]
    slot = lax.broadcasted_iota(jnp.int32, species.shape, 1)
    used_ref[...] = jnp.where(slot < live_ref[...].reshape(1, 1), count_ref[...], 0).astype(F32)
    half = vel_ref[...] + 0.5 * STEP * inverse_mass(species) * force_ref[...]
    moved = pos_ref[...] + STEP * half
    half_ref[...] = half
    moved_ref[...] = moved
    spare = jnp.zeros((1, species.shape[1]), F32)
    sources = split3(jnp.concatenate([moved, species.astype(F32), half, spare], axis=0))
    sends = send_ref[...]
    picked = sum_parts(mm(sources, one_hot(by_direction(sends), species.shape[1])))
    sent = sends.astype(F32)
    ghost_n = sent.shape[1]
    rest = jnp.zeros((TILE[0], TILE[1] - 4 * ghost_n), F32)
    out_ref[...] = jnp.zeros_like(out_ref)
    for k in range(len(DIRECTIONS)):
        block = picked[:, k * ghost_n : (k + 1) * ghost_n]
        out_ref[ahead_ref[k]] = jnp.concatenate([block[:4], block[4:], sent[:4], sent[4:], rest], axis=1)


def total_force(own, back, sends):
    pick = one_hot(by_direction(sends), own.shape[1])
    return own + sum_parts(mm_nt(split3(padded_rows(back, 8)), pick))[0:3]


def forces_tile(own, on_ghosts):
    room = TILE[1] - on_ghosts.shape[1]
    upper = jnp.concatenate([on_ghosts, own[:, :room]], axis=1)
    last = [own[c : c + 1, room:] for c in range(3)]
    last.append(jnp.zeros((1, TILE[1] - 3 * (own.shape[1] - room)), F32))
    return jnp.concatenate([upper, jnp.concatenate(last, axis=1)], axis=0)


def domain_force(all_ref, shift_gx, shift_yz, sends, atom_n):
    ghost_n = sends.shape[1]
    back = []
    for k, (a, b) in enumerate(DIRECTIONS):
        place = device_at(shift_gx + a, shift_yz + b)
        back.append(all_ref[place][0:3, k * ghost_n : (k + 1) * ghost_n])
    tile = all_ref[device_at(shift_gx, shift_yz)]
    room = TILE[1] - len(DIRECTIONS) * ghost_n
    over = atom_n - room
    last = jnp.concatenate([tile[3:4, c * over : (c + 1) * over] for c in range(3)], axis=0)
    own = jnp.concatenate([tile[0:3, TILE[1] - room :], last], axis=1)
    return total_force(own, jnp.concatenate(back, axis=1), sends)


def step_on(moved, half, kinds, forces):
    kick = 0.5 * STEP * inverse_mass(kinds) * forces
    half_two = half + kick + kick
    return half_two, moved + STEP * half_two


def last_kernel(own_ref, send_ref, half_two_ref, species_ref, in_ref, vel_ref, force_ref):
    forces = total_force(own_ref[...], take(in_ref), send_ref[...])
    force_ref[...] = forces
    vel_ref[...] = half_two_ref[...] + 0.5 * STEP * inverse_mass(species_ref[...]) * forces


def weights_kernel(
    radial_ref,
    embed_ref,
    readout_ref,
    env_t_ref,
    latent_ref,
    into_ref,
    on_hidden_ref,
    on_inner_ref,
    on_bent_ref,
    on_weight_ref,
    readout_t_ref,
    radial_back_ref,
):
    latent = latent_ref.shape[1]
    eye = identity(latent)
    half = BF16(0.5)
    latent_w = latent_ref[...]
    readout = readout_ref[...]
    none = jnp.zeros((BASIS_PAD - 8, latent), BF16)
    readout16 = padded_rows(readout.astype(F32), BASIS_PAD).astype(BF16)
    radial16 = jnp.concatenate([radial_ref[...] * half, none], axis=0)
    latent_t = mm_nt(eye, latent_w * half).astype(BF16)
    on_hidden_ref[...] = jnp.concatenate([latent_t[:, :latent], env_t_ref[...], readout16], axis=0)
    on_inner_ref[...] = latent_t[:, latent:]
    on_bent_ref[...] = (latent_w.astype(F32) * (0.5 * readout.astype(F32))).astype(BF16)
    on_weight_ref[...] = mm_nt(eye, jnp.concatenate([env_t_ref[...], readout16], axis=0)).astype(BF16)
    readout_t_ref[...] = mm_nt(eye, jnp.broadcast_to(readout.astype(F32), (128, latent)).astype(BF16))
    radial_back_ref[...] = radial16
    into = jnp.concatenate([embed_ref[1] * half, embed_ref[0] * half, radial16], axis=0)
    into_ref[...] = mm_nt(eye, into).astype(BF16)


def list_kernel(used_ref, slots_ref, neigh_ref, centre_ref, total_ref):
    atom_n, slot_n = slots_ref.shape
    blocks, lanes = neigh_ref.shape
    slots_t = mm_nt(identity(slot_n), slots_ref[...].astype(F32).astype(BF16)).astype(BF16)
    used = used_ref[...]
    row_i = lax.broadcasted_iota(jnp.int32, (atom_n, atom_n), 0)
    col_i = lax.broadcasted_iota(jnp.int32, (atom_n, atom_n), 1)
    end = jnp.sum(jnp.where(col_i <= row_i, used, 0.0), axis=1, keepdims=True)
    own = jnp.sum(jnp.where(col_i == row_i, used, 0.0), axis=1, keepdims=True)
    total = jnp.sum(used)
    total_ref[0] = total.astype(jnp.int32)
    lane = lax.broadcasted_iota(jnp.int32, (1, lanes), 1)

    def one_block(block):
        place = (lane + block * lanes).astype(F32)
        past = end <= place
        centre = jnp.sum(jnp.where(past, 1.0, 0.0), axis=0, keepdims=True)
        start = jnp.sum(jnp.where(past, own, 0.0), axis=0, keepdims=True)
        slot = (place - start).astype(jnp.int32)
        centre_id = centre.astype(jnp.int32)
        rows = mm(slots_t, one_hot(centre_id, atom_n))
        slot_ids = lax.broadcasted_iota(jnp.int32, (slot_n, lanes), 0)
        neigh = jnp.sum(jnp.where(slot_ids == slot, rows, 0.0), axis=0, keepdims=True)
        valid = place < total
        neigh_ref[pl.ds(block, 1), :] = jnp.where(valid, neigh.astype(jnp.int32), -1)
        centre_ref[pl.ds(block, 1), :] = jnp.where(valid, centre_id, -1)

    def some_blocks(step, carry):
        for more in range(LISTED):
            one_block(step * LISTED + more)
        return carry

    group = LISTED * lanes
    lax.fori_loop(0, (total.astype(jnp.int32) + group - 1) // group, some_blocks, 0)


def list_pairs(used, neighbours):
    blocks = pl.cdiv(neighbours.size, LANES * LISTED) * LISTED
    pairs = jax.ShapeDtypeStruct((blocks, LANES), jnp.int32)
    return pl.pallas_call(
        list_kernel,
        out_shape=[pairs, pairs, jax.ShapeDtypeStruct((1,), jnp.int32)],
        in_specs=[VMEM] * 2,
        out_specs=[VMEM, VMEM, SMEM],
        compiler_params=pltpu.CompilerParams(vmem_limit_bytes=16 * 2**20),
        cost_estimate=pl.CostEstimate(flops=10**9, bytes_accessed=2**16, transcendentals=0),
        name="list_pairs",
    )(used, neighbours)


def prepare_weights(radial_weight, species_embed, env_weight, latent_weight, readout):
    latent, features = env_weight.shape[1:]
    shapes = (
        ((latent, 2 * SPECIES + BASIS_PAD), BF16),
        ((latent + features + BASIS_PAD, latent), BF16),
        ((latent, features), BF16),
        ((latent + features, latent), BF16),
        ((latent, features + BASIS_PAD), BF16),
        ((latent, 128), F32),
        ((BASIS_PAD, latent), BF16),
    )
    operands = [radial_weight, species_embed, readout[None, :], env_weight[0].T, latent_weight[0]]
    return pl.pallas_call(
        weights_kernel,
        out_shape=[jax.ShapeDtypeStruct(*shape) for shape in shapes],
        in_specs=[VMEM] * len(operands),
        out_specs=[VMEM] * len(shapes),
        compiler_params=pltpu.CompilerParams(vmem_limit_bytes=24 * 2**20),
        cost_estimate=pl.CostEstimate(flops=10**9, bytes_accessed=4 * 2**20, transcendentals=0),
        name="prepare_weights",
    )(*operands)


def silu_pair(half_in):
    bent = jnp.tanh(half_in)
    part = half_in * bent
    return half_in + part, (1.0 + bent) * (1.0 + (half_in - part))


def force_kernel(
    total_ref,
    neigh_ref,
    centre_ref,
    moved_ref,
    own_kind_ref,
    into_ref,
    on_hidden_ref,
    on_inner_ref,
    on_bent_ref,
    on_weight_ref,
    readout_ref,
    radial_back_ref,
    in_ref,
    *refs,
    second_call,
    out_ghost_n,
):
    *refs, hot_s, use_s, u_s, slope_s, raw_s, part_s, ain_s, energy_s, c_s, dc_s, f_s = refs
    blocks, lanes = neigh_ref.shape
    atom_n = moved_ref.shape[1]
    ghost_n = out_ghost_n
    ext_n = atom_n + ghost_n * len(DIRECTIONS)
    own_kind = own_kind_ref[...]
    from_owners = [in_ref[place] for place in towards(-1)]
    ghosts = jnp.concatenate(
        [
            jnp.concatenate([owner[:, n * ghost_n : (n + 1) * ghost_n] for owner in from_owners], axis=1)
            for n in range(2)
        ],
        axis=0,
    )
    ghost_kind = ghosts[3:4].astype(jnp.int32)
    if second_call:
        half_ref, send_ref, all_ref, half_two_ref, end_ref, own_out_ref, out_ref = refs
        on_ghosts = []
        for k, (a, b) in enumerate(DIRECTIONS):
            sends = jnp.concatenate(
                [from_owners[k][:, n * ghost_n : (n + 1) * ghost_n] for n in (2, 3)], axis=0
            ).astype(jnp.int32)
            whole = domain_force(all_ref, -a, -b, sends, atom_n)
            picked = mm(split3(padded_rows(whole, 8)), one_hot(sends[k : k + 1], atom_n))
            on_ghosts.append(sum_parts(picked)[0:3])
        _, ghost_pos = step_on(
            ghosts[0:3], ghosts[4:7], ghost_kind, jnp.concatenate(on_ghosts, axis=1)
        )
        whole = domain_force(all_ref, 0, 0, send_ref[...], atom_n)
        half_two, own_pos = step_on(moved_ref[...], half_ref[...], own_kind, whole)
        half_two_ref[...] = half_two
        end_ref[...] = own_pos
    else:
        (out_ref,) = refs
        own_pos, ghost_pos = moved_ref[...], ghosts[0:3]
    kind = jnp.concatenate([own_kind, ghost_kind], axis=1)
    pos = jnp.concatenate([own_pos, ghost_pos], axis=1)
    basis_n = SPECIES
    latent, features = on_inner_ref.shape
    total = total_ref[0]
    full = (total + lanes - 1 - TAIL) // lanes
    scale = COUPLING * SLOTS ** (-0.5)

    pos8 = padded_rows(pos, 8) * (1.0 / RADIUS)
    pos_parts = split3(jnp.concatenate([pos8, -pos8[:, :atom_n]], axis=1))
    row8 = lax.broadcasted_iota(jnp.int32, (SPECIES, ext_n), 0)
    kinds = jnp.where(row8 == kind, 1.0, 0.0)
    basis_in = identity(BASIS_PAD).astype(F32)
    selected = jnp.concatenate(
        [
            jnp.concatenate([kinds, jnp.zeros((SPECIES + BASIS_PAD, ext_n), F32)], axis=0),
            jnp.concatenate(
                [jnp.zeros((SPECIES, atom_n), F32), kinds[:, :atom_n], jnp.zeros((BASIS_PAD, atom_n), F32)], axis=0
            ),
            jnp.concatenate([jnp.zeros((2 * SPECIES, BASIS_PAD), F32), basis_in], axis=0),
        ],
        axis=1,
    )
    weight_in = mm(into_ref[...], selected.astype(BF16)).astype(BF16)

    mid_row = lax.broadcasted_iota(jnp.int32, (BASIS_PAD, lanes), 0).astype(F32)
    mids = (mid_row + 0.5) / basis_n
    sharp = 2.0 * basis_n * basis_n

    c_s[...] = jnp.zeros_like(c_s)
    dc_s[...] = jnp.zeros_like(dc_s)
    f_s[...] = jnp.zeros_like(f_s)

    def each_block(one):
        def step(block, carry):
            one(block, lanes)
            return carry

        lax.fori_loop(0, full, step, 0)
        pl.when(total > full * lanes)(functools.partial(one, full, TAIL))

    def geometry(block, width):
        vec = u_s[block, :, :width]
        square = jnp.sum(vec * vec, axis=0, keepdims=True)
        inside = jnp.maximum(1.0 - square, 0.0)
        inside = jnp.where(centre_ref[pl.ds(block, 1), :width] >= 0, inside, 0.0)
        apart = square - mids[:, :width]
        return vec, inside, apart, jnp.exp(-sharp * apart * apart)

    def first(block, width):
        hot_j = one_hot(neigh_ref[pl.ds(block, 1), :width], ext_n)
        hot_c = one_hot(centre_ref[pl.ds(block, 1), :width], atom_n)
        hot = jnp.concatenate([hot_j, hot_c], axis=0)
        hot_s[block, :, :width] = hot
        u_s[block, :, :width] = sum_parts(mm(pos_parts, hot))
        vec, inside, _, basis = geometry(block, width)
        use = jnp.concatenate([hot_c * vec[k : k + 1].astype(BF16) for k in range(3)], axis=0)
        use_s[block, :, :width] = use
        pre = mm(weight_in, jnp.concatenate([hot, basis.astype(BF16)], axis=0))
        hidden, slope = silu_pair(pre)
        slope_s[block, :, :width] = slope.astype(BF16)
        taken = mm(on_hidden_ref[...], hidden.astype(BF16))
        part_s[block, :, :width] = taken[:latent]
        raw = taken[latent : latent + features]
        raw_s[block, :, :width] = raw
        energy_s[block, :, :width] = taken[latent + features : latent + features + 8]
        c_s[...] += mm_nt((raw * (inside * inside)).astype(BF16), use)

    each_block(first)
    c_all = c_s[...] * scale
    c_b = c_all.astype(BF16)

    def second(block, width):
        _, inside, _, _ = geometry(block, width)
        use = use_s[block, :, :width]
        env = inside * inside
        weight = raw_s[block, :, :width] * env
        inner = weight * mm(c_b, use)
        later = part_s[block, :, :width] + mm(on_inner_ref[...], inner.astype(BF16))
        gain, bent = silu_pair(later)
        readout = jnp.concatenate([readout_ref[...]] * (width // 128), axis=1)
        energy_s[block, :, :width] += jnp.sum(gain * readout, axis=0, keepdims=True)
        taken = mm(on_bent_ref[...], bent.astype(BF16))
        part_s[block, :, :width] = taken[:latent]
        a_in = taken[latent:] * env
        ain_s[block, :, :width] = a_in
        dc_s[...] += mm_nt((a_in * weight).astype(BF16), use)

    each_block(second)
    c_dc = jnp.concatenate([c_all, dc_s[...] * scale], axis=0).astype(BF16)
    both = jnp.concatenate([c_all.T, dc_s[...].T * scale], axis=1).astype(BF16)

    def third(block, width):
        vec, inside, apart, basis = geometry(block, width)
        use = use_s[block, :, :width]
        hot = hot_s[block, :, :width]
        env = inside * inside
        raw = raw_s[block, :, :width]
        weight = raw * env
        a_in = ain_s[block, :, :width]
        along = mm(c_dc, use)
        d_weight = a_in * along[:features] + along[features:]
        d_env = jnp.sum(d_weight * raw, axis=0, keepdims=True) + energy_s[block, :, :width][0:1]
        ones = jnp.ones((BASIS_PAD, width), BF16)
        d_hidden = part_s[block, :, :width] + mm(
            on_weight_ref[...], jnp.concatenate([d_weight.astype(BF16), ones], axis=0)
        )
        d_pre = (d_hidden * slope_s[block, :, :width].astype(F32)).astype(BF16)
        d_basis = mm(radial_back_ref[...], d_pre)
        d_square = env * jnp.sum(d_basis * basis * apart, axis=0, keepdims=True) * (-2.0 * sharp)
        d_square = d_square - 2.0 * inside * d_env
        d_all = mm(both, jnp.concatenate([a_in * weight, weight], axis=0).astype(BF16))
        hot_c = hot[ext_n:].astype(F32)
        picked = [
            jnp.sum(d_all[k * atom_n : (k + 1) * atom_n] * hot_c, axis=0, keepdims=True)
            for k in range(3)
        ]
        d_vec = jnp.concatenate(picked + [jnp.zeros((5, width), F32)], axis=0)
        d_vec = (d_vec + 2.0 * d_square * vec) * (1.0 / RADIUS)
        f_s[...] += mm_nt(split3(d_vec), hot)

    each_block(third)
    summed = f_s[0:8] + f_s[8:16] + f_s[16:24]
    on_centre = summed[0:3, ext_n:]
    on_neigh = summed[0:3, :ext_n]
    own = on_centre - on_neigh[:, :atom_n]
    if second_call:
        own_out_ref[...] = own
        put(out_ref, -on_neigh[:, atom_n:])
    else:
        tile = forces_tile(own, -on_neigh[:, atom_n:])
        out_ref[...] = jnp.broadcast_to(tile[None], out_ref.shape)


def pair_forces(pairs, own_pos, own_kind, weights, incoming, ghost_n, second=()):
    neigh, centre, total = pairs
    blocks, lanes = neigh.shape
    latent, features = weights[2].shape
    atom_n = own_pos.shape[1]
    devices = incoming.shape[0]
    ext_n = atom_n + ghost_n * len(DIRECTIONS)
    operands = [total, neigh, centre, own_pos, own_kind, *weights, incoming, *second]
    if second:
        out_shape = [jax.ShapeDtypeStruct((3, atom_n), F32)] * 3
        out_shape.append(jax.ShapeDtypeStruct((devices, 3, ghost_n), F32))
    else:
        out_shape = [jax.ShapeDtypeStruct((devices, *TILE), F32)]
    pair_rows = blocks * lanes
    return pl.pallas_call(
        functools.partial(force_kernel, second_call=bool(second), out_ghost_n=ghost_n),
        out_shape=out_shape,
        in_specs=[SMEM] + [VMEM] * (len(operands) - 1),
        out_specs=[VMEM] * len(out_shape),
        scratch_shapes=[
            pltpu.VMEM((blocks, ext_n + atom_n, lanes), BF16),
            pltpu.VMEM((blocks, 3 * atom_n, lanes), BF16),
            pltpu.VMEM((blocks, 8, lanes), F32),
            pltpu.VMEM((blocks, latent, lanes), BF16),
            pltpu.VMEM((blocks, features, lanes), F32),
            pltpu.VMEM((blocks, latent, lanes), F32),
            pltpu.VMEM((blocks, features, lanes), F32),
            pltpu.VMEM((blocks, 8, lanes), F32),
            pltpu.VMEM((features, 3 * atom_n), F32),
            pltpu.VMEM((features, 3 * atom_n), F32),
            pltpu.VMEM((24, ext_n + atom_n), F32),
        ],
        compiler_params=pltpu.CompilerParams(vmem_limit_bytes=48 * 2**20),
        cost_estimate=pl.CostEstimate(
            flops=pair_rows * latent * 2700, bytes_accessed=4 * 2**20, transcendentals=0
        ),
        name="pair_forces",
    )(*operands)


def small_call(kernel, name, operands, out_shape, smem_n=0):
    return pl.pallas_call(
        kernel,
        out_shape=out_shape,
        in_specs=[SMEM] * smem_n + [VMEM] * (len(operands) - smem_n),
        out_specs=[VMEM] * len(out_shape),
        compiler_params=pltpu.CompilerParams(vmem_limit_bytes=16 * 2**20),
        name=name,
    )(*operands)


def devices_at(shift_gx, shift_yz):
    gx_n, yz_n = lax.axis_size("gx"), lax.axis_size("yz")
    gx = (lax.axis_index("gx") + jnp.asarray(shift_gx, jnp.int32) + gx_n) % gx_n
    yz = (lax.axis_index("yz") + jnp.asarray(shift_yz, jnp.int32) + yz_n) % yz_n
    return gx * yz_n + yz


def exchange(blocks):
    return lax.all_to_all(blocks, ("gx", "yz"), 0, 0, tiled=True)


def body(
    positions,
    velocities,
    forces_start,
    species,
    live_atoms,
    send_list,
    neighbours,
    neighbour_count,
    radial_weight,
    species_embed,
    env_weight,
    latent_weight,
    readout,
):
    atom_n = positions.shape[1]
    ghost_n = send_list.shape[1]
    devices = lax.axis_size("gx") * lax.axis_size("yz")
    atoms = jax.ShapeDtypeStruct((3, atom_n), F32)

    kinds = species.reshape(1, atom_n)
    ahead = devices_at([a for a, _ in DIRECTIONS], [b for _, b in DIRECTIONS])
    moved, half, used, sent = small_call(
        start_kernel,
        "start",
        [
            ahead,
            positions,
            velocities,
            forces_start,
            kinds,
            live_atoms,
            neighbour_count.reshape(1, atom_n),
            send_list,
        ],
        [atoms, atoms, jax.ShapeDtypeStruct((1, atom_n), F32), jax.ShapeDtypeStruct((devices, *TILE), F32)],
        smem_n=1,
    )
    got = exchange(sent)
    pairs = list_pairs(used, neighbours)
    weights = prepare_weights(radial_weight, species_embed, env_weight, latent_weight, readout)
    (sent,) = pair_forces(pairs, moved, kinds, weights, got, ghost_n)
    every = exchange(sent)
    half_two, positions_end, own, sent = pair_forces(
        pairs, moved, kinds, weights, got, ghost_n, (half, send_list, every)
    )
    back = exchange(sent)
    velocities_end, forces_end = small_call(
        last_kernel, "last", [own, send_list, half_two, kinds, back], [atoms, atoms]
    )
    return (positions_end, velocities_end, forces_end)


def solution(mesh):
    placed = (
        P(None, ("gx", "yz")),
        P(None, ("gx", "yz")),
        P(None, ("gx", "yz")),
        P(("gx", "yz")),
        P(("gx", "yz")),
        P(None, ("gx", "yz")),
        P(("gx", "yz"), None),
        P(("gx", "yz")),
        P(),
        P(),
        P(),
        P(),
        P(),
    )
    return jax.shard_map(
        body,
        mesh=mesh,
        in_specs=placed,
        out_specs=(P(None, ("gx", "yz")), P(None, ("gx", "yz")), P(None, ("gx", "yz"))),
        check_vma=False,
    )
```

```python
import functools

import jax
import jax.numpy as jnp
from jax import lax
from jax.experimental import pallas as pl
from jax.experimental.pallas import tpu as pltpu
from jax.sharding import PartitionSpec as P

SPECIES = 8
SLOTS = 128
RADIUS = 6.0
STEP = 0.25
COUPLING = 4.0
MASSES = (1.008, 12.011, 14.007, 15.999, 32.06, 22.99, 35.45, 30.97)

LANES = 1024
TAIL = 768
GROUP = 256
LISTED = 2
DIRECTIONS = ((-1, -1), (-1, 0), (-1, 1), (0, -1), (0, 1), (1, -1), (1, 0), (1, 1))
TILE = (4, 128)
BASIS_PAD = 16

F32 = jnp.float32
BF16 = jnp.bfloat16


def mm(left, right):
    return jnp.dot(left, right, preferred_element_type=F32)


def mm_nt(left, right):
    return lax.dot_general(left, right, (((1,), (1,)), ((), ())), preferred_element_type=F32)


def split3(values):
    high = values.astype(BF16)
    rest = values - high.astype(F32)
    mid = rest.astype(BF16)
    low = (rest - mid.astype(F32)).astype(BF16)
    return jnp.concatenate([high.astype(F32), mid.astype(F32), low.astype(F32)], axis=0).astype(BF16)


def one_hot(ids, rows):
    row_ids = lax.broadcasted_iota(jnp.int32, (rows, ids.shape[1]), 0)
    return jnp.where(row_ids == ids, 1.0, 0.0).astype(BF16)


SMEM = pl.BlockSpec(memory_space=pltpu.SMEM)
VMEM = pl.BlockSpec(memory_space=pltpu.VMEM)


def identity(size):
    row = lax.broadcasted_iota(jnp.int32, (size, size), 0)
    col = lax.broadcasted_iota(jnp.int32, (size, size), 1)
    return jnp.where(row == col, 1.0, 0.0).astype(BF16)


def padded_rows(values, rows):
    have, lanes = values.shape
    return jnp.concatenate([values, jnp.zeros((rows - have, lanes), values.dtype)], axis=0)


def sum_parts(parts):
    rows = parts.shape[0] // 3
    return parts[:rows] + parts[rows : 2 * rows] + parts[2 * rows :]


def by_direction(rows):
    return jnp.concatenate([rows[k : k + 1] for k in range(len(DIRECTIONS))], axis=1)


def device_at(shift_gx, shift_yz):
    gx_n, yz_n = lax.axis_size("gx"), lax.axis_size("yz")
    gx = lax.rem(lax.axis_index("gx") + (shift_gx % gx_n), gx_n)
    yz = lax.rem(lax.axis_index("yz") + (shift_yz % yz_n), yz_n)
    return gx * yz_n + yz


def towards(sign):
    return [device_at(sign * a, sign * b) for a, b in DIRECTIONS]


def put(out_ref, blocks):
    places = towards(-1)
    ghost_n = blocks.shape[1] // len(DIRECTIONS)
    out_ref[...] = jnp.zeros_like(out_ref)
    for k in range(len(DIRECTIONS)):
        out_ref[places[k]] = blocks[:, k * ghost_n : (k + 1) * ghost_n]


def take(in_ref):
    return jnp.concatenate([in_ref[place] for place in towards(1)], axis=1)


def inverse_mass(species):
    inverse = jnp.zeros(species.shape, F32)
    for spec_id, mass in enumerate(MASSES):
        inverse = jnp.where(species == spec_id, F32(1.0 / mass), inverse)
    return inverse


def start_kernel(
    ahead_ref,
    pos_ref,
    vel_ref,
    force_ref,
    species_ref,
    live_ref,
    count_ref,
    send_ref,
    moved_ref,
    half_ref,
    used_ref,
    out_ref,
):
    species = species_ref[...]
    slot = lax.broadcasted_iota(jnp.int32, species.shape, 1)
    used_ref[...] = jnp.where(slot < live_ref[...].reshape(1, 1), count_ref[...], 0).astype(F32)
    half = vel_ref[...] + 0.5 * STEP * inverse_mass(species) * force_ref[...]
    moved = pos_ref[...] + STEP * half
    half_ref[...] = half
    moved_ref[...] = moved
    spare = jnp.zeros((1, species.shape[1]), F32)
    sources = split3(jnp.concatenate([moved, species.astype(F32), half, spare], axis=0))
    sends = send_ref[...]
    picked = sum_parts(mm(sources, one_hot(by_direction(sends), species.shape[1])))
    sent = sends.astype(F32)
    ghost_n = sent.shape[1]
    rest = jnp.zeros((TILE[0], TILE[1] - 4 * ghost_n), F32)
    out_ref[...] = jnp.zeros_like(out_ref)
    for k in range(len(DIRECTIONS)):
        block = picked[:, k * ghost_n : (k + 1) * ghost_n]
        out_ref[ahead_ref[k]] = jnp.concatenate([block[:4], block[4:], sent[:4], sent[4:], rest], axis=1)


def total_force(own, back, sends):
    pick = one_hot(by_direction(sends), own.shape[1])
    return own + sum_parts(mm_nt(split3(padded_rows(back, 8)), pick))[0:3]


def forces_tile(own, on_ghosts):
    room = TILE[1] - on_ghosts.shape[1]
    upper = jnp.concatenate([on_ghosts, own[:, :room]], axis=1)
    last = [own[c : c + 1, room:] for c in range(3)]
    last.append(jnp.zeros((1, TILE[1] - 3 * (own.shape[1] - room)), F32))
    return jnp.concatenate([upper, jnp.concatenate(last, axis=1)], axis=0)


def domain_force(all_ref, shift_gx, shift_yz, sends, atom_n):
    ghost_n = sends.shape[1]
    back = []
    for k, (a, b) in enumerate(DIRECTIONS):
        place = device_at(shift_gx + a, shift_yz + b)
        back.append(all_ref[place][0:3, k * ghost_n : (k + 1) * ghost_n])
    tile = all_ref[device_at(shift_gx, shift_yz)]
    room = TILE[1] - len(DIRECTIONS) * ghost_n
    over = atom_n - room
    last = jnp.concatenate([tile[3:4, c * over : (c + 1) * over] for c in range(3)], axis=0)
    own = jnp.concatenate([tile[0:3, TILE[1] - room :], last], axis=1)
    return total_force(own, jnp.concatenate(back, axis=1), sends)


def step_on(moved, half, kinds, forces):
    kick = 0.5 * STEP * inverse_mass(kinds) * forces
    half_two = half + kick + kick
    return half_two, moved + STEP * half_two


def last_kernel(own_ref, send_ref, half_two_ref, species_ref, in_ref, vel_ref, force_ref):
    forces = total_force(own_ref[...], take(in_ref), send_ref[...])
    force_ref[...] = forces
    vel_ref[...] = half_two_ref[...] + 0.5 * STEP * inverse_mass(species_ref[...]) * forces


def weights_kernel(
    radial_ref,
    embed_ref,
    readout_ref,
    env_t_ref,
    latent_ref,
    into_ref,
    on_hidden_ref,
    on_inner_ref,
    on_bent_ref,
    on_weight_ref,
    readout_t_ref,
    radial_back_ref,
):
    latent = latent_ref.shape[1]
    eye = identity(latent)
    half = BF16(0.5)
    latent_w = latent_ref[...]
    readout = readout_ref[...]
    none = jnp.zeros((BASIS_PAD - 8, latent), BF16)
    readout16 = padded_rows(readout.astype(F32), BASIS_PAD).astype(BF16)
    radial16 = jnp.concatenate([radial_ref[...] * half, none], axis=0)
    latent_t = mm_nt(eye, latent_w * half).astype(BF16)
    on_hidden_ref[...] = jnp.concatenate([latent_t[:, :latent], env_t_ref[...], readout16], axis=0)
    on_inner_ref[...] = latent_t[:, latent:]
    on_bent_ref[...] = (latent_w.astype(F32) * (0.5 * readout.astype(F32))).astype(BF16)
    on_weight_ref[...] = mm_nt(eye, jnp.concatenate([env_t_ref[...], readout16], axis=0)).astype(BF16)
    readout_t_ref[...] = mm_nt(eye, jnp.broadcast_to(readout.astype(F32), (128, latent)).astype(BF16))
    radial_back_ref[...] = radial16
    into = jnp.concatenate([embed_ref[1] * half, embed_ref[0] * half, radial16], axis=0)
    into_ref[...] = mm_nt(eye, into).astype(BF16)


def list_kernel(used_ref, slots_ref, neigh_ref, centre_ref, total_ref):
    atom_n, slot_n = slots_ref.shape
    blocks, lanes = neigh_ref.shape
    slots_t = mm_nt(identity(slot_n), slots_ref[...].astype(F32).astype(BF16)).astype(BF16)
    used = used_ref[...]
    row_i = lax.broadcasted_iota(jnp.int32, (atom_n, atom_n), 0)
    col_i = lax.broadcasted_iota(jnp.int32, (atom_n, atom_n), 1)
    end = jnp.sum(jnp.where(col_i <= row_i, used, 0.0), axis=1, keepdims=True)
    own = jnp.sum(jnp.where(col_i == row_i, used, 0.0), axis=1, keepdims=True)
    total = jnp.sum(used)
    total_ref[0] = total.astype(jnp.int32)
    lane = lax.broadcasted_iota(jnp.int32, (1, lanes), 1)

    def one_block(block):
        place = (lane + block * lanes).astype(F32)
        past = end <= place
        centre = jnp.sum(jnp.where(past, 1.0, 0.0), axis=0, keepdims=True)
        start = jnp.sum(jnp.where(past, own, 0.0), axis=0, keepdims=True)
        slot = (place - start).astype(jnp.int32)
        centre_id = centre.astype(jnp.int32)
        rows = mm(slots_t, one_hot(centre_id, atom_n))
        slot_ids = lax.broadcasted_iota(jnp.int32, (slot_n, lanes), 0)
        neigh = jnp.sum(jnp.where(slot_ids == slot, rows, 0.0), axis=0, keepdims=True)
        valid = place < total
        neigh_ref[pl.ds(block, 1), :] = jnp.where(valid, neigh.astype(jnp.int32), -1)
        centre_ref[pl.ds(block, 1), :] = jnp.where(valid, centre_id, -1)

    def some_blocks(step, carry):
        for more in range(LISTED):
            one_block(step * LISTED + more)
        return carry

    group = LISTED * lanes
    lax.fori_loop(0, (total.astype(jnp.int32) + group - 1) // group, some_blocks, 0)


def list_pairs(used, neighbours):
    blocks = pl.cdiv(neighbours.size, LANES * LISTED) * LISTED
    pairs = jax.ShapeDtypeStruct((blocks, LANES), jnp.int32)
    return pl.pallas_call(
        list_kernel,
        out_shape=[pairs, pairs, jax.ShapeDtypeStruct((1,), jnp.int32)],
        in_specs=[VMEM] * 2,
        out_specs=[VMEM, VMEM, SMEM],
        compiler_params=pltpu.CompilerParams(vmem_limit_bytes=16 * 2**20),
        cost_estimate=pl.CostEstimate(flops=10**9, bytes_accessed=2**16, transcendentals=0),
        name="list_pairs",
    )(used, neighbours)


def prepare_weights(radial_weight, species_embed, env_weight, latent_weight, readout):
    latent, features = env_weight.shape[1:]
    shapes = (
        ((latent, 2 * SPECIES + BASIS_PAD), BF16),
        ((latent + features + BASIS_PAD, latent), BF16),
        ((latent, features), BF16),
        ((latent + features, latent), BF16),
        ((latent, features + BASIS_PAD), BF16),
        ((latent, 128), F32),
        ((BASIS_PAD, latent), BF16),
    )
    operands = [radial_weight, species_embed, readout[None, :], env_weight[0].T, latent_weight[0]]
    return pl.pallas_call(
        weights_kernel,
        out_shape=[jax.ShapeDtypeStruct(*shape) for shape in shapes],
        in_specs=[VMEM] * len(operands),
        out_specs=[VMEM] * len(shapes),
        compiler_params=pltpu.CompilerParams(vmem_limit_bytes=24 * 2**20),
        cost_estimate=pl.CostEstimate(flops=10**9, bytes_accessed=4 * 2**20, transcendentals=0),
        name="prepare_weights",
    )(*operands)


def silu_pair(half_in):
    bent = jnp.tanh(half_in)
    part = half_in * bent
    return half_in + part, (1.0 + bent) * (1.0 + (half_in - part))


def force_kernel(
    total_ref,
    neigh_ref,
    centre_ref,
    moved_ref,
    own_kind_ref,
    into_ref,
    on_hidden_ref,
    on_inner_ref,
    on_bent_ref,
    on_weight_ref,
    readout_ref,
    radial_back_ref,
    in_ref,
    *refs,
    second_call,
    out_ghost_n,
):
    *refs, hot_s, use_s, u_s, slope_s, raw_s, part_s, ain_s, energy_s, c_s, dc_s, f_s = refs
    blocks, lanes = neigh_ref.shape
    atom_n = moved_ref.shape[1]
    ghost_n = out_ghost_n
    ext_n = atom_n + ghost_n * len(DIRECTIONS)
    own_kind = own_kind_ref[...]
    from_owners = [in_ref[place] for place in towards(-1)]
    ghosts = jnp.concatenate(
        [
            jnp.concatenate([owner[:, n * ghost_n : (n + 1) * ghost_n] for owner in from_owners], axis=1)
            for n in range(2)
        ],
        axis=0,
    )
    ghost_kind = ghosts[3:4].astype(jnp.int32)
    if second_call:
        half_ref, send_ref, all_ref, half_two_ref, end_ref, own_out_ref, out_ref = refs
        on_ghosts = []
        for k, (a, b) in enumerate(DIRECTIONS):
            sends = jnp.concatenate(
                [from_owners[k][:, n * ghost_n : (n + 1) * ghost_n] for n in (2, 3)], axis=0
            ).astype(jnp.int32)
            whole = domain_force(all_ref, -a, -b, sends, atom_n)
            picked = mm(split3(padded_rows(whole, 8)), one_hot(sends[k : k + 1], atom_n))
            on_ghosts.append(sum_parts(picked)[0:3])
        _, ghost_pos = step_on(
            ghosts[0:3], ghosts[4:7], ghost_kind, jnp.concatenate(on_ghosts, axis=1)
        )
        whole = domain_force(all_ref, 0, 0, send_ref[...], atom_n)
        half_two, own_pos = step_on(moved_ref[...], half_ref[...], own_kind, whole)
        half_two_ref[...] = half_two
        end_ref[...] = own_pos
    else:
        (out_ref,) = refs
        own_pos, ghost_pos = moved_ref[...], ghosts[0:3]
    kind = jnp.concatenate([own_kind, ghost_kind], axis=1)
    pos = jnp.concatenate([own_pos, ghost_pos], axis=1)
    basis_n = SPECIES
    latent, features = on_inner_ref.shape
    total = total_ref[0]
    full = (total + lanes - 1 - TAIL) // lanes
    scale = COUPLING * SLOTS ** (-0.5)

    pos8 = padded_rows(pos, 8) * (1.0 / RADIUS)
    pos_parts = split3(jnp.concatenate([pos8, -pos8[:, :atom_n]], axis=1))
    row8 = lax.broadcasted_iota(jnp.int32, (SPECIES, ext_n), 0)
    kinds = jnp.where(row8 == kind, 1.0, 0.0)
    basis_in = identity(BASIS_PAD).astype(F32)
    selected = jnp.concatenate(
        [
            jnp.concatenate([kinds, jnp.zeros((SPECIES + BASIS_PAD, ext_n), F32)], axis=0),
            jnp.concatenate(
                [jnp.zeros((SPECIES, atom_n), F32), kinds[:, :atom_n], jnp.zeros((BASIS_PAD, atom_n), F32)], axis=0
            ),
            jnp.concatenate([jnp.zeros((2 * SPECIES, BASIS_PAD), F32), basis_in], axis=0),
        ],
        axis=1,
    )
    weight_in = mm(into_ref[...], selected.astype(BF16)).astype(BF16)

    mid_row = lax.broadcasted_iota(jnp.int32, (BASIS_PAD, lanes), 0).astype(F32)
    mids = (mid_row + 0.5) / basis_n
    sharp = 2.0 * basis_n * basis_n

    c_s[...] = jnp.zeros_like(c_s)
    dc_s[...] = jnp.zeros_like(dc_s)
    f_s[...] = jnp.zeros_like(f_s)

    def each_block(one):
        def step(block, carry):
            one(block, lanes)
            return carry

        lax.fori_loop(0, full, step, 0)
        pl.when(total > full * lanes)(functools.partial(one, full, TAIL))

    def geometry(block, width):
        vec = u_s[block, :, :width]
        square = jnp.sum(vec * vec, axis=0, keepdims=True)
        inside = jnp.maximum(1.0 - square, 0.0)
        inside = jnp.where(centre_ref[pl.ds(block, 1), :width] >= 0, inside, 0.0)
        apart = square - mids[:, :width]
        return vec, inside, apart, jnp.exp(-sharp * apart * apart)

    def staggered(width, begin, finish):
        spans = [slice(at, min(at + GROUP, width)) for at in range(0, width, GROUP)]
        held = begin(spans[0])
        for span, later in zip(spans, spans[1:] + [None]):
            coming = None if later is None else begin(later)
            finish(span, held)
            held = coming

    def first(block, width):
        hot_j = one_hot(neigh_ref[pl.ds(block, 1), :width], ext_n)
        hot_c = one_hot(centre_ref[pl.ds(block, 1), :width], atom_n)
        hot = jnp.concatenate([hot_j, hot_c], axis=0)
        hot_s[block, :, :width] = hot
        u_s[block, :, :width] = sum_parts(mm(pos_parts, hot))
        vec, inside, _, basis = geometry(block, width)
        use = jnp.concatenate([hot_c * vec[k : k + 1].astype(BF16) for k in range(3)], axis=0)
        use_s[block, :, :width] = use
        given = jnp.concatenate([hot, basis.astype(BF16)], axis=0)
        raws = []

        def begin(span):
            return mm(weight_in, given[:, span])

        def finish(span, pre):
            hidden, slope = silu_pair(pre)
            slope_s[block, :, span] = slope.astype(BF16)
            taken = mm(on_hidden_ref[...], hidden.astype(BF16))
            part_s[block, :, span] = taken[:latent]
            raws.append(taken[latent : latent + features])
            raw_s[block, :, span] = raws[-1]
            energy_s[block, :, span] = taken[latent + features : latent + features + 8]

        staggered(width, begin, finish)
        raw = jnp.concatenate(raws, axis=1)
        c_s[...] += mm_nt((raw * (inside * inside)).astype(BF16), use)

    each_block(first)
    c_all = c_s[...] * scale
    c_b = c_all.astype(BF16)

    def second(block, width):
        _, inside, _, _ = geometry(block, width)
        use = use_s[block, :, :width]
        env = inside * inside
        weight = raw_s[block, :, :width] * env
        inner = (weight * mm(c_b, use)).astype(BF16)
        readout = jnp.concatenate([readout_ref[...]] * (GROUP // 128), axis=1)
        a_ins = []

        def begin(span):
            return part_s[block, :, span] + mm(on_inner_ref[...], inner[:, span])

        def finish(span, later):
            gain, bent = silu_pair(later)
            energy_s[block, :, span] += jnp.sum(gain * readout, axis=0, keepdims=True)
            taken = mm(on_bent_ref[...], bent.astype(BF16))
            part_s[block, :, span] = taken[:latent]
            a_ins.append(taken[latent:] * env[:, span])
            ain_s[block, :, span] = a_ins[-1]

        staggered(width, begin, finish)
        a_in = jnp.concatenate(a_ins, axis=1)
        dc_s[...] += mm_nt((a_in * weight).astype(BF16), use)

    each_block(second)
    c_dc = jnp.concatenate([c_all, dc_s[...] * scale], axis=0).astype(BF16)
    both = jnp.concatenate([c_all.T, dc_s[...].T * scale], axis=1).astype(BF16)

    def third(block, width):
        vec, inside, apart, basis = geometry(block, width)
        use = use_s[block, :, :width]
        hot = hot_s[block, :, :width]
        env = inside * inside
        raw = raw_s[block, :, :width]
        weight = raw * env
        a_in = ain_s[block, :, :width]
        along = mm(c_dc, use)
        d_weight = a_in * along[:features] + along[features:]
        d_env = jnp.sum(d_weight * raw, axis=0, keepdims=True) + energy_s[block, 0:1, :width]
        ones = jnp.ones((BASIS_PAD, width), BF16)
        given = jnp.concatenate([d_weight.astype(BF16), ones], axis=0)
        d_bases = []

        def begin(span):
            return part_s[block, :, span] + mm(on_weight_ref[...], given[:, span])

        def finish(span, d_hidden):
            d_pre = (d_hidden * slope_s[block, :, span].astype(F32)).astype(BF16)
            d_bases.append(mm(radial_back_ref[...], d_pre))

        staggered(width, begin, finish)
        d_basis = jnp.concatenate(d_bases, axis=1)
        d_square = env * jnp.sum(d_basis * basis * apart, axis=0, keepdims=True) * (-2.0 * sharp)
        d_square = d_square - 2.0 * inside * d_env
        d_all = mm(both, jnp.concatenate([a_in * weight, weight], axis=0).astype(BF16))
        hot_c = hot[ext_n:].astype(F32)
        picked = [
            jnp.sum(d_all[k * atom_n : (k + 1) * atom_n] * hot_c, axis=0, keepdims=True)
            for k in range(3)
        ]
        d_vec = jnp.concatenate(picked + [jnp.zeros((5, width), F32)], axis=0)
        d_vec = (d_vec + 2.0 * d_square * vec) * (1.0 / RADIUS)
        f_s[...] += mm_nt(split3(d_vec), hot)

    each_block(third)
    summed = f_s[0:8] + f_s[8:16] + f_s[16:24]
    on_centre = summed[0:3, ext_n:]
    on_neigh = summed[0:3, :ext_n]
    own = on_centre - on_neigh[:, :atom_n]
    if second_call:
        own_out_ref[...] = own
        put(out_ref, -on_neigh[:, atom_n:])
    else:
        tile = forces_tile(own, -on_neigh[:, atom_n:])
        out_ref[...] = jnp.broadcast_to(tile[None], out_ref.shape)


def pair_forces(pairs, own_pos, own_kind, weights, incoming, ghost_n, second=()):
    neigh, centre, total = pairs
    blocks, lanes = neigh.shape
    latent, features = weights[2].shape
    atom_n = own_pos.shape[1]
    devices = incoming.shape[0]
    ext_n = atom_n + ghost_n * len(DIRECTIONS)
    operands = [total, neigh, centre, own_pos, own_kind, *weights, incoming, *second]
    if second:
        out_shape = [jax.ShapeDtypeStruct((3, atom_n), F32)] * 3
        out_shape.append(jax.ShapeDtypeStruct((devices, 3, ghost_n), F32))
    else:
        out_shape = [jax.ShapeDtypeStruct((devices, *TILE), F32)]
    pair_rows = blocks * lanes
    return pl.pallas_call(
        functools.partial(force_kernel, second_call=bool(second), out_ghost_n=ghost_n),
        out_shape=out_shape,
        in_specs=[SMEM] + [VMEM] * (len(operands) - 1),
        out_specs=[VMEM] * len(out_shape),
        scratch_shapes=[
            pltpu.VMEM((blocks, ext_n + atom_n, lanes), BF16),
            pltpu.VMEM((blocks, 3 * atom_n, lanes), BF16),
            pltpu.VMEM((blocks, 8, lanes), F32),
            pltpu.VMEM((blocks, latent, lanes), BF16),
            pltpu.VMEM((blocks, features, lanes), F32),
            pltpu.VMEM((blocks, latent, lanes), F32),
            pltpu.VMEM((blocks, features, lanes), F32),
            pltpu.VMEM((blocks, 8, lanes), F32),
            pltpu.VMEM((features, 3 * atom_n), F32),
            pltpu.VMEM((features, 3 * atom_n), F32),
            pltpu.VMEM((24, ext_n + atom_n), F32),
        ],
        compiler_params=pltpu.CompilerParams(vmem_limit_bytes=48 * 2**20),
        cost_estimate=pl.CostEstimate(
            flops=pair_rows * latent * 2700, bytes_accessed=4 * 2**20, transcendentals=0
        ),
        name="pair_forces",
    )(*operands)


def small_call(kernel, name, operands, out_shape, smem_n=0):
    return pl.pallas_call(
        kernel,
        out_shape=out_shape,
        in_specs=[SMEM] * smem_n + [VMEM] * (len(operands) - smem_n),
        out_specs=[VMEM] * len(out_shape),
        compiler_params=pltpu.CompilerParams(vmem_limit_bytes=16 * 2**20),
        name=name,
    )(*operands)


def devices_at(shift_gx, shift_yz):
    gx_n, yz_n = lax.axis_size("gx"), lax.axis_size("yz")
    gx = (lax.axis_index("gx") + jnp.asarray(shift_gx, jnp.int32) + gx_n) % gx_n
    yz = (lax.axis_index("yz") + jnp.asarray(shift_yz, jnp.int32) + yz_n) % yz_n
    return gx * yz_n + yz


def exchange(blocks):
    return lax.all_to_all(blocks, ("gx", "yz"), 0, 0, tiled=True)


def body(
    positions,
    velocities,
    forces_start,
    species,
    live_atoms,
    send_list,
    neighbours,
    neighbour_count,
    radial_weight,
    species_embed,
    env_weight,
    latent_weight,
    readout,
):
    atom_n = positions.shape[1]
    ghost_n = send_list.shape[1]
    devices = lax.axis_size("gx") * lax.axis_size("yz")
    atoms = jax.ShapeDtypeStruct((3, atom_n), F32)

    kinds = species.reshape(1, atom_n)
    ahead = devices_at([a for a, _ in DIRECTIONS], [b for _, b in DIRECTIONS])
    moved, half, used, sent = small_call(
        start_kernel,
        "start",
        [
            ahead,
            positions,
            velocities,
            forces_start,
            kinds,
            live_atoms,
            neighbour_count.reshape(1, atom_n),
            send_list,
        ],
        [atoms, atoms, jax.ShapeDtypeStruct((1, atom_n), F32), jax.ShapeDtypeStruct((devices, *TILE), F32)],
        smem_n=1,
    )
    got = exchange(sent)
    pairs = list_pairs(used, neighbours)
    weights = prepare_weights(radial_weight, species_embed, env_weight, latent_weight, readout)
    (sent,) = pair_forces(pairs, moved, kinds, weights, got, ghost_n)
    every = exchange(sent)
    half_two, positions_end, own, sent = pair_forces(
        pairs, moved, kinds, weights, got, ghost_n, (half, send_list, every)
    )
    back = exchange(sent)
    velocities_end, forces_end = small_call(
        last_kernel, "last", [own, send_list, half_two, kinds, back], [atoms, atoms]
    )
    return (positions_end, velocities_end, forces_end)


def solution(mesh):
    placed = (
        P(None, ("gx", "yz")),
        P(None, ("gx", "yz")),
        P(None, ("gx", "yz")),
        P(("gx", "yz")),
        P(("gx", "yz")),
        P(None, ("gx", "yz")),
        P(("gx", "yz"), None),
        P(("gx", "yz")),
        P(),
        P(),
        P(),
        P(),
        P(),
    )
    return jax.shard_map(
        body,
        mesh=mesh,
        in_specs=placed,
        out_specs=(P(None, ("gx", "yz")), P(None, ("gx", "yz")), P(None, ("gx", "yz"))),
        check_vma=False,
    )
```

```python
import functools

import jax
import jax.numpy as jnp
from jax import lax
from jax.experimental import pallas as pl
from jax.experimental.pallas import tpu as pltpu
from jax.sharding import PartitionSpec as P

SPECIES = 8
SLOTS = 128
RADIUS = 6.0
STEP = 0.25
COUPLING = 4.0
MASSES = (1.008, 12.011, 14.007, 15.999, 32.06, 22.99, 35.45, 30.97)

LANES = 1024
TAIL = 768
LISTED = 2
DIRECTIONS = ((-1, -1), (-1, 0), (-1, 1), (0, -1), (0, 1), (1, -1), (1, 0), (1, 1))
TILE = (4, 128)
BASIS_PAD = 16

F32 = jnp.float32
BF16 = jnp.bfloat16


def mm(left, right):
    return jnp.dot(left, right, preferred_element_type=F32)


def mm_nt(left, right):
    return lax.dot_general(left, right, (((1,), (1,)), ((), ())), preferred_element_type=F32)


def split3(values):
    high = values.astype(BF16)
    rest = values - high.astype(F32)
    mid = rest.astype(BF16)
    low = (rest - mid.astype(F32)).astype(BF16)
    return jnp.concatenate([high.astype(F32), mid.astype(F32), low.astype(F32)], axis=0).astype(BF16)


def lane_table(values):
    rows, lanes = values.shape
    return jnp.concatenate([values, jnp.zeros((rows, 128 - lanes), F32)], axis=1)


def look_up(table, ids):
    inside = jnp.minimum(jnp.maximum(ids, 0), 127)
    found = []
    for at in range(0, ids.shape[1], 128):
        index = jnp.broadcast_to(inside[:, at : at + 128], table.shape)
        found.append(jnp.take_along_axis(table, index, axis=1, mode="promise_in_bounds"))
    return jnp.concatenate(found, axis=1)


def one_hot(ids, rows):
    row_ids = lax.broadcasted_iota(jnp.int32, (rows, ids.shape[1]), 0)
    return jnp.where(row_ids == ids, 1.0, 0.0).astype(BF16)


SMEM = pl.BlockSpec(memory_space=pltpu.SMEM)
VMEM = pl.BlockSpec(memory_space=pltpu.VMEM)


def identity(size):
    row = lax.broadcasted_iota(jnp.int32, (size, size), 0)
    col = lax.broadcasted_iota(jnp.int32, (size, size), 1)
    return jnp.where(row == col, 1.0, 0.0).astype(BF16)


def padded_rows(values, rows):
    have, lanes = values.shape
    return jnp.concatenate([values, jnp.zeros((rows - have, lanes), values.dtype)], axis=0)


def sum_parts(parts):
    rows = parts.shape[0] // 3
    return parts[:rows] + parts[rows : 2 * rows] + parts[2 * rows :]


def by_direction(rows):
    return jnp.concatenate([rows[k : k + 1] for k in range(len(DIRECTIONS))], axis=1)


def device_at(shift_gx, shift_yz):
    gx_n, yz_n = lax.axis_size("gx"), lax.axis_size("yz")
    gx = lax.rem(lax.axis_index("gx") + (shift_gx % gx_n), gx_n)
    yz = lax.rem(lax.axis_index("yz") + (shift_yz % yz_n), yz_n)
    return gx * yz_n + yz


def towards(sign):
    return [device_at(sign * a, sign * b) for a, b in DIRECTIONS]


def put(out_ref, blocks):
    places = towards(-1)
    ghost_n = blocks.shape[1] // len(DIRECTIONS)
    out_ref[...] = jnp.zeros_like(out_ref)
    for k in range(len(DIRECTIONS)):
        out_ref[places[k]] = blocks[:, k * ghost_n : (k + 1) * ghost_n]


def take(in_ref):
    return jnp.concatenate([in_ref[place] for place in towards(1)], axis=1)


def inverse_mass(species):
    inverse = jnp.zeros(species.shape, F32)
    for spec_id, mass in enumerate(MASSES):
        inverse = jnp.where(species == spec_id, F32(1.0 / mass), inverse)
    return inverse


def start_kernel(
    ahead_ref,
    pos_ref,
    vel_ref,
    force_ref,
    species_ref,
    live_ref,
    count_ref,
    send_ref,
    moved_ref,
    half_ref,
    used_ref,
    out_ref,
):
    species = species_ref[...]
    slot = lax.broadcasted_iota(jnp.int32, species.shape, 1)
    used_ref[...] = jnp.where(slot < live_ref[...].reshape(1, 1), count_ref[...], 0).astype(F32)
    half = vel_ref[...] + 0.5 * STEP * inverse_mass(species) * force_ref[...]
    moved = pos_ref[...] + STEP * half
    half_ref[...] = half
    moved_ref[...] = moved
    spare = jnp.zeros((1, species.shape[1]), F32)
    sources = split3(jnp.concatenate([moved, species.astype(F32), half, spare], axis=0))
    sends = send_ref[...]
    picked = sum_parts(mm(sources, one_hot(by_direction(sends), species.shape[1])))
    sent = sends.astype(F32)
    ghost_n = sent.shape[1]
    rest = jnp.zeros((TILE[0], TILE[1] - 4 * ghost_n), F32)
    out_ref[...] = jnp.zeros_like(out_ref)
    for k in range(len(DIRECTIONS)):
        block = picked[:, k * ghost_n : (k + 1) * ghost_n]
        out_ref[ahead_ref[k]] = jnp.concatenate([block[:4], block[4:], sent[:4], sent[4:], rest], axis=1)


def total_force(own, back, sends):
    pick = one_hot(by_direction(sends), own.shape[1])
    return own + sum_parts(mm_nt(split3(padded_rows(back, 8)), pick))[0:3]


def forces_tile(own, on_ghosts):
    room = TILE[1] - on_ghosts.shape[1]
    upper = jnp.concatenate([on_ghosts, own[:, :room]], axis=1)
    last = [own[c : c + 1, room:] for c in range(3)]
    last.append(jnp.zeros((1, TILE[1] - 3 * (own.shape[1] - room)), F32))
    return jnp.concatenate([upper, jnp.concatenate(last, axis=1)], axis=0)


def domain_force(all_ref, shift_gx, shift_yz, sends, atom_n):
    ghost_n = sends.shape[1]
    back = []
    for k, (a, b) in enumerate(DIRECTIONS):
        place = device_at(shift_gx + a, shift_yz + b)
        back.append(all_ref[place][0:3, k * ghost_n : (k + 1) * ghost_n])
    tile = all_ref[device_at(shift_gx, shift_yz)]
    room = TILE[1] - len(DIRECTIONS) * ghost_n
    over = atom_n - room
    last = jnp.concatenate([tile[3:4, c * over : (c + 1) * over] for c in range(3)], axis=0)
    own = jnp.concatenate([tile[0:3, TILE[1] - room :], last], axis=1)
    return total_force(own, jnp.concatenate(back, axis=1), sends)


def step_on(moved, half, kinds, forces):
    kick = 0.5 * STEP * inverse_mass(kinds) * forces
    half_two = half + kick + kick
    return half_two, moved + STEP * half_two


def last_kernel(own_ref, send_ref, half_two_ref, species_ref, in_ref, vel_ref, force_ref):
    forces = total_force(own_ref[...], take(in_ref), send_ref[...])
    force_ref[...] = forces
    vel_ref[...] = half_two_ref[...] + 0.5 * STEP * inverse_mass(species_ref[...]) * forces


def weights_kernel(
    radial_ref,
    embed_ref,
    readout_ref,
    env_t_ref,
    latent_ref,
    into_ref,
    on_hidden_ref,
    on_inner_ref,
    on_bent_ref,
    on_weight_ref,
    readout_t_ref,
    radial_back_ref,
):
    latent = latent_ref.shape[1]
    eye = identity(latent)
    half = BF16(0.5)
    latent_w = latent_ref[...]
    readout = readout_ref[...]
    none = jnp.zeros((BASIS_PAD - 8, latent), BF16)
    readout16 = padded_rows(readout.astype(F32), BASIS_PAD).astype(BF16)
    radial16 = jnp.concatenate([radial_ref[...] * half, none], axis=0)
    latent_t = mm_nt(eye, latent_w * half).astype(BF16)
    on_hidden_ref[...] = jnp.concatenate([latent_t[:, :latent], env_t_ref[...], readout16], axis=0)
    on_inner_ref[...] = latent_t[:, latent:]
    on_bent_ref[...] = (latent_w.astype(F32) * (0.5 * readout.astype(F32))).astype(BF16)
    on_weight_ref[...] = mm_nt(eye, jnp.concatenate([env_t_ref[...], readout16], axis=0)).astype(BF16)
    readout_t_ref[...] = mm_nt(eye, jnp.broadcast_to(readout.astype(F32), (128, latent)).astype(BF16))
    radial_back_ref[...] = radial16
    into = jnp.concatenate([embed_ref[1] * half, embed_ref[0] * half, radial16], axis=0)
    into_ref[...] = mm_nt(eye, into).astype(BF16)


def list_kernel(used_ref, slots_ref, neigh_ref, centre_ref, total_ref):
    atom_n, slot_n = slots_ref.shape
    blocks, lanes = neigh_ref.shape
    slots_t = mm_nt(identity(slot_n), slots_ref[...].astype(F32).astype(BF16)).astype(BF16)
    used = used_ref[...]
    row_i = lax.broadcasted_iota(jnp.int32, (atom_n, atom_n), 0)
    col_i = lax.broadcasted_iota(jnp.int32, (atom_n, atom_n), 1)
    end = jnp.sum(jnp.where(col_i <= row_i, used, 0.0), axis=1, keepdims=True)
    own = jnp.sum(jnp.where(col_i == row_i, used, 0.0), axis=1, keepdims=True)
    total = jnp.sum(used)
    total_ref[0] = total.astype(jnp.int32)
    lane = lax.broadcasted_iota(jnp.int32, (1, lanes), 1)

    def one_block(block):
        place = (lane + block * lanes).astype(F32)
        past = end <= place
        centre = jnp.sum(jnp.where(past, 1.0, 0.0), axis=0, keepdims=True)
        start = jnp.sum(jnp.where(past, own, 0.0), axis=0, keepdims=True)
        slot = (place - start).astype(jnp.int32)
        centre_id = centre.astype(jnp.int32)
        rows = mm(slots_t, one_hot(centre_id, atom_n))
        slot_ids = lax.broadcasted_iota(jnp.int32, (slot_n, lanes), 0)
        neigh = jnp.sum(jnp.where(slot_ids == slot, rows, 0.0), axis=0, keepdims=True)
        valid = place < total
        neigh_ref[pl.ds(block, 1), :] = jnp.where(valid, neigh.astype(jnp.int32), -1)
        centre_ref[pl.ds(block, 1), :] = jnp.where(valid, centre_id, -1)

    def some_blocks(step, carry):
        for more in range(LISTED):
            one_block(step * LISTED + more)
        return carry

    group = LISTED * lanes
    lax.fori_loop(0, (total.astype(jnp.int32) + group - 1) // group, some_blocks, 0)


def list_pairs(used, neighbours):
    blocks = pl.cdiv(neighbours.size, LANES * LISTED) * LISTED
    pairs = jax.ShapeDtypeStruct((blocks, LANES), jnp.int32)
    return pl.pallas_call(
        list_kernel,
        out_shape=[pairs, pairs, jax.ShapeDtypeStruct((1,), jnp.int32)],
        in_specs=[VMEM] * 2,
        out_specs=[VMEM, VMEM, SMEM],
        compiler_params=pltpu.CompilerParams(vmem_limit_bytes=16 * 2**20),
        cost_estimate=pl.CostEstimate(flops=10**9, bytes_accessed=2**16, transcendentals=0),
        name="list_pairs",
    )(used, neighbours)


def prepare_weights(radial_weight, species_embed, env_weight, latent_weight, readout):
    latent, features = env_weight.shape[1:]
    shapes = (
        ((latent, 2 * SPECIES + BASIS_PAD), BF16),
        ((latent + features + BASIS_PAD, latent), BF16),
        ((latent, features), BF16),
        ((latent + features, latent), BF16),
        ((latent, features + BASIS_PAD), BF16),
        ((latent, 128), F32),
        ((BASIS_PAD, latent), BF16),
    )
    operands = [radial_weight, species_embed, readout[None, :], env_weight[0].T, latent_weight[0]]
    return pl.pallas_call(
        weights_kernel,
        out_shape=[jax.ShapeDtypeStruct(*shape) for shape in shapes],
        in_specs=[VMEM] * len(operands),
        out_specs=[VMEM] * len(shapes),
        compiler_params=pltpu.CompilerParams(vmem_limit_bytes=24 * 2**20),
        cost_estimate=pl.CostEstimate(flops=10**9, bytes_accessed=4 * 2**20, transcendentals=0),
        name="prepare_weights",
    )(*operands)


def silu_pair(half_in):
    bent = jnp.tanh(half_in)
    part = half_in * bent
    return half_in + part, (1.0 + bent) * (1.0 + (half_in - part))


def force_kernel(
    total_ref,
    neigh_ref,
    centre_ref,
    moved_ref,
    own_kind_ref,
    into_ref,
    on_hidden_ref,
    on_inner_ref,
    on_bent_ref,
    on_weight_ref,
    readout_ref,
    radial_back_ref,
    in_ref,
    *refs,
    second_call,
    out_ghost_n,
):
    *refs, hot_s, use_s, u_s, slope_s, raw_s, part_s, ain_s, energy_s, c_s, dc_s, f_s = refs
    blocks, lanes = neigh_ref.shape
    atom_n = moved_ref.shape[1]
    ghost_n = out_ghost_n
    ext_n = atom_n + ghost_n * len(DIRECTIONS)
    own_kind = own_kind_ref[...]
    from_owners = [in_ref[place] for place in towards(-1)]
    ghosts = jnp.concatenate(
        [
            jnp.concatenate([owner[:, n * ghost_n : (n + 1) * ghost_n] for owner in from_owners], axis=1)
            for n in range(2)
        ],
        axis=0,
    )
    ghost_kind = ghosts[3:4].astype(jnp.int32)
    if second_call:
        half_ref, send_ref, all_ref, half_two_ref, end_ref, own_out_ref, out_ref = refs
        sends, wholes = [], []
        for k, (a, b) in enumerate(DIRECTIONS):
            rows = [from_owners[k][:, n * ghost_n : (n + 1) * ghost_n] for n in (2, 3)]
            sends.append(jnp.concatenate(rows, axis=0).astype(jnp.int32))
            wholes.append(domain_force(all_ref, -a, -b, sends[k], atom_n))
        own_whole = domain_force(all_ref, 0, 0, send_ref[...], atom_n)
        on_ghosts = [
            sum_parts(mm(split3(padded_rows(whole, 8)), one_hot(sends[k][k : k + 1], atom_n)))[0:3]
            for k, whole in enumerate(wholes)
        ]
        _, ghost_pos = step_on(
            ghosts[0:3], ghosts[4:7], ghost_kind, jnp.concatenate(on_ghosts, axis=1)
        )
        half_two, own_pos = step_on(moved_ref[...], half_ref[...], own_kind, own_whole)
        half_two_ref[...] = half_two
        end_ref[...] = own_pos
    else:
        (out_ref,) = refs
        own_pos, ghost_pos = moved_ref[...], ghosts[0:3]
    kind = jnp.concatenate([own_kind, ghost_kind], axis=1)
    basis_n = SPECIES
    latent, features = on_inner_ref.shape
    total = total_ref[0]
    full = (total + lanes - 1 - TAIL) // lanes
    scale = COUPLING * SLOTS ** (-0.5)

    own_table = lane_table(padded_rows(own_pos, 8) * (1.0 / RADIUS))
    ghost_table = lane_table(padded_rows(ghost_pos, 8) * (1.0 / RADIUS))
    row8 = lax.broadcasted_iota(jnp.int32, (SPECIES, ext_n), 0)
    kinds = jnp.where(row8 == kind, 1.0, 0.0)
    basis_in = identity(BASIS_PAD).astype(F32)
    selected = jnp.concatenate(
        [
            jnp.concatenate([kinds, jnp.zeros((SPECIES + BASIS_PAD, ext_n), F32)], axis=0),
            jnp.concatenate(
                [jnp.zeros((SPECIES, atom_n), F32), kinds[:, :atom_n], jnp.zeros((BASIS_PAD, atom_n), F32)], axis=0
            ),
            jnp.concatenate([jnp.zeros((2 * SPECIES, BASIS_PAD), F32), basis_in], axis=0),
        ],
        axis=1,
    )
    weight_in = mm(into_ref[...], selected.astype(BF16)).astype(BF16)

    mid_row = lax.broadcasted_iota(jnp.int32, (BASIS_PAD, lanes), 0).astype(F32)
    mids = (mid_row + 0.5) / basis_n
    sharp = 2.0 * basis_n * basis_n

    c_s[...] = jnp.zeros_like(c_s)
    dc_s[...] = jnp.zeros_like(dc_s)
    f_s[...] = jnp.zeros_like(f_s)

    def each_block(one):
        def step(block, carry):
            one(block, lanes)
            return carry

        lax.fori_loop(0, full, step, 0)
        pl.when(total > full * lanes)(functools.partial(one, full, TAIL))

    def geometry(block, width):
        vec = u_s[block, :, :width]
        square = jnp.sum(vec * vec, axis=0, keepdims=True)
        inside = jnp.maximum(1.0 - square, 0.0)
        inside = jnp.where(centre_ref[pl.ds(block, 1), :width] >= 0, inside, 0.0)
        apart = square - mids[:, :width]
        return vec, inside, apart, jnp.exp(-sharp * apart * apart)

    def first(block, width):
        neigh = neigh_ref[pl.ds(block, 1), :width]
        centre = centre_ref[pl.ds(block, 1), :width]
        hot_c = one_hot(centre, atom_n)
        hot = jnp.concatenate([one_hot(neigh, ext_n), hot_c], axis=0)
        hot_s[block, :, :width] = hot
        there = jnp.where(
            neigh < atom_n, look_up(own_table, neigh), look_up(ghost_table, neigh - atom_n)
        )
        u_s[block, :, :width] = there - look_up(own_table, centre)
        vec, inside, _, basis = geometry(block, width)
        use = jnp.concatenate([hot_c * vec[k : k + 1].astype(BF16) for k in range(3)], axis=0)
        use_s[block, :, :width] = use
        pre = mm(weight_in, jnp.concatenate([hot, basis.astype(BF16)], axis=0))
        hidden, slope = silu_pair(pre)
        slope_s[block, :, :width] = slope.astype(BF16)
        taken = mm(on_hidden_ref[...], hidden.astype(BF16))
        part_s[block, :, :width] = taken[:latent]
        raw = taken[latent : latent + features]
        raw_s[block, :, :width] = raw
        energy_s[block, :, :width] = taken[latent + features : latent + features + 8]
        c_s[...] += mm_nt((raw * (inside * inside)).astype(BF16), use)

    each_block(first)
    c_all = c_s[...] * scale
    c_b = c_all.astype(BF16)

    def second(block, width):
        _, inside, _, _ = geometry(block, width)
        use = use_s[block, :, :width]
        env = inside * inside
        weight = raw_s[block, :, :width] * env
        inner = weight * mm(c_b, use)
        later = part_s[block, :, :width] + mm(on_inner_ref[...], inner.astype(BF16))
        gain, bent = silu_pair(later)
        readout = jnp.concatenate([readout_ref[...]] * (width // 128), axis=1)
        energy_s[block, :, :width] += jnp.sum(gain * readout, axis=0, keepdims=True)
        taken = mm(on_bent_ref[...], bent.astype(BF16))
        part_s[block, :, :width] = taken[:latent]
        a_in = taken[latent:] * env
        ain_s[block, :, :width] = a_in
        dc_s[...] += mm_nt((a_in * weight).astype(BF16), use)

    each_block(second)
    c_dc = jnp.concatenate([c_all, dc_s[...] * scale], axis=0).astype(BF16)
    both = jnp.concatenate([c_all.T, dc_s[...].T * scale], axis=1).astype(BF16)

    def third(block, width):
        vec, inside, apart, basis = geometry(block, width)
        use = use_s[block, :, :width]
        hot = hot_s[block, :, :width]
        env = inside * inside
        raw = raw_s[block, :, :width]
        weight = raw * env
        a_in = ain_s[block, :, :width]
        along = mm(c_dc, use)
        d_weight = a_in * along[:features] + along[features:]
        d_env = jnp.sum(d_weight * raw, axis=0, keepdims=True) + energy_s[block, :, :width][0:1]
        ones = jnp.ones((BASIS_PAD, width), BF16)
        d_hidden = part_s[block, :, :width] + mm(
            on_weight_ref[...], jnp.concatenate([d_weight.astype(BF16), ones], axis=0)
        )
        d_pre = (d_hidden * slope_s[block, :, :width].astype(F32)).astype(BF16)
        d_basis = mm(radial_back_ref[...], d_pre)
        d_square = env * jnp.sum(d_basis * basis * apart, axis=0, keepdims=True) * (-2.0 * sharp)
        d_square = d_square - 2.0 * inside * d_env
        d_all = mm(both, jnp.concatenate([a_in * weight, weight], axis=0).astype(BF16))
        hot_c = hot[ext_n:].astype(F32)
        picked = [
            jnp.sum(d_all[k * atom_n : (k + 1) * atom_n] * hot_c, axis=0, keepdims=True)
            for k in range(3)
        ]
        d_vec = jnp.concatenate(picked + [jnp.zeros((5, width), F32)], axis=0)
        d_vec = (d_vec + 2.0 * d_square * vec) * (1.0 / RADIUS)
        f_s[...] += mm_nt(split3(d_vec), hot)

    each_block(third)
    summed = f_s[0:8] + f_s[8:16] + f_s[16:24]
    on_centre = summed[0:3, ext_n:]
    on_neigh = summed[0:3, :ext_n]
    own = on_centre - on_neigh[:, :atom_n]
    if second_call:
        own_out_ref[...] = own
        put(out_ref, -on_neigh[:, atom_n:])
    else:
        tile = forces_tile(own, -on_neigh[:, atom_n:])
        out_ref[...] = jnp.broadcast_to(tile[None], out_ref.shape)


def pair_forces(pairs, own_pos, own_kind, weights, incoming, ghost_n, second=()):
    neigh, centre, total = pairs
    blocks, lanes = neigh.shape
    latent, features = weights[2].shape
    atom_n = own_pos.shape[1]
    devices = incoming.shape[0]
    ext_n = atom_n + ghost_n * len(DIRECTIONS)
    operands = [total, neigh, centre, own_pos, own_kind, *weights, incoming, *second]
    if second:
        out_shape = [jax.ShapeDtypeStruct((3, atom_n), F32)] * 3
        out_shape.append(jax.ShapeDtypeStruct((devices, 3, ghost_n), F32))
    else:
        out_shape = [jax.ShapeDtypeStruct((devices, *TILE), F32)]
    pair_rows = blocks * lanes
    return pl.pallas_call(
        functools.partial(force_kernel, second_call=bool(second), out_ghost_n=ghost_n),
        out_shape=out_shape,
        in_specs=[SMEM] + [VMEM] * (len(operands) - 1),
        out_specs=[VMEM] * len(out_shape),
        scratch_shapes=[
            pltpu.VMEM((blocks, ext_n + atom_n, lanes), BF16),
            pltpu.VMEM((blocks, 3 * atom_n, lanes), BF16),
            pltpu.VMEM((blocks, 8, lanes), F32),
            pltpu.VMEM((blocks, latent, lanes), BF16),
            pltpu.VMEM((blocks, features, lanes), F32),
            pltpu.VMEM((blocks, latent, lanes), F32),
            pltpu.VMEM((blocks, features, lanes), F32),
            pltpu.VMEM((blocks, 8, lanes), F32),
            pltpu.VMEM((features, 3 * atom_n), F32),
            pltpu.VMEM((features, 3 * atom_n), F32),
            pltpu.VMEM((24, ext_n + atom_n), F32),
        ],
        compiler_params=pltpu.CompilerParams(vmem_limit_bytes=48 * 2**20),
        cost_estimate=pl.CostEstimate(
            flops=pair_rows * latent * 2700, bytes_accessed=4 * 2**20, transcendentals=0
        ),
        name="pair_forces",
    )(*operands)


def small_call(kernel, name, operands, out_shape, smem_n=0):
    return pl.pallas_call(
        kernel,
        out_shape=out_shape,
        in_specs=[SMEM] * smem_n + [VMEM] * (len(operands) - smem_n),
        out_specs=[VMEM] * len(out_shape),
        compiler_params=pltpu.CompilerParams(vmem_limit_bytes=16 * 2**20),
        name=name,
    )(*operands)


def devices_at(shift_gx, shift_yz):
    gx_n, yz_n = lax.axis_size("gx"), lax.axis_size("yz")
    gx = (lax.axis_index("gx") + jnp.asarray(shift_gx, jnp.int32) + gx_n) % gx_n
    yz = (lax.axis_index("yz") + jnp.asarray(shift_yz, jnp.int32) + yz_n) % yz_n
    return gx * yz_n + yz


def exchange(blocks):
    return lax.all_to_all(blocks, ("gx", "yz"), 0, 0, tiled=True)


def body(
    positions,
    velocities,
    forces_start,
    species,
    live_atoms,
    send_list,
    neighbours,
    neighbour_count,
    radial_weight,
    species_embed,
    env_weight,
    latent_weight,
    readout,
):
    atom_n = positions.shape[1]
    ghost_n = send_list.shape[1]
    devices = lax.axis_size("gx") * lax.axis_size("yz")
    atoms = jax.ShapeDtypeStruct((3, atom_n), F32)

    kinds = species.reshape(1, atom_n)
    ahead = devices_at([a for a, _ in DIRECTIONS], [b for _, b in DIRECTIONS])
    moved, half, used, sent = small_call(
        start_kernel,
        "start",
        [
            ahead,
            positions,
            velocities,
            forces_start,
            kinds,
            live_atoms,
            neighbour_count.reshape(1, atom_n),
            send_list,
        ],
        [atoms, atoms, jax.ShapeDtypeStruct((1, atom_n), F32), jax.ShapeDtypeStruct((devices, *TILE), F32)],
        smem_n=1,
    )
    got = exchange(sent)
    pairs = list_pairs(used, neighbours)
    weights = prepare_weights(radial_weight, species_embed, env_weight, latent_weight, readout)
    (sent,) = pair_forces(pairs, moved, kinds, weights, got, ghost_n)
    every = exchange(sent)
    half_two, positions_end, own, sent = pair_forces(
        pairs, moved, kinds, weights, got, ghost_n, (half, send_list, every)
    )
    back = exchange(sent)
    velocities_end, forces_end = small_call(
        last_kernel, "last", [own, send_list, half_two, kinds, back], [atoms, atoms]
    )
    return (positions_end, velocities_end, forces_end)


def solution(mesh):
    placed = (
        P(None, ("gx", "yz")),
        P(None, ("gx", "yz")),
        P(None, ("gx", "yz")),
        P(("gx", "yz")),
        P(("gx", "yz")),
        P(None, ("gx", "yz")),
        P(("gx", "yz"), None),
        P(("gx", "yz")),
        P(),
        P(),
        P(),
        P(),
        P(),
    )
    return jax.shard_map(
        body,
        mesh=mesh,
        in_specs=placed,
        out_specs=(P(None, ("gx", "yz")), P(None, ("gx", "yz")), P(None, ("gx", "yz"))),
        check_vma=False,
    )
```

```python
import functools

import jax
import jax.numpy as jnp
from jax import lax
from jax.experimental import pallas as pl
from jax.experimental.pallas import tpu as pltpu
from jax.sharding import PartitionSpec as P

SPECIES = 8
SLOTS = 128
RADIUS = 6.0
STEP = 0.25
COUPLING = 4.0
MASSES = (1.008, 12.011, 14.007, 15.999, 32.06, 22.99, 35.45, 30.97)

LANES = 1024
TAIL = 768
LISTED = 2
DIRECTIONS = ((-1, -1), (-1, 0), (-1, 1), (0, -1), (0, 1), (1, -1), (1, 0), (1, 1))
TILE = (4, 128)
BASIS_PAD = 16

F32 = jnp.float32
BF16 = jnp.bfloat16


def mm(left, right):
    return jnp.dot(left, right, preferred_element_type=F32)


def mm_nt(left, right):
    return lax.dot_general(left, right, (((1,), (1,)), ((), ())), preferred_element_type=F32)


def split3(values):
    high = values.astype(BF16)
    rest = values - high.astype(F32)
    mid = rest.astype(BF16)
    low = (rest - mid.astype(F32)).astype(BF16)
    return jnp.concatenate([high.astype(F32), mid.astype(F32), low.astype(F32)], axis=0).astype(BF16)


def lane_table(values):
    rows, lanes = values.shape
    return jnp.concatenate([values, jnp.zeros((rows, 128 - lanes), F32)], axis=1)


def look_up(table, ids):
    inside = jnp.minimum(jnp.maximum(ids, 0), 127)
    found = []
    for at in range(0, ids.shape[1], 128):
        index = jnp.broadcast_to(inside[:, at : at + 128], table.shape)
        found.append(jnp.take_along_axis(table, index, axis=1, mode="promise_in_bounds"))
    return jnp.concatenate(found, axis=1)


def one_hot(ids, rows):
    row_ids = lax.broadcasted_iota(jnp.int32, (rows, ids.shape[1]), 0)
    return jnp.where(row_ids == ids, 1.0, 0.0).astype(BF16)


VMEM = pl.BlockSpec(memory_space=pltpu.VMEM)


def identity(size):
    row = lax.broadcasted_iota(jnp.int32, (size, size), 0)
    col = lax.broadcasted_iota(jnp.int32, (size, size), 1)
    return jnp.where(row == col, 1.0, 0.0).astype(BF16)


def padded_rows(values, rows):
    have, lanes = values.shape
    return jnp.concatenate([values, jnp.zeros((rows - have, lanes), values.dtype)], axis=0)


def sum_parts(parts):
    rows = parts.shape[0] // 3
    return parts[:rows] + parts[rows : 2 * rows] + parts[2 * rows :]


def by_direction(rows):
    return jnp.concatenate([rows[k : k + 1] for k in range(len(DIRECTIONS))], axis=1)


def device_at(shift_gx, shift_yz):
    gx_n, yz_n = lax.axis_size("gx"), lax.axis_size("yz")
    gx = lax.rem(lax.axis_index("gx") + (shift_gx % gx_n), gx_n)
    yz = lax.rem(lax.axis_index("yz") + (shift_yz % yz_n), yz_n)
    return gx * yz_n + yz


def towards(sign):
    return [device_at(sign * a, sign * b) for a, b in DIRECTIONS]


def put(out_ref, blocks):
    places = towards(-1)
    ghost_n = blocks.shape[1] // len(DIRECTIONS)
    out_ref[...] = jnp.zeros_like(out_ref)
    for k in range(len(DIRECTIONS)):
        out_ref[places[k]] = blocks[:, k * ghost_n : (k + 1) * ghost_n]


def take(in_ref):
    return jnp.concatenate([in_ref[place] for place in towards(1)], axis=1)


def inverse_mass(species):
    inverse = jnp.zeros(species.shape, F32)
    for spec_id, mass in enumerate(MASSES):
        inverse = jnp.where(species == spec_id, F32(1.0 / mass), inverse)
    return inverse


def start_kernel(
    _,
    pos_ref,
    vel_ref,
    force_ref,
    species_ref,
    live_ref,
    count_ref,
    send_ref,
    moved_ref,
    half_ref,
    used_ref,
    out_ref,
):
    species = species_ref[...]
    slot = lax.broadcasted_iota(jnp.int32, species.shape, 1)
    used_ref[...] = jnp.where(slot < live_ref[...].reshape(1, 1), count_ref[...], 0).astype(F32)
    half = vel_ref[...] + 0.5 * STEP * inverse_mass(species) * force_ref[...]
    moved = pos_ref[...] + STEP * half
    half_ref[...] = half
    moved_ref[...] = moved
    spare = jnp.zeros((1, species.shape[1]), F32)
    sources = split3(jnp.concatenate([moved, species.astype(F32), half, spare], axis=0))
    sends = send_ref[...]
    picked = sum_parts(mm(sources, one_hot(by_direction(sends), species.shape[1])))
    sent = sends.astype(F32)
    ghost_n = sent.shape[1]
    rest = jnp.zeros((TILE[0], TILE[1] - 4 * ghost_n), F32)
    out_ref[...] = jnp.zeros_like(out_ref)
    for k, place in enumerate(towards(1)):
        block = picked[:, k * ghost_n : (k + 1) * ghost_n]
        out_ref[place] = jnp.concatenate([block[:4], block[4:], sent[:4], sent[4:], rest], axis=1)


def total_force(own, back, sends):
    pick = one_hot(by_direction(sends), own.shape[1])
    return own + sum_parts(mm_nt(split3(padded_rows(back, 8)), pick))[0:3]


def forces_tile(own, on_ghosts):
    room = TILE[1] - on_ghosts.shape[1]
    upper = jnp.concatenate([on_ghosts, own[:, :room]], axis=1)
    last = [own[c : c + 1, room:] for c in range(3)]
    last.append(jnp.zeros((1, TILE[1] - 3 * (own.shape[1] - room)), F32))
    return jnp.concatenate([upper, jnp.concatenate(last, axis=1)], axis=0)


def domain_force(all_ref, shift_gx, shift_yz, sends, atom_n):
    ghost_n = sends.shape[1]
    back = []
    for k, (a, b) in enumerate(DIRECTIONS):
        place = device_at(shift_gx + a, shift_yz + b)
        back.append(all_ref[place][0:3, k * ghost_n : (k + 1) * ghost_n])
    tile = all_ref[device_at(shift_gx, shift_yz)]
    room = TILE[1] - len(DIRECTIONS) * ghost_n
    over = atom_n - room
    last = jnp.concatenate([tile[3:4, c * over : (c + 1) * over] for c in range(3)], axis=0)
    own = jnp.concatenate([tile[0:3, TILE[1] - room :], last], axis=1)
    return total_force(own, jnp.concatenate(back, axis=1), sends)


def step_on(moved, half, kinds, forces):
    kick = 0.5 * STEP * inverse_mass(kinds) * forces
    half_two = half + kick + kick
    return half_two, moved + STEP * half_two


def last_kernel(own_ref, send_ref, half_two_ref, species_ref, in_ref, vel_ref, force_ref):
    forces = total_force(own_ref[...], take(in_ref), send_ref[...])
    force_ref[...] = forces
    vel_ref[...] = half_two_ref[...] + 0.5 * STEP * inverse_mass(species_ref[...]) * forces


def weights_kernel(
    radial_ref,
    embed_ref,
    readout_ref,
    env_t_ref,
    latent_ref,
    into_ref,
    on_hidden_ref,
    on_inner_ref,
    on_bent_ref,
    on_weight_ref,
    readout_t_ref,
    radial_back_ref,
):
    latent = latent_ref.shape[1]
    eye = identity(latent)
    half = BF16(0.5)
    latent_w = latent_ref[...]
    readout = readout_ref[...]
    none = jnp.zeros((BASIS_PAD - 8, latent), BF16)
    readout16 = padded_rows(readout.astype(F32), BASIS_PAD).astype(BF16)
    radial16 = jnp.concatenate([radial_ref[...] * half, none], axis=0)
    latent_t = mm_nt(eye, latent_w * half).astype(BF16)
    on_hidden_ref[...] = jnp.concatenate([latent_t[:, :latent], env_t_ref[...], readout16], axis=0)
    on_inner_ref[...] = latent_t[:, latent:]
    on_bent_ref[...] = (latent_w.astype(F32) * (0.5 * readout.astype(F32))).astype(BF16)
    on_weight_ref[...] = mm_nt(eye, jnp.concatenate([env_t_ref[...], readout16], axis=0)).astype(BF16)
    readout_t_ref[...] = mm_nt(eye, jnp.broadcast_to(readout.astype(F32), (128, latent)).astype(BF16))
    radial_back_ref[...] = radial16
    into = jnp.concatenate([embed_ref[1] * half, embed_ref[0] * half, radial16], axis=0)
    into_ref[...] = mm_nt(eye, into).astype(BF16)


def list_kernel(used_ref, slots_ref, neigh_ref, centre_ref):
    atom_n, slot_n = slots_ref.shape
    blocks, lanes = neigh_ref.shape
    slots_t = mm_nt(identity(slot_n), slots_ref[...].astype(F32).astype(BF16)).astype(BF16)
    used = used_ref[...]
    row_i = lax.broadcasted_iota(jnp.int32, (atom_n, atom_n), 0)
    col_i = lax.broadcasted_iota(jnp.int32, (atom_n, atom_n), 1)
    end = jnp.sum(jnp.where(col_i <= row_i, used, 0.0), axis=1, keepdims=True)
    own = jnp.sum(jnp.where(col_i == row_i, used, 0.0), axis=1, keepdims=True)
    total = jnp.sum(used)
    lane = lax.broadcasted_iota(jnp.int32, (1, lanes), 1)

    def one_block(block):
        place = (lane + block * lanes).astype(F32)
        past = end <= place
        centre = jnp.sum(jnp.where(past, 1.0, 0.0), axis=0, keepdims=True)
        start = jnp.sum(jnp.where(past, own, 0.0), axis=0, keepdims=True)
        slot = (place - start).astype(jnp.int32)
        centre_id = centre.astype(jnp.int32)
        rows = mm(slots_t, one_hot(centre_id, atom_n))
        slot_ids = lax.broadcasted_iota(jnp.int32, (slot_n, lanes), 0)
        neigh = jnp.sum(jnp.where(slot_ids == slot, rows, 0.0), axis=0, keepdims=True)
        valid = place < total
        neigh_ref[pl.ds(block, 1), :] = jnp.where(valid, neigh.astype(jnp.int32), -1)
        centre_ref[pl.ds(block, 1), :] = jnp.where(valid, centre_id, -1)

    def some_blocks(step, carry):
        for more in range(LISTED):
            one_block(step * LISTED + more)
        return carry

    group = LISTED * lanes
    lax.fori_loop(0, (total.astype(jnp.int32) + group - 1) // group, some_blocks, 0)


def list_pairs(used, neighbours):
    blocks = pl.cdiv(neighbours.size, LANES * LISTED) * LISTED
    pairs = jax.ShapeDtypeStruct((blocks, LANES), jnp.int32)
    return pl.pallas_call(
        list_kernel,
        out_shape=[pairs, pairs],
        in_specs=[VMEM] * 2,
        out_specs=[VMEM] * 2,
        compiler_params=pltpu.CompilerParams(vmem_limit_bytes=16 * 2**20),
        cost_estimate=pl.CostEstimate(flops=10**9, bytes_accessed=2**16, transcendentals=0),
        name="list_pairs",
    )(used, neighbours)


def prepare_weights(radial_weight, species_embed, env_weight, latent_weight, readout):
    latent, features = env_weight.shape[1:]
    shapes = (
        ((latent, 2 * SPECIES + BASIS_PAD), BF16),
        ((latent + features + BASIS_PAD, latent), BF16),
        ((latent, features), BF16),
        ((latent + features, latent), BF16),
        ((latent, features + BASIS_PAD), BF16),
        ((latent, 128), F32),
        ((BASIS_PAD, latent), BF16),
    )
    operands = [radial_weight, species_embed, readout[None, :], env_weight[0].T, latent_weight[0]]
    return pl.pallas_call(
        weights_kernel,
        out_shape=[jax.ShapeDtypeStruct(*shape) for shape in shapes],
        in_specs=[VMEM] * len(operands),
        out_specs=[VMEM] * len(shapes),
        compiler_params=pltpu.CompilerParams(vmem_limit_bytes=24 * 2**20),
        cost_estimate=pl.CostEstimate(flops=10**9, bytes_accessed=4 * 2**20, transcendentals=0),
        name="prepare_weights",
    )(*operands)


def silu_pair(half_in):
    bent = jnp.tanh(half_in)
    part = half_in * bent
    return half_in + part, (1.0 + bent) * (1.0 + (half_in - part))


def force_kernel(
    used_ref,
    neigh_ref,
    centre_ref,
    moved_ref,
    own_kind_ref,
    into_ref,
    on_hidden_ref,
    on_inner_ref,
    on_bent_ref,
    on_weight_ref,
    readout_ref,
    radial_back_ref,
    in_ref,
    *refs,
    second_call,
    out_ghost_n,
):
    *refs, hot_s, use_s, u_s, slope_s, raw_s, part_s, ain_s, energy_s, c_s, dc_s, f_s = refs
    blocks, lanes = neigh_ref.shape
    atom_n = moved_ref.shape[1]
    ghost_n = out_ghost_n
    ext_n = atom_n + ghost_n * len(DIRECTIONS)
    own_kind = own_kind_ref[...]
    from_owners = [in_ref[place] for place in towards(-1)]
    ghosts = jnp.concatenate(
        [
            jnp.concatenate([owner[:, n * ghost_n : (n + 1) * ghost_n] for owner in from_owners], axis=1)
            for n in range(2)
        ],
        axis=0,
    )
    ghost_kind = ghosts[3:4].astype(jnp.int32)
    if second_call:
        half_ref, send_ref, all_ref, half_two_ref, end_ref, own_out_ref, out_ref = refs
        sends, wholes = [], []
        for k, (a, b) in enumerate(DIRECTIONS):
            rows = [from_owners[k][:, n * ghost_n : (n + 1) * ghost_n] for n in (2, 3)]
            sends.append(jnp.concatenate(rows, axis=0).astype(jnp.int32))
            wholes.append(domain_force(all_ref, -a, -b, sends[k], atom_n))
        own_whole = domain_force(all_ref, 0, 0, send_ref[...], atom_n)
        on_ghosts = [
            sum_parts(mm(split3(padded_rows(whole, 8)), one_hot(sends[k][k : k + 1], atom_n)))[0:3]
            for k, whole in enumerate(wholes)
        ]
        _, ghost_pos = step_on(
            ghosts[0:3], ghosts[4:7], ghost_kind, jnp.concatenate(on_ghosts, axis=1)
        )
        half_two, own_pos = step_on(moved_ref[...], half_ref[...], own_kind, own_whole)
        half_two_ref[...] = half_two
        end_ref[...] = own_pos
    else:
        (out_ref,) = refs
        own_pos, ghost_pos = moved_ref[...], ghosts[0:3]
    kind = jnp.concatenate([own_kind, ghost_kind], axis=1)
    basis_n = SPECIES
    latent, features = on_inner_ref.shape
    total = jnp.sum(used_ref[...]).astype(jnp.int32)
    full = (total + lanes - 1 - TAIL) // lanes
    scale = COUPLING * SLOTS ** (-0.5)

    own_table = lane_table(padded_rows(own_pos, 8) * (1.0 / RADIUS))
    ghost_table = lane_table(padded_rows(ghost_pos, 8) * (1.0 / RADIUS))
    row8 = lax.broadcasted_iota(jnp.int32, (SPECIES, ext_n), 0)
    kinds = jnp.where(row8 == kind, 1.0, 0.0)
    basis_in = identity(BASIS_PAD).astype(F32)
    selected = jnp.concatenate(
        [
            jnp.concatenate([kinds, jnp.zeros((SPECIES + BASIS_PAD, ext_n), F32)], axis=0),
            jnp.concatenate(
                [jnp.zeros((SPECIES, atom_n), F32), kinds[:, :atom_n], jnp.zeros((BASIS_PAD, atom_n), F32)], axis=0
            ),
            jnp.concatenate([jnp.zeros((2 * SPECIES, BASIS_PAD), F32), basis_in], axis=0),
        ],
        axis=1,
    )
    weight_in = mm(into_ref[...], selected.astype(BF16)).astype(BF16)

    mid_row = lax.broadcasted_iota(jnp.int32, (BASIS_PAD, lanes), 0).astype(F32)
    mids = (mid_row + 0.5) / basis_n
    sharp = 2.0 * basis_n * basis_n

    c_s[...] = jnp.zeros_like(c_s)
    dc_s[...] = jnp.zeros_like(dc_s)
    f_s[...] = jnp.zeros_like(f_s)

    def each_block(one):
        def step(block, carry):
            one(block, lanes)
            return carry

        lax.fori_loop(0, full, step, 0)
        pl.when(total > full * lanes)(functools.partial(one, full, TAIL))

    def geometry(block, width):
        vec = u_s[block, :, :width]
        square = jnp.sum(vec * vec, axis=0, keepdims=True)
        inside = jnp.maximum(1.0 - square, 0.0)
        inside = jnp.where(centre_ref[pl.ds(block, 1), :width] >= 0, inside, 0.0)
        apart = square - mids[:, :width]
        return vec, inside, apart, jnp.exp(-sharp * apart * apart)

    def first(block, width):
        neigh = neigh_ref[pl.ds(block, 1), :width]
        centre = centre_ref[pl.ds(block, 1), :width]
        hot_c = one_hot(centre, atom_n)
        hot = jnp.concatenate([one_hot(neigh, ext_n), hot_c], axis=0)
        hot_s[block, :, :width] = hot
        there = jnp.where(
            neigh < atom_n, look_up(own_table, neigh), look_up(ghost_table, neigh - atom_n)
        )
        u_s[block, :, :width] = there - look_up(own_table, centre)
        vec, inside, _, basis = geometry(block, width)
        use = jnp.concatenate([hot_c * vec[k : k + 1].astype(BF16) for k in range(3)], axis=0)
        use_s[block, :, :width] = use
        pre = mm(weight_in, jnp.concatenate([hot, basis.astype(BF16)], axis=0))
        hidden, slope = silu_pair(pre)
        slope_s[block, :, :width] = slope.astype(BF16)
        taken = mm(on_hidden_ref[...], hidden.astype(BF16))
        part_s[block, :, :width] = taken[:latent]
        raw = taken[latent : latent + features]
        raw_s[block, :, :width] = raw
        energy_s[block, :, :width] = taken[latent + features : latent + features + 8]
        c_s[...] += mm_nt((raw * (inside * inside)).astype(BF16), use)

    each_block(first)
    c_all = c_s[...] * scale
    c_b = c_all.astype(BF16)

    def second(block, width):
        _, inside, _, _ = geometry(block, width)
        use = use_s[block, :, :width]
        env = inside * inside
        weight = raw_s[block, :, :width] * env
        inner = weight * mm(c_b, use)
        later = part_s[block, :, :width] + mm(on_inner_ref[...], inner.astype(BF16))
        gain, bent = silu_pair(later)
        readout = jnp.concatenate([readout_ref[...]] * (width // 128), axis=1)
        energy_s[block, :, :width] += jnp.sum(gain * readout, axis=0, keepdims=True)
        taken = mm(on_bent_ref[...], bent.astype(BF16))
        part_s[block, :, :width] = taken[:latent]
        a_in = taken[latent:] * env
        ain_s[block, :, :width] = a_in
        dc_s[...] += mm_nt((a_in * weight).astype(BF16), use)

    each_block(second)
    c_dc = jnp.concatenate([c_all, dc_s[...] * scale], axis=0).astype(BF16)
    both = jnp.concatenate([c_all.T, dc_s[...].T * scale], axis=1).astype(BF16)

    def third(block, width):
        vec, inside, apart, basis = geometry(block, width)
        use = use_s[block, :, :width]
        hot = hot_s[block, :, :width]
        env = inside * inside
        raw = raw_s[block, :, :width]
        weight = raw * env
        a_in = ain_s[block, :, :width]
        along = mm(c_dc, use)
        d_all = mm(both, jnp.concatenate([a_in * weight, weight], axis=0).astype(BF16))
        hot_c = hot[ext_n:].astype(F32)
        picked = [
            jnp.sum(d_all[k * atom_n : (k + 1) * atom_n] * hot_c, axis=0, keepdims=True)
            for k in range(3)
        ]
        d_weight = a_in * along[:features] + along[features:]
        d_env = jnp.sum(d_weight * raw, axis=0, keepdims=True) + energy_s[block, :, :width][0:1]
        ones = jnp.ones((BASIS_PAD, width), BF16)
        d_hidden = part_s[block, :, :width] + mm(
            on_weight_ref[...], jnp.concatenate([d_weight.astype(BF16), ones], axis=0)
        )
        d_pre = (d_hidden * slope_s[block, :, :width].astype(F32)).astype(BF16)
        d_basis = mm(radial_back_ref[...], d_pre)
        d_square = env * jnp.sum(d_basis * basis * apart, axis=0, keepdims=True) * (-2.0 * sharp)
        d_square = d_square - 2.0 * inside * d_env
        d_vec = jnp.concatenate(picked + [jnp.zeros((5, width), F32)], axis=0)
        d_vec = (d_vec + 2.0 * d_square * vec) * (1.0 / RADIUS)
        f_s[...] += mm_nt(split3(d_vec), hot)

    each_block(third)
    summed = f_s[0:8] + f_s[8:16] + f_s[16:24]
    on_centre = summed[0:3, ext_n:]
    on_neigh = summed[0:3, :ext_n]
    own = on_centre - on_neigh[:, :atom_n]
    if second_call:
        own_out_ref[...] = own
        put(out_ref, -on_neigh[:, atom_n:])
    else:
        tile = forces_tile(own, -on_neigh[:, atom_n:])
        out_ref[...] = jnp.broadcast_to(tile[None], out_ref.shape)


def pair_forces(pairs, own_pos, own_kind, weights, incoming, ghost_n, second=()):
    used, neigh, centre = pairs
    blocks, lanes = neigh.shape
    latent, features = weights[2].shape
    atom_n = own_pos.shape[1]
    devices = incoming.shape[0]
    ext_n = atom_n + ghost_n * len(DIRECTIONS)
    operands = [used, neigh, centre, own_pos, own_kind, *weights, incoming, *second]
    if second:
        out_shape = [jax.ShapeDtypeStruct((3, atom_n), F32)] * 3
        out_shape.append(jax.ShapeDtypeStruct((devices, 3, ghost_n), F32))
    else:
        out_shape = [jax.ShapeDtypeStruct((devices, *TILE), F32)]
    pair_rows = blocks * lanes
    return pl.pallas_call(
        functools.partial(force_kernel, second_call=bool(second), out_ghost_n=ghost_n),
        out_shape=out_shape,
        in_specs=[VMEM] * len(operands),
        out_specs=[VMEM] * len(out_shape),
        scratch_shapes=[
            pltpu.VMEM((blocks, ext_n + atom_n, lanes), BF16),
            pltpu.VMEM((blocks, 3 * atom_n, lanes), BF16),
            pltpu.VMEM((blocks, 8, lanes), F32),
            pltpu.VMEM((blocks, latent, lanes), BF16),
            pltpu.VMEM((blocks, features, lanes), F32),
            pltpu.VMEM((blocks, latent, lanes), F32),
            pltpu.VMEM((blocks, features, lanes), F32),
            pltpu.VMEM((blocks, 8, lanes), F32),
            pltpu.VMEM((features, 3 * atom_n), F32),
            pltpu.VMEM((features, 3 * atom_n), F32),
            pltpu.VMEM((24, ext_n + atom_n), F32),
        ],
        compiler_params=pltpu.CompilerParams(vmem_limit_bytes=48 * 2**20),
        cost_estimate=pl.CostEstimate(
            flops=pair_rows * latent * 2700, bytes_accessed=4 * 2**20, transcendentals=0
        ),
        name="pair_forces",
    )(*operands)


def small_call(kernel, name, operands, out_shape):
    return pl.pallas_call(
        kernel,
        out_shape=out_shape,
        in_specs=[VMEM] * len(operands),
        out_specs=[VMEM] * len(out_shape),
        compiler_params=pltpu.CompilerParams(vmem_limit_bytes=16 * 2**20),
        name=name,
    )(*operands)


def devices_at(shift_gx, shift_yz):
    gx_n, yz_n = lax.axis_size("gx"), lax.axis_size("yz")
    gx = (lax.axis_index("gx") + jnp.asarray(shift_gx, jnp.int32) + gx_n) % gx_n
    yz = (lax.axis_index("yz") + jnp.asarray(shift_yz, jnp.int32) + yz_n) % yz_n
    return gx * yz_n + yz


def exchange(blocks):
    return lax.all_to_all(blocks, ("gx", "yz"), 0, 0, tiled=True)


def body(
    positions,
    velocities,
    forces_start,
    species,
    live_atoms,
    send_list,
    neighbours,
    neighbour_count,
    radial_weight,
    species_embed,
    env_weight,
    latent_weight,
    readout,
):
    atom_n = positions.shape[1]
    ghost_n = send_list.shape[1]
    devices = lax.axis_size("gx") * lax.axis_size("yz")
    atoms = jax.ShapeDtypeStruct((3, atom_n), F32)

    kinds = species.reshape(1, atom_n)
    ahead = devices_at([a for a, _ in DIRECTIONS], [b for _, b in DIRECTIONS])
    moved, half, used, sent = small_call(
        start_kernel,
        "start",
        [
            ahead[None, :],
            positions,
            velocities,
            forces_start,
            kinds,
            live_atoms,
            neighbour_count.reshape(1, atom_n),
            send_list,
        ],
        [atoms, atoms, jax.ShapeDtypeStruct((1, atom_n), F32), jax.ShapeDtypeStruct((devices, *TILE), F32)],
    )
    got = exchange(sent)
    pairs = (used, *list_pairs(used, neighbours))
    weights = prepare_weights(radial_weight, species_embed, env_weight, latent_weight, readout)
    (sent,) = pair_forces(pairs, moved, kinds, weights, got, ghost_n)
    every = exchange(sent)
    half_two, positions_end, own, sent = pair_forces(
        pairs, moved, kinds, weights, got, ghost_n, (half, send_list, every)
    )
    back = exchange(sent)
    velocities_end, forces_end = small_call(
        last_kernel, "last", [own, send_list, half_two, kinds, back], [atoms, atoms]
    )
    return (positions_end, velocities_end, forces_end)


def solution(mesh):
    placed = (
        P(None, ("gx", "yz")),
        P(None, ("gx", "yz")),
        P(None, ("gx", "yz")),
        P(("gx", "yz")),
        P(("gx", "yz")),
        P(None, ("gx", "yz")),
        P(("gx", "yz"), None),
        P(("gx", "yz")),
        P(),
        P(),
        P(),
        P(),
        P(),
    )
    return jax.shard_map(
        body,
        mesh=mesh,
        in_specs=placed,
        out_specs=(P(None, ("gx", "yz")), P(None, ("gx", "yz")), P(None, ("gx", "yz"))),
        check_vma=False,
    )
```
